128 devices in a mesh: section: 2 (over core), dp: 64 (over y, z, x).
Axes of the slice: x: 4, y: 4, z: 4, core: 2. Of those that a mesh axis runs over, the one named last changes fastest.
Arguments:
- tokens: bfloat16 [2, 2, 64, 256, 512], P('section', None, 'dp'), may hold values from -16 to 16
- cotangent: bfloat16 [2, 2, 64, 256, 512], P('section', None, 'dp'), may hold values from -6 to 6
- source_lengths: int32 [2, 64, 8], P(None, 'dp'), may hold values from 1 to 128, 256 in all within a row
- target_segments: int32 [2, 64, 256], P(None, 'dp'), may hold values from 0 to 7, never falling along the last dimension, each value on 1 to 128 neighbouring positions
- self_in: bfloat16 [2, 512, 1536], P('section'), may hold values from -0.25 to 0.25
- self_out: bfloat16 [2, 512, 512], P('section'), may hold values from -1.5 to 1.5
- cross_weight: bfloat16 [2, 512, 1024], P('section'), may hold values from -0.625 to 0.625
- hidden_in: bfloat16 [2, 512, 2048], P('section'), may hold values from -0.25 to 0.25
- hidden_out: bfloat16 [2, 2048, 512], P('section'), may hold values from -0.125 to 0.125
- norm_params: float32 [2, 6, 512], P('section'), may hold values from -1.2 to 1.6, as said below
Outputs:
- layer_out: bfloat16 [2, 2, 64, 256, 512], P('section', None, 'dp')
- token_grads: float32 [2, 2, 64, 256, 512], P('section', None, 'dp')
- grad_self_in: float32 [2, 512, 1536], P('section', 'dp')
- grad_self_out: float32 [2, 512, 512], P('section', 'dp')
- grad_cross: float32 [2, 512, 1024], P('section', 'dp')
- grad_hidden_in: float32 [2, 512, 2048], P('section', 'dp')
- grad_hidden_out: float32 [2, 2048, 512], P('section', 'dp')
- grad_norms: float32 [2, 6, 512], P('section', None, 'dp')
The draws below stay inside these ranges and needn't reach their ends.
Inputs may be any that keep to these rules, and one draw needn't show every extreme that they name: `source_lengths`: the 8 lengths of each row sum to 256; the longest document of each row has exactly 128 tokens. `target_segments`: along each row the numbers never fall; each of 0 to 7 appears on 1 to 128 positions, one of them on exactly 128. `norm_params`: gains are positive.
All inputs are finite; a program needn't handle non-finite values.
Results may differ from the reference program's by a relative error of at most 0.017.
Values may be sent and summed in bfloat16 or wider, within the bound.
A program may use at most 320 MiB of HBM per device.

```python
import math
import jax
import jax.numpy as jnp
import numpy as np
from jax import lax

D = 512
HEADS = 8
FF = 2048
HEAD_DIM = 64
ROW = 256
MOST = 128
NSEG = 8
MB = 2
ROWS = 64


def draw_cross_weight(key, part):
    key = jax.random.fold_in(key, 7)
    values = jnp.clip(jax.random.normal(key, (2, D, 2 * D), jnp.float32), -5.0, 5.0)
    column = jnp.arange(2 * D)
    factor = jnp.where(column >= D, (D // 8) ** (-0.5), D ** (-0.5))
    return (values * factor).astype(jnp.bfloat16)


def draw_norm_params(key, part):
    key = jax.random.fold_in(key, 11)
    values = jnp.clip(jax.random.normal(key, (2, 6, D), jnp.float32), -4.0, 4.0)
    row_index = jnp.arange(6)[None, :, None]
    return jnp.where(row_index % 2 == 0, 1.0 + 0.15 * values, 0.3 * values)


def with_spikes(result, stream_key, source, target, blocks, factor):
    owner, partner = [(jnp.arange(result.shape[dim]) // (result.shape[dim] // blocks)).reshape([-1 if axis == dim else 1 for axis in range(result.ndim)]) for dim in (source, target)]
    chosen = jax.random.permutation(stream_key, blocks)[partner]
    strong = (owner == chosen) | (owner == (partner + blocks // 2) % blocks)
    return jnp.where(strong, factor * result, result)


def level_of(stream_key, shape, shards, low, high):
    def one(dim, parts):
        draws = jax.random.uniform(jax.random.fold_in(jax.random.fold_in(stream_key, 6), dim), (parts,), jnp.float32, low / len(shards), high / len(shards))
        return jnp.repeat(jnp.exp(draws), shape[dim] // parts).reshape((-1,) + (1,) * (len(shape) - dim - 1))

    loudness = one(*shards[0])
    for cut in shards[1:]:
        loudness = loudness * one(*cut)
    return loudness


def split_up(amount, total, most, lean):
    weights = [(1 << 20) // math.isqrt(rank ** lean) + 1 for rank in range(2, amount + 1)]
    surplus, counts = total - most - (amount - 1), [1] * (amount - 1)
    while surplus > 0:
        movable = [i for i in range(amount - 1) if counts[i] < most]
        mass, budget = sum([weights[i] for i in movable]), surplus
        for i in movable:
            more = min(most - counts[i], max(1, budget * weights[i] // mass), surplus)
            counts[i] = counts[i] + more
            surplus = surplus - more
    return np.array([most] + counts)


def uneven(key, count, total, limit, lean):
    if count == 2:
        one = jax.random.randint(key, (), max(1, total - limit), min(limit, total - 1) + 1)
        return jnp.stack([one, total - one])
    sizes = jnp.asarray(split_up(count, total, limit, lean), jnp.int32)
    pairs = (count - 1) // 2
    giver, receiver = sizes[1:1 + 2 * pairs:2], sizes[2:2 + 2 * pairs:2]
    room = jnp.minimum(giver - 1, limit - receiver)
    moved = jax.random.randint(jax.random.fold_in(key, 1), (pairs,), 0, 1 << 20) % (room + 1)
    sizes = sizes.at[1:1 + 2 * pairs:2].set(giver - moved).at[2:2 + 2 * pairs:2].set(receiver + moved)
    return sizes[jax.random.permutation(jax.random.fold_in(key, 2), count)]


def noise(rng, shape, spread, reach, cuts=(), kind=jnp.bfloat16):
    level = level_of(rng, shape, cuts, -0.22, 0.18) if cuts else 1.0
    entries = jax.random.normal(rng, shape, jnp.float32) * spread * level
    return jnp.minimum(jnp.maximum(entries, -reach), reach).astype(kind)


def gaussian_with(rng, dims, scale, most, cuts, heavy, held_as=jnp.bfloat16):
    entries = scale * jax.random.normal(rng, dims, jnp.float32)
    if cuts:
        entries = entries * level_of(rng, dims, cuts, -0.22, 0.18)
    return jnp.clip(with_spikes(entries, jax.random.fold_in(rng, 3), *heavy), -most, most).astype(held_as)


def setup_inputs(seed: int = 0) -> dict:
    keys = jax.random.split(jax.random.key(seed), 11)
    tokens = gaussian_with(keys[0], (2, MB, ROWS, ROW, D), 1.0, 16.0, ((0, 2), (2, 64)), (2, 4, 64, 4.0))
    cotangent = noise(keys[1], (2, MB, ROWS, ROW, D), 1.0, 6.0, ((0, 2), (2, 64)))
    source_lengths = jax.vmap(lambda own: uneven(own, NSEG, ROW, MOST, 2))(jax.random.split(keys[2], MB * ROWS)).reshape((MB, ROWS, NSEG)).astype(jnp.int32)
    target_segments = jax.vmap(lambda own: jnp.searchsorted(jnp.cumsum(uneven(own, NSEG, ROW, MOST, 2)), jnp.arange(ROW), side="right"))(jax.random.split(keys[3], MB * ROWS)).reshape((MB, ROWS, ROW)).astype(jnp.int32)
    self_in = noise(keys[4], (2, D, 3 * D), D ** -0.5, 0.25, ((0, 2),))
    self_out = noise(keys[5], (2, D, D), (D // 32) ** -0.5, 1.5, ((0, 2),))
    cross_weight = draw_cross_weight(jax.random.fold_in(keys[10], 71), 0)
    hidden_in = noise(keys[7], (2, D, FF), D ** -0.5, 0.25, ((0, 2),))
    hidden_out = noise(keys[8], (2, FF, D), FF ** -0.5, 0.125, ((0, 2),))
    norm_params = draw_norm_params(jax.random.fold_in(keys[10], 71), 0)
    return dict(tokens=tokens, cotangent=cotangent, source_lengths=source_lengths, target_segments=target_segments, self_in=self_in, self_out=self_out, cross_weight=cross_weight, hidden_in=hidden_in, hidden_out=hidden_out, norm_params=norm_params)


@jax.custom_vjp
def low(v):
    return lax.optimization_barrier(v.astype(jnp.bfloat16)).astype(jnp.float32)

@jax.custom_vjp
def low_back(v):
    return v

def low_keep(v):
    return (low(v), None)

def low_pass(kept, grad):
    return (grad,)

def back_keep(v):
    return (v, None)

def back_low(kept, grad):
    return (low(grad),)
low.defvjp(low_keep, low_pass)
low_back.defvjp(back_keep, back_low)
highest = lax.Precision.HIGHEST
root_half = 0.7071067811865476

def layer_norm(values, gain, shift):
    center = values - lax.optimization_barrier(jnp.mean(values, -1, keepdims=True))
    return center * lax.rsqrt(lax.optimization_barrier(jnp.mean(center * center, -1, keepdims=True)) + 1e-05) * gain + shift

def project(values, weight):
    return low_back(jnp.einsum('gld,de->gle', low(values), weight, precision=highest))

def gaussian_unit(values):
    return values * (0.5 * (1.0 + lax.erf(values * root_half)))

def heads_of(values):
    return values.reshape(values.shape[0], values.shape[1], HEADS, HEAD_DIM)

def attend(queries, keys_in, values, allowed):
    scores = jnp.einsum('gqhe,gkhe->ghqk', heads_of(queries), heads_of(keys_in), precision=highest) * HEAD_DIM ** (-0.5)
    scores = jnp.where(allowed[:, None], low_back(scores), -1e+30)
    largest = lax.optimization_barrier(jnp.max(scores, -1, keepdims=True))
    expval = jnp.exp(scores - largest)
    shares = low(expval / lax.optimization_barrier(jnp.sum(expval, -1, keepdims=True)))
    context = jnp.einsum('ghqk,gkhe->gqhe', shares, heads_of(values), precision=highest)
    return low(low_back(context.reshape(queries.shape)))

def self_block(inputs, allowed, self_in, self_out):
    projected = low(project(inputs, self_in))
    context = attend(projected[..., :D], projected[..., D:2 * D], projected[..., 2 * D:], allowed)
    return project(context, self_out)

def feed_forward(inputs, hidden_in, hidden_out):
    return project(gaussian_unit(project(inputs, hidden_in)), hidden_out)

def segments_of(lengths):
    bounds = jnp.cumsum(lengths, -1)
    places = jnp.arange(ROW, dtype=jnp.int32)
    return lax.optimization_barrier(jnp.sum((places[None, :, None] >= bounds[:, None, :]).astype(jnp.int32), -1))

def layer_pair(source, target, lengths, segments, weights):
    self_in, self_out, cross_weight, hidden_in, hidden_out, norm_params = weights
    source_ids = segments_of(lengths)
    source_mask = source_ids[:, :, None] == source_ids[:, None, :]
    target_mask = segments[:, :, None] == segments[:, None, :]
    cross_mask = segments[:, :, None] == source_ids[:, None, :]
    first_out = layer_norm(source + self_block(source, source_mask, self_in[0], self_out[0]), norm_params[0, 0], norm_params[0, 1])
    second_out = layer_norm(first_out + feed_forward(first_out, hidden_in[0], hidden_out[0]), norm_params[0, 2], norm_params[0, 3])
    memory = layer_norm(second_out, norm_params[0, 4], norm_params[0, 5])
    key_value = low(project(memory, cross_weight[0]))
    target_first = layer_norm(target + self_block(target, target_mask, self_in[1], self_out[1]), norm_params[1, 0], norm_params[1, 1])
    queries = low(project(target_first, cross_weight[1][:, :D]))
    context = attend(queries, key_value[..., :D], key_value[..., D:], cross_mask)
    target_second = layer_norm(target_first + project(context, cross_weight[1][:, D:]), norm_params[1, 4], norm_params[1, 5])
    target_third = layer_norm(target_second + feed_forward(target_second, hidden_in[1], hidden_out[1]), norm_params[1, 2], norm_params[1, 3])
    return (memory, target_third)

def reference(tokens, cotangent, source_lengths, target_segments, self_in, self_out, cross_weight, hidden_in, hidden_out, norm_params):
    groups = MB * ROWS // 16

    def regroup(array):
        return array.reshape((groups, 16) + array.shape[2:])
    weights = tuple((matrix.astype(jnp.float32) for matrix in (self_in, self_out, cross_weight, hidden_in, hidden_out, norm_params)))
    lengths = regroup(source_lengths)
    segments = regroup(target_segments)

    def forward(source, target, params):

        def one_group(operands):
            return layer_pair(operands[0], operands[1], operands[2], operands[3], params)
        return lax.map(jax.checkpoint(one_group), (source, target, lengths, segments))
    source = regroup(tokens[0].astype(jnp.float32))
    target = regroup(tokens[1].astype(jnp.float32))
    outputs, pullback = jax.vjp(forward, source, target, weights)
    grad_source, grad_target, grad_weights = pullback((regroup(cotangent[0].astype(jnp.float32)), regroup(cotangent[1].astype(jnp.float32))))
    full_shape = (MB, ROWS, ROW, D)
    layer_out = jnp.stack([outputs[0].reshape(full_shape), outputs[1].reshape(full_shape)]).astype(jnp.bfloat16)
    token_grads = jnp.stack([grad_source.reshape(full_shape), grad_target.reshape(full_shape)])
    return (layer_out, token_grads, grad_weights[0], grad_weights[1], grad_weights[2], grad_weights[3], grad_weights[4], grad_weights[5])
```

```python
from functools import partial
from functools import reduce

import jax
import jax.numpy as jnp
from jax import lax
from jax.experimental import pallas as pl
from jax.experimental.pallas import tpu as pltpu
from jax.sharding import PartitionSpec as P

HEADS = 8


root_half = 0.7071067811865476
inverse_root = 0.3989422804014327


def as_sent(value):
    return jax.tree.map(lambda a: a.astype(jnp.bfloat16) if a.dtype == jnp.float32 else a, value)


def shifted(value, axis, steps):
    count = lax.axis_size(axis)
    leading, last = (max(0, -steps), min(count, count - steps))
    return lax.ppermute(value, axis, [(source, source + steps) for source in range(leading, last)])


def on_section(active, worker):

    def zeroed():
        return jax.tree.map(lambda leaf: jnp.zeros_like(leaf), worker())

    return lax.cond(active, worker, zeroed)


def linear(values, weight):
    return jnp.einsum("rld,de->rle", values, weight, preferred_element_type=jnp.float32)


def linear_back(gradient, weight):
    return jnp.einsum("rle,de->rld", gradient, weight, preferred_element_type=jnp.float32)


def outer_sum(values, gradient):
    return jnp.einsum("rld,rle->de", values, gradient, preferred_element_type=jnp.float32)


def split_heads(values, head_count):
    return values.reshape(values.shape[0], values.shape[1], head_count, -1)


def attend_scores(queries, keys_in, allowed, head_count):
    query_heads = split_heads(queries, head_count)
    factor = query_heads.shape[-1] ** (-0.5)
    scores = (
        jnp.einsum(
            "rqhe,rkhe->rhqk",
            query_heads,
            split_heads(keys_in, head_count),
            preferred_element_type=jnp.float32,
        )
        * factor
    )
    return jnp.where(allowed[:, None], scores, -1e30)


def attend_forward(queries, keys_in, values, allowed, head_count):
    scores = attend_scores(queries, keys_in, allowed, head_count)
    largest = jnp.max(scores, -1, keepdims=True)
    expval = jnp.exp(scores - largest)
    totals = jnp.sum(expval, -1, keepdims=True)
    shares = (expval / totals).astype(jnp.bfloat16)
    context = jnp.einsum(
        "rhqk,rkhe->rqhe",
        shares,
        split_heads(values, head_count),
        preferred_element_type=jnp.float32,
    )
    return (context.reshape(queries.shape).astype(jnp.bfloat16), largest + jnp.log(totals))


def attend_backward(queries, keys_in, values, allowed, head_count, logsum, grad_context):
    scores = attend_scores(queries, keys_in, allowed, head_count)
    shares = jnp.exp(scores - logsum)
    grad_heads = split_heads(grad_context, head_count)
    grad_shares = jnp.einsum(
        "rqhe,rkhe->rhqk",
        grad_heads,
        split_heads(values, head_count),
        preferred_element_type=jnp.float32,
    )
    grad_values = jnp.einsum(
        "rhqk,rqhe->rkhe",
        shares.astype(jnp.bfloat16),
        grad_heads,
        preferred_element_type=jnp.float32,
    )
    grad_scores = shares * (grad_shares - jnp.sum(grad_shares * shares, -1, keepdims=True))
    rounded = grad_scores.astype(jnp.bfloat16)
    factor = grad_heads.shape[-1] ** (-0.5)
    grad_queries = (
        jnp.einsum(
            "rhqk,rkhe->rqhe",
            rounded,
            split_heads(keys_in, head_count),
            preferred_element_type=jnp.float32,
        )
        * factor
    )
    grad_keys = (
        jnp.einsum(
            "rhqk,rqhe->rkhe",
            rounded,
            split_heads(queries, head_count),
            preferred_element_type=jnp.float32,
        )
        * factor
    )
    return (
        grad_queries.reshape(queries.shape),
        grad_keys.reshape(keys_in.shape),
        grad_values.reshape(values.shape),
    )


def norm_forward(values, gain, shift):
    center = values - jnp.mean(values, -1, keepdims=True)
    inverse = lax.rsqrt(jnp.mean(center * center, -1, keepdims=True) + 1e-05)
    normed = center * inverse
    return (normed * gain + shift, normed, inverse)


def norm_backward(gradient, normed, inverse, gain):
    scaled = gradient * gain
    grad_in = inverse * (
        scaled
        - jnp.mean(scaled, -1, keepdims=True)
        - normed * jnp.mean(scaled * normed, -1, keepdims=True)
    )
    return (grad_in, jnp.sum(gradient * normed, (0, 1)), jnp.sum(gradient, (0, 1)))


def gelu_parts(hidden):
    normal_cdf = 0.5 * (1.0 + lax.erf(hidden * root_half))
    return (
        hidden * normal_cdf,
        normal_cdf + hidden * jnp.exp(-0.5 * hidden * hidden) * inverse_root,
    )


def self_forward(inputs, allowed, self_in, self_out, head_count):
    model_width = inputs.shape[-1]
    projected = linear(inputs, self_in).astype(jnp.bfloat16)
    context, logsum = attend_forward(
        projected[..., :model_width],
        projected[..., model_width : 2 * model_width],
        projected[..., 2 * model_width :],
        allowed,
        head_count,
    )
    return (projected, context, logsum, linear(context, self_out))


def self_backward(
    inputs, allowed, self_in, self_out, head_count, projected, context, logsum, gradient
):
    model_width = inputs.shape[-1]
    grad_branch = gradient.astype(jnp.bfloat16)
    grad_self_out = outer_sum(context, grad_branch)
    grad_context = linear_back(grad_branch, self_out).astype(jnp.bfloat16)
    grad_query, grad_key, grad_value = attend_backward(
        projected[..., :model_width],
        projected[..., model_width : 2 * model_width],
        projected[..., 2 * model_width :],
        allowed,
        head_count,
        logsum,
        grad_context,
    )
    grad_projected = jnp.concatenate([grad_query, grad_key, grad_value], -1).astype(jnp.bfloat16)
    return (outer_sum(inputs, grad_projected), grad_self_out, linear_back(grad_projected, self_in))


def ffn_forward(inputs, hidden_in, hidden_out):
    activated, slopes = gelu_parts(linear(inputs, hidden_in))
    activated = activated.astype(jnp.bfloat16)
    return (activated, slopes, linear(activated, hidden_out))


def ffn_backward(inputs, hidden_in, hidden_out, activated, slopes, gradient):
    grad_result = gradient.astype(jnp.bfloat16)
    grad_hidden = (linear_back(grad_result, hidden_out) * slopes).astype(jnp.bfloat16)
    return (
        outer_sum(inputs, grad_hidden),
        outer_sum(activated, grad_result),
        linear_back(grad_hidden, hidden_in),
    )


def encoder_forward(source, allowed, params, head_count):
    self_in, self_out, cross_weight, hidden_in, hidden_out, norm_params = params
    projected, context, logsum, branch = self_forward(
        source, allowed, self_in, self_out, head_count
    )
    first_out, first_normed, first_scale = norm_forward(
        source.astype(jnp.float32) + branch, norm_params[0], norm_params[1]
    )
    first_low = first_out.astype(jnp.bfloat16)
    activated, slopes, ffn_result = ffn_forward(first_low, hidden_in, hidden_out)
    second_out, second_normed, second_scale = norm_forward(
        first_out + ffn_result, norm_params[2], norm_params[3]
    )
    memory, memory_normed, memory_scale = norm_forward(second_out, norm_params[4], norm_params[5])
    memory_low = memory.astype(jnp.bfloat16)
    key_value = linear(memory_low, cross_weight).astype(jnp.bfloat16)
    stored = (
        projected,
        context,
        logsum,
        first_normed,
        first_scale,
        first_low,
        activated,
        slopes,
        second_normed,
        second_scale,
        memory_normed,
        memory_scale,
        memory_low,
    )
    return (memory, key_value, stored)


def encoder_step(source, allowed, params, head_count, grad_memory, grad_pairs):
    self_in, self_out, cross_weight, hidden_in, hidden_out, norm_params = params
    memory, key_value, stored = encoder_forward(source, allowed, params, head_count)
    (
        projected,
        context,
        logsum,
        first_normed,
        first_scale,
        first_low,
        activated,
        slopes,
        second_normed,
        second_scale,
        memory_normed,
        memory_scale,
        memory_low,
    ) = stored
    grad_cross = outer_sum(memory_low, grad_pairs)
    gradient = grad_memory + linear_back(grad_pairs, cross_weight)
    gradient, gain_memory, shift_memory = norm_backward(
        gradient, memory_normed, memory_scale, norm_params[4]
    )
    gradient, gain_ffn, shift_ffn = norm_backward(
        gradient, second_normed, second_scale, norm_params[2]
    )
    grad_hidden_in, grad_hidden_out, through = ffn_backward(
        first_low, hidden_in, hidden_out, activated, slopes, gradient
    )
    gradient = gradient + through
    gradient, gain_attend, shift_attend = norm_backward(
        gradient, first_normed, first_scale, norm_params[0]
    )
    grad_self_in, grad_self_out, through = self_backward(
        source, allowed, self_in, self_out, head_count, projected, context, logsum, gradient
    )
    grad_norms = jnp.stack(
        [gain_attend, shift_attend, gain_ffn, shift_ffn, gain_memory, shift_memory]
    )
    return (
        gradient + through,
        (grad_self_in, grad_self_out, grad_cross, grad_hidden_in, grad_hidden_out, grad_norms),
    )


def decoder_step(target, key_value, self_allowed, cross_allowed, params, head_count, grad_output):
    self_in, self_out, cross_weight, hidden_in, hidden_out, norm_params = params
    model_width = target.shape[-1]
    projected, context, logsum, branch = self_forward(
        target, self_allowed, self_in, self_out, head_count
    )
    first_out, first_normed, first_scale = norm_forward(
        target.astype(jnp.float32) + branch, norm_params[0], norm_params[1]
    )
    first_low = first_out.astype(jnp.bfloat16)
    queries = linear(first_low, cross_weight[:, :model_width]).astype(jnp.bfloat16)
    cross_context, cross_logsum = attend_forward(
        queries,
        key_value[..., :model_width],
        key_value[..., model_width:],
        cross_allowed,
        head_count,
    )
    second_out, second_normed, second_scale = norm_forward(
        first_out + linear(cross_context, cross_weight[:, model_width:]),
        norm_params[4],
        norm_params[5],
    )
    second_low = second_out.astype(jnp.bfloat16)
    activated, slopes, ffn_result = ffn_forward(second_low, hidden_in, hidden_out)
    third_out, third_normed, third_scale = norm_forward(
        second_out + ffn_result, norm_params[2], norm_params[3]
    )
    gradient, gain_ffn, shift_ffn = norm_backward(
        grad_output, third_normed, third_scale, norm_params[2]
    )
    grad_hidden_in, grad_hidden_out, through = ffn_backward(
        second_low, hidden_in, hidden_out, activated, slopes, gradient
    )
    gradient = gradient + through
    gradient, gain_cross, shift_cross = norm_backward(
        gradient, second_normed, second_scale, norm_params[4]
    )
    grad_branch = gradient.astype(jnp.bfloat16)
    grad_cross_out = outer_sum(cross_context, grad_branch)
    grad_context = linear_back(grad_branch, cross_weight[:, model_width:]).astype(jnp.bfloat16)
    grad_query, grad_key, grad_value = attend_backward(
        queries,
        key_value[..., :model_width],
        key_value[..., model_width:],
        cross_allowed,
        head_count,
        cross_logsum,
        grad_context,
    )
    grad_query = grad_query.astype(jnp.bfloat16)
    grad_cross_in = outer_sum(first_low, grad_query)
    gradient = gradient + linear_back(grad_query, cross_weight[:, :model_width])
    grad_pairs = jnp.concatenate([grad_key, grad_value], -1).astype(jnp.bfloat16)
    gradient, gain_attend, shift_attend = norm_backward(
        gradient, first_normed, first_scale, norm_params[0]
    )
    grad_self_in, grad_self_out, through = self_backward(
        target, self_allowed, self_in, self_out, head_count, projected, context, logsum, gradient
    )
    grad_norms = jnp.stack(
        [gain_attend, shift_attend, gain_ffn, shift_ffn, gain_cross, shift_cross]
    )
    grad_cross = jnp.concatenate([grad_cross_in, grad_cross_out], 1)
    return (
        third_out,
        gradient + through,
        grad_pairs,
        (grad_self_in, grad_self_out, grad_cross, grad_hidden_in, grad_hidden_out, grad_norms),
    )


def add_all(left_part, right_part):
    return tuple((first_term + other_term for first_term, other_term in zip(left_part, right_part)))


MESH = pl.DeviceIdType.MESH
UNITS = 29
ROWS_OUT = UNITS * 16
PARTS = ((0, 160, (0, 1, 2)), (160, 160, (1, 2, 0)), (320, 144, (2, 0, 1)))


def half_of(rows):
    return (rows // 32) * 16


def place():
    dp = lax.axis_index("dp")
    return [lax.div(dp, 16), lax.rem(lax.div(dp, 4), 4), lax.rem(dp, 4)]


def beside(position, axis, step):
    moved = list(position)
    moved[axis] = lax.rem(moved[axis] + (step + 4), 4)
    return {"dp": (moved[0] * 4 + moved[1]) * 4 + moved[2]}


def greet(position):
    barrier = pltpu.get_barrier_semaphore()
    for axis in range(3):
        for step in (1, -1):
            pl.semaphore_signal(barrier, inc=1, device_id=beside(position, axis, step), device_id_type=MESH)
    pl.semaphore_wait(barrier, 6)


def widened(value):
    return value.astype(jnp.float32)


class Ring:
    def __init__(self, source, dim, first, rows, position, axis, scratch, sems):
        self.source, self.dim, self.first, self.rows = source, dim, first, rows
        self.half = half_of(rows)
        self.position, self.axis = position, axis
        self.last, self.next, self.far_last, self.far_next, self.send_last, self.send_next = scratch
        self.sems = sems

    def block(self, step, low, count):
        where = lax.rem(self.position[self.axis] + (step + 4), 4)
        index = [slice(None)] * self.dim + [where]
        index += [slice(None)] * (len(self.source.shape) - 2 - len(index))
        return self.source.at[tuple(index + [pl.ds(self.first + low, count), slice(None)])]

    def copy(self, slot, source, target, step):
        return pltpu.make_async_remote_copy(
            src_ref=source, dst_ref=target, send_sem=self.sems.at[0, slot], recv_sem=self.sems.at[1, slot],
            device_id=beside(self.position, self.axis, step), device_id_type=MESH)

    def rows_of(self, ref, low, count):
        lead = [slice(None)] * (len(ref.shape) - 2)
        return ref.at[tuple(lead + [pl.ds(low, count), slice(None)])]

    def begin(self):
        h, r = self.half, self.rows
        self.copies = [
            self.copy(0, self.block(2, 0, h), self.far_last, 1),
            self.copy(1, self.block(2, h, r - h), self.far_next, -1),
            self.copy(2, self.block(1, h, r - h), self.rows_of(self.last, h, r - h), 1),
            self.copy(3, self.block(-1, 0, h), self.rows_of(self.next, 0, h), -1),
            self.copy(4, self.send_next, self.rows_of(self.last, 0, h), 1),
            self.copy(5, self.send_last, self.rows_of(self.next, h, r - h), -1),
        ]
        for copy in self.copies[:4]:
            copy.start()

    def middle(self):
        h, r = self.half, self.rows
        self.copies[0].wait_recv()
        self.send_next[...] = (widened(self.block(1, 0, h)[...]) + widened(self.far_last[...])).astype(jnp.bfloat16)
        self.copies[4].start()
        self.copies[1].wait_recv()
        self.send_last[...] = (widened(self.block(-1, h, r - h)[...]) + widened(self.far_next[...])).astype(jnp.bfloat16)
        self.copies[5].start()

    def end(self):
        for copy in self.copies[2:]:
            copy.wait_recv()
        return widened(self.block(0, 0, self.rows)[...]) + widened(self.last[...]) + widened(self.next[...])

    def close(self):
        for copy in self.copies:
            copy.wait_send()


def scratch_of(lead, rows):
    h = half_of(rows)
    return [pltpu.VMEM(lead + (n, 128), jnp.bfloat16) for n in (rows, rows, h, rows - h, rows - h, h)]


def sum_kernel(partial_ref, total_ref, *scratch):
    position = place()
    sems = scratch[-1]
    buffers = scratch[:-1]
    greet(position)
    rings = []
    at = 0
    for part, (first, rows, order) in enumerate(PARTS):
        mine = []
        for phase in range(3):
            size = 6 + (1 if phase else 0)
            mine.append(buffers[at : at + size])
            at += size
        rings.append(mine)
    active = []
    for part, (first, rows, order) in enumerate(PARTS):
        active.append(Ring(partial_ref, order[0], first, rows, position, order[0], rings[part][0], sems.at[part, 0]))
    done = []
    for phase in range(3):
        for ring in active:
            ring.begin()
        for ring in active:
            ring.middle()
        following = []
        for part, (first, rows, order) in enumerate(PARTS):
            value = active[part].end()
            done.append(active[part])
            if phase == 2:
                total_ref[first : first + rows, :] = value
                continue
            held = rings[part][phase + 1][6]
            held[...] = value.astype(jnp.bfloat16)
            left = [a for a in (0, 1, 2) if a not in order[: phase + 1]]
            axis = order[phase + 1]
            following.append(Ring(held, left.index(axis), 0, rows, position, axis, rings[part][phase + 1][:6], sems.at[part, phase + 1]))
        active = following
    for ring in done:
        ring.close()


def sum_over_dp(partial):
    shapes = []
    for first, rows, order in PARTS:
        for phase in range(3):
            shapes += scratch_of((4,) * (2 - phase), rows)
            if phase:
                shapes.append(pltpu.VMEM((4,) * (3 - phase) + (rows, 128), jnp.bfloat16))
    return pl.pallas_call(
        sum_kernel,
        out_shape=jax.ShapeDtypeStruct((ROWS_OUT, 128), jnp.float32),
        in_specs=[pl.BlockSpec(memory_space=pltpu.VMEM)],
        out_specs=pl.BlockSpec(memory_space=pltpu.VMEM),
        scratch_shapes=shapes + [pltpu.SemaphoreType.DMA((3, 3, 2, 6))],
        compiler_params=pltpu.CompilerParams(collective_id=1, has_side_effects=True, vmem_limit_bytes=40 << 20),
        name="sum_over_dp",
    )(partial)


def tiles_of(gradient):
    rows, columns = gradient.shape
    if rows == 2048:
        tiles = gradient.reshape(64, 4, 8, columns // 128, 128).transpose(0, 1, 3, 2, 4)
    else:
        tiles = gradient.reshape(64, 8, columns // 128, 128).transpose(0, 2, 1, 3)
    return tiles.reshape(64, -1, 128)


def reduce_end(gradient):
    norms = jnp.pad(gradient[5].reshape(6, 64, 8).transpose(1, 0, 2), ((0, 0), (0, 10), (0, 120)))
    packed = jnp.concatenate([tiles_of(g) for g in gradient[:5]] + [norms], 1).astype(jnp.bfloat16)
    total = sum_over_dp(packed.reshape(4, 4, 4, ROWS_OUT, 128))
    results = []
    at = 0
    for g in gradient[:5]:
        rows, columns = g.shape
        count = rows // 64 * columns // 128
        block = total[at : at + count]
        at += count
        if rows == 2048:
            block = block.reshape(4, columns // 128, 8, 128).transpose(0, 2, 1, 3)
        else:
            block = block.reshape(columns // 128, 8, 128).transpose(1, 0, 2)
        results.append(block.reshape(1, rows // 64, columns))
    results.append(total[at : at + 6, :8][None])
    return tuple(results)


def body(
    tokens,
    cotangent,
    source_lengths,
    target_segments,
    self_in,
    self_out,
    cross_weight,
    hidden_in,
    hidden_out,
    norm_params,
):
    section_index = lax.axis_index("section")
    params = (self_in[0], self_out[0], cross_weight[0], hidden_in[0], hidden_out[0], norm_params[0])
    micro_count = tokens.shape[1]
    bounds = jnp.cumsum(source_lengths, -1)
    places = jnp.arange(tokens.shape[3], dtype=jnp.int32)
    source_ids = jnp.sum(
        (places[None, None, :, None] >= bounds[:, :, None, :]).astype(jnp.int32), -1
    )
    source_masks = source_ids[..., :, None] == source_ids[..., None, :]
    target_masks = target_segments[..., :, None] == target_segments[..., None, :]
    cross_masks = target_segments[..., :, None] == source_ids[..., None, :]

    def encode_all():
        memories = []
        key_values = []
        for micro_index in range(micro_count):
            memory, key_value, stored = encoder_forward(
                tokens[0, micro_index], source_masks[micro_index], params, HEADS
            )
            memories.append(memory)
            key_values.append(key_value)
        return (jnp.stack(memories), jnp.stack(key_values))

    memory_all, key_value_all = on_section(section_index == 0, encode_all)
    arrived = shifted(as_sent(key_value_all), "section", 1).astype(key_value_all.dtype)
    outputs = []
    token_parts = []
    returned = []
    decoder_grads = []
    for micro_index in range(micro_count):
        worker = partial(
            decoder_step,
            tokens[0, micro_index],
            arrived[micro_index],
            target_masks[micro_index],
            cross_masks[micro_index],
            params,
            HEADS,
            cotangent[0, micro_index].astype(jnp.float32),
        )
        output, grad_target, grad_pairs, gradient = on_section(section_index == 1, worker)
        outputs.append(output)
        token_parts.append(grad_target)
        returned.append(grad_pairs)
        decoder_grads.append(gradient)
    returned_all = shifted(jnp.stack(returned), "section", -1)
    collected = []
    for micro_index in range(micro_count):
        worker = partial(
            encoder_step,
            tokens[0, micro_index],
            source_masks[micro_index],
            params,
            HEADS,
            cotangent[0, micro_index].astype(jnp.float32),
            returned_all[micro_index],
        )
        grad_source, gradient = on_section(section_index == 0, worker)
        token_parts[micro_index] = token_parts[micro_index] + grad_source
        combined = add_all(decoder_grads[micro_index], gradient)
        collected.append(combined)
    summed = reduce(add_all, collected)
    summed = reduce_end(summed)
    layer_out = (memory_all + jnp.stack(outputs)).astype(jnp.bfloat16)[None]
    token_grads = jnp.stack(token_parts)[None]
    return (
        layer_out,
        token_grads,
        summed[0],
        summed[1],
        summed[2],
        summed[3],
        summed[4],
        summed[5],
    )


def solution(mesh):
    return jax.shard_map(
        body,
        mesh=mesh,
        in_specs=(
            P("section", None, "dp", None, None),
            P("section", None, "dp", None, None),
            P(None, "dp", None),
            P(None, "dp", None),
            P("section", None, None),
            P("section", None, None),
            P("section", None, None),
            P("section", None, None),
            P("section", None, None),
            P("section", None, None),
        ),
        out_specs=(
            P("section", None, "dp", None, None),
            P("section", None, "dp", None, None),
            P("section", "dp", None),
            P("section", "dp", None),
            P("section", "dp", None),
            P("section", "dp", None),
            P("section", "dp", None),
            P("section", None, "dp"),
        ),
        check_vma=False,
    )
```

```python
import functools
import jax
import jax.numpy as jnp
from jax import lax
from jax.experimental import pallas as pl
from jax.experimental.pallas import tpu as pltpu
from jax.sharding import PartitionSpec as P

HEADS = 8
D = 512
FF = 2048
ROW = 256
NSEG = 8
UNITS = 29
ROWS_OUT = UNITS * 16
root_half = 0.7071067811865476
inverse_root = 0.3989422804014327
F32 = jnp.float32
BF16 = jnp.bfloat16


def dot(a, b):
    return lax.dot_general(a, b, (((1,), (0,)), ((), ())), preferred_element_type=F32)


def dot_nt(a, b):
    return lax.dot_general(a, b, (((1,), (1,)), ((), ())), preferred_element_type=F32)


def dot_tn(a, b):
    return lax.dot_general(a, b, (((0,), (0,)), ((), ())), preferred_element_type=F32)


def sides(factor):
    lane = lax.broadcasted_iota(jnp.int32, (1, 128), 1)
    low = jnp.where(lane < 64, factor, 0.0).astype(BF16)
    high = jnp.where(lane < 64, 0.0, factor).astype(BF16)
    return (low, high)


def attend(query, key, value, bias, shares, context):
    scaled, plain = sides(0.125), sides(1.0)
    for pair in range(HEADS // 2):
        q, k, v = query(pair), key(pair), value(pair)
        total = None
        for side in range(2):
            scores = dot_nt(q * scaled[side], k) + bias[...]
            expval = jnp.exp(scores - jnp.max(scores, -1, keepdims=True))
            share = (expval * (1.0 / jnp.sum(expval, -1, keepdims=True))).astype(BF16)
            shares[2 * pair + side] = share
            part = dot(share, v * plain[side])
            total = part if total is None else total + part
        context[:, 128 * pair : 128 * pair + 128] = total.astype(BF16)


def attend_back(query, key, value, shares, context, grad_context, put_query, put_key, put_value):
    scaled, plain = sides(0.125), sides(1.0)
    for pair in range(HEADS // 2):
        q, k, v = query(pair), key(pair), value(pair)
        columns = slice(128 * pair, 128 * pair + 128)
        g = grad_context[:, columns]
        along = g.astype(F32) * context[:, columns].astype(F32)
        grads = [None, None, None]
        for side in range(2):
            share = shares[2 * pair + side]
            mine = g * plain[side]
            delta = jnp.sum(along * plain[side].astype(F32), -1, keepdims=True)
            ds = (share.astype(F32) * (dot_nt(mine, v) - delta)).astype(BF16)
            parts = (dot(ds, k * scaled[side]), dot_tn(ds, q * scaled[side]), dot_tn(share, mine))
            grads = [p if t is None else t + p for t, p in zip(grads, parts)]
        for put, grad in zip((put_query, put_key, put_value), grads):
            put(pair, grad.astype(BF16))


def mean(values):
    return jnp.sum(values, -1, keepdims=True) * (1.0 / D)


def norm(values, params, which, normed, scale):
    center = values - mean(values)
    inverse = lax.rsqrt(mean(center * center) + 1e-05)
    result = center * inverse
    normed[...] = result
    scale[...] = inverse
    return result * params[2 * which : 2 * which + 1, :] + params[2 * which + 1 : 2 * which + 2, :]


def norm_back(gradient, params, which, normed, scale, grad_norms):
    n = normed[...]
    grad_norms[2 * which : 2 * which + 1, :] = jnp.sum(gradient * n, 0, keepdims=True)
    grad_norms[2 * which + 1 : 2 * which + 2, :] = jnp.sum(gradient, 0, keepdims=True)
    scaled = gradient * params[2 * which : 2 * which + 1, :]
    return scale[...] * (scaled - mean(scaled) - n * mean(scaled * n))


def pack(packed, unit, value):
    shards = value.shape[0] // 8
    blocks = value.reshape(shards, 8, value.shape[1])
    for i in range(value.shape[1] // 256):
        two = jnp.concatenate([blocks[:, :, 256 * i : 256 * i + 128], blocks[:, :, 256 * i + 128 : 256 * i + 256]], 1)
        packed[:, 16 * (unit + i) : 16 * (unit + i) + 16, :] = two.astype(BF16)


def pack_tall(packed, unit, first, value):
    blocks = value.reshape(16, 4, 8, 512)
    for r in range(4):
        for i in range(2):
            two = jnp.concatenate([blocks[:, r, :, 256 * i : 256 * i + 128], blocks[:, r, :, 256 * i + 128 : 256 * i + 256]], 1)
            at = 16 * (unit + 2 * r + i)
            packed[first : first + 16, at : at + 16, :] = two.astype(BF16)


def pack_norms(packed, grad_norms):
    turned = jnp.concatenate([grad_norms[...], jnp.zeros((120, 512), F32)], 0).T
    tiles = turned.reshape(64, 8, 128)
    packed[:, 448:464, :] = jnp.concatenate([tiles, jnp.zeros((64, 8, 128), F32)], 1).astype(BF16)


SELF_IN, SELF_OUT, CROSS, HIDDEN_IN, HIDDEN_OUT = 0, 6, 8, 12, 20


def columns_of(ref, first):
    return lambda pair: ref[:, first + 128 * pair : first + 128 * pair + 128]


def putter(ref, first):
    def put(pair, value):
        ref[:, first + 128 * pair : first + 128 * pair + 128] = value
    return put


def self_forward(inputs, self_in, self_out, bias, params, kept):
    projected, shares, context, normed, scale = kept
    for i in range(3):
        projected[:, 512 * i : 512 * i + 512] = dot(inputs[...], self_in[:, 512 * i : 512 * i + 512]).astype(BF16)
    attend(columns_of(projected, 0), columns_of(projected, 512), columns_of(projected, 1024), bias, shares, context)
    branch = dot(context[...], self_out[...])
    return norm(inputs[...].astype(F32) + branch, params, 0, normed, scale)


def self_backward(gradient, inputs, self_in, self_out, kept, grad_context, grad_projected, packed):
    projected, shares, context, normed, scale = kept
    low = gradient.astype(BF16)
    pack(packed, SELF_OUT, dot_tn(context[...], low))
    grad_context[...] = dot_nt(low, self_out[...]).astype(BF16)
    attend_back(columns_of(projected, 0), columns_of(projected, 512), columns_of(projected, 1024), shares, context, grad_context,
                putter(grad_projected, 0), putter(grad_projected, 512), putter(grad_projected, 1024))
    for i in range(3):
        pack(packed, SELF_IN + 2 * i, dot_tn(inputs[...], grad_projected[:, 512 * i : 512 * i + 512]))
    return dot_nt(grad_projected[...], self_in[...])


def ffn_forward(low, hidden_in, hidden_out, activated, slopes):
    for i in range(4):
        hidden = dot(low[...], hidden_in[:, 512 * i : 512 * i + 512])
        cdf = 0.5 * (1.0 + lax.erf(hidden * root_half))
        activated[:, 512 * i : 512 * i + 512] = (hidden * cdf).astype(BF16)
        slopes[:, 512 * i : 512 * i + 512] = cdf + hidden * jnp.exp(-0.5 * hidden * hidden) * inverse_root
    return dot(activated[...], hidden_out[...])


def ffn_backward(gradient, low, hidden_in, hidden_out, activated, slopes, grad_hidden, packed):
    result = gradient.astype(BF16)
    for i in range(4):
        rows = slice(512 * i, 512 * i + 512)
        grad_hidden[:, rows] = (dot_nt(result, hidden_out[rows, :]) * slopes[:, rows]).astype(BF16)
        pack_tall(packed, HIDDEN_OUT, 16 * i, dot_tn(activated[:, rows], result))
    for i in range(4):
        pack(packed, HIDDEN_IN + 2 * i, dot_tn(low[...], grad_hidden[:, 512 * i : 512 * i + 512]))
    return dot_nt(grad_hidden[...], hidden_in[...])


WEIGHT_SHAPES = ((512, 1536), (512, 512), (512, 1024), (512, 2048), (2048, 512))


def keep_attention():
    return [pltpu.VMEM((256, 1536), BF16), pltpu.VMEM((8, 256, 256), BF16), pltpu.VMEM((256, 512), BF16)]


def keep_norm():
    return [pltpu.VMEM((256, 512), F32), pltpu.VMEM((256, 1), F32)]


def keep_ffn():
    return [pltpu.VMEM((256, 512), BF16), pltpu.VMEM((256, 2048), BF16), pltpu.VMEM((256, 2048), F32)]


def pair_kernel(stages, section, lengths, segments, source, target, cot_memory, cot_third, norm_enc, norm_dec, *rest):
    own, other = rest[:5], rest[5:10]
    memory_out, third_out, source_grad, target_grad, packed_enc, packed_dec = rest[10:16]
    rest = list(rest[16:])

    def take(n):
        taken = rest[:n]
        del rest[:n]
        return taken

    enc_w, dec_w = take(5), take(5)
    enc_self = take(5)
    enc_ffn, enc_n1, enc_n2, memory_low, key_value, grad_key_value = take(3), take(2), take(2), *take(3)
    dec_self = take(5)
    queries, cross_shares, cross_context, dec_n2 = *take(3), take(2)
    first_low = take(1)[0]
    dec_ffn, dec_n1 = take(3), take(2)
    bias, cross_bias, target_bias = take(3)
    carry, grad_context, grad_projected, grad_hidden, grad_norms = take(5)
    sems = take(1)[0]

    me = section[0]

    @pl.when(me == 0)
    def _():
        for i in range(5):
            pltpu.make_async_copy(own[i], enc_w[i], sems.at[0, i]).start()
            pltpu.make_async_copy(other[i], dec_w[i], sems.at[1, i]).start()

    @pl.when(me != 0)
    def _():
        for i in range(5):
            pltpu.make_async_copy(other[i], enc_w[i], sems.at[0, i]).start()
            pltpu.make_async_copy(own[i], dec_w[i], sems.at[1, i]).start()

    def ready(j, i):
        pltpu.make_async_copy(own[i], (enc_w, dec_w)[j][i], sems.at[j, i]).wait()

    def stage_masks():
        lane = lax.broadcasted_iota(jnp.int32, (1, ROW), 1)
        down = lax.broadcasted_iota(jnp.int32, (ROW, 1), 0)
        ids_row, ids_col = jnp.zeros((1, ROW), jnp.int32), jnp.zeros((ROW, 1), jnp.int32)
        bound = jnp.int32(0)
        for j in range(NSEG):
            bound = bound + lengths[j]
            ids_row = ids_row + (lane >= bound).astype(jnp.int32)
            ids_col = ids_col + (down >= bound).astype(jnp.int32)
        tgt_row = segments[...].astype(F32)
        tgt_col = jnp.broadcast_to(tgt_row, (128, ROW)).T[:, 0:1]
        ids_row, ids_col = ids_row.astype(F32), ids_col.astype(F32)
        bias[...] = jnp.where(ids_col == ids_row, 0.0, -1e30)
        target_bias[...] = jnp.where(tgt_col == tgt_row, 0.0, -1e30)
        cross_bias[...] = jnp.where(tgt_col == ids_row, 0.0, -1e30)

    def stage_enc_self():
        ready(0, 0)
        ready(0, 1)
        first = self_forward(source, enc_w[0], enc_w[1], bias, norm_enc, enc_self)
        carry[...] = first
        enc_ffn[0][...] = first.astype(BF16)

    def stage_enc_ffn():
        ready(0, 3)
        ready(0, 4)
        result = ffn_forward(enc_ffn[0], enc_w[3], enc_w[4], enc_ffn[1], enc_ffn[2])
        second = norm(carry[...] + result, norm_enc, 1, *enc_n1)
        memory = norm(second, norm_enc, 2, *enc_n2)
        memory_low[...] = memory.astype(BF16)
        memory_out[...] = memory.astype(BF16)
        ready(0, 2)
        for i in range(2):
            key_value[:, 512 * i : 512 * i + 512] = dot(memory_low[...], enc_w[2][:, 512 * i : 512 * i + 512]).astype(BF16)

    def stage_dec_self():
        ready(1, 0)
        ready(1, 1)
        first = self_forward(target, dec_w[0], dec_w[1], target_bias, norm_dec, dec_self)
        carry[...] = first
        first_low[...] = first.astype(BF16)
        ready(1, 2)
        queries[...] = dot(first_low[...], dec_w[2][:, :512]).astype(BF16)

    def stage_dec_cross():
        attend(columns_of(queries, 0), columns_of(key_value, 0), columns_of(key_value, 512), cross_bias, cross_shares, cross_context)
        second = norm(carry[...] + dot(cross_context[...], dec_w[2][:, 512:]), norm_dec, 2, *dec_n2)
        carry[...] = second
        dec_ffn[0][...] = second.astype(BF16)

    def stage_dec_ffn():
        ready(1, 3)
        ready(1, 4)
        third = norm(carry[...] + ffn_forward(dec_ffn[0], dec_w[3], dec_w[4], dec_ffn[1], dec_ffn[2]), norm_dec, 1, *dec_n1)
        third_out[...] = third.astype(BF16)

    def stage_dec_ffn_back():
        gradient = norm_back(cot_third[...].astype(F32), norm_dec, 1, *dec_n1, grad_norms)
        gradient = gradient + ffn_backward(gradient, *dec_ffn[:1], dec_w[3], dec_w[4], *dec_ffn[1:], grad_hidden, packed_dec)
        carry[...] = norm_back(gradient, norm_dec, 2, *dec_n2, grad_norms)

    def stage_dec_cross_back():
        gradient = carry[...]
        low = gradient.astype(BF16)
        pack(packed_dec, CROSS + 2, dot_tn(cross_context[...], low))
        grad_context[...] = dot_nt(low, dec_w[2][:, 512:]).astype(BF16)
        attend_back(columns_of(queries, 0), columns_of(key_value, 0), columns_of(key_value, 512), cross_shares, cross_context, grad_context,
                    putter(grad_projected, 0), putter(grad_key_value, 0), putter(grad_key_value, 512))
        grad_query = grad_projected[:, :512]
        pack(packed_dec, CROSS, dot_tn(first_low[...], grad_query))
        gradient = gradient + dot_nt(grad_query, dec_w[2][:, :512])
        carry[...] = norm_back(gradient, norm_dec, 0, *dec_self[3:], grad_norms)

    def stage_dec_self_back():
        gradient = carry[...]
        target_grad[...] = gradient + self_backward(gradient, target, dec_w[0], dec_w[1], dec_self, grad_context, grad_projected, packed_dec)
        pack_norms(packed_dec, grad_norms)

    def stage_enc_memory_back():
        for i in range(2):
            pack(packed_enc, CROSS + 2 * i, dot_tn(memory_low[...], grad_key_value[:, 512 * i : 512 * i + 512]))
        gradient = cot_memory[...].astype(F32) + dot_nt(grad_key_value[...], enc_w[2][...])
        gradient = norm_back(gradient, norm_enc, 2, *enc_n2, grad_norms)
        carry[...] = norm_back(gradient, norm_enc, 1, *enc_n1, grad_norms)

    def stage_enc_ffn_back():
        gradient = carry[...]
        gradient = gradient + ffn_backward(gradient, enc_ffn[0], enc_w[3], enc_w[4], *enc_ffn[1:], grad_hidden, packed_enc)
        carry[...] = norm_back(gradient, norm_enc, 0, *enc_self[3:], grad_norms)

    def stage_enc_self_back():
        gradient = carry[...]
        source_grad[...] = gradient + self_backward(gradient, source, enc_w[0], enc_w[1], enc_self, grad_context, grad_projected, packed_enc)
        pack_norms(packed_enc, grad_norms)

    steps = [stage_masks, stage_enc_self, stage_enc_ffn, stage_dec_self, stage_dec_cross, stage_dec_ffn, stage_dec_ffn_back,
             stage_dec_cross_back, stage_dec_self_back, stage_enc_memory_back, stage_enc_ffn_back, stage_enc_self_back]
    grad_norms[...] = jnp.zeros_like(grad_norms)
    for step in steps[:stages]:
        step()
    waited = {(0, 0): 2, (0, 1): 2, (0, 3): 3, (0, 4): 3, (0, 2): 3, (1, 0): 4, (1, 1): 4, (1, 2): 4, (1, 3): 6, (1, 4): 6}
    for (j, i), stage in waited.items():
        if stages < stage:
            ready(j, i)


def run_pair(section, lengths, segments, source, target, cot_memory, cot_third, norm_enc, norm_dec, own, other, stages=12, name="pair"):
    weights = [pltpu.VMEM(shape, BF16) for shape in WEIGHT_SHAPES]
    wide = pltpu.VMEM((256, 512), F32)
    low = pltpu.VMEM((256, 512), BF16)
    square = pltpu.VMEM((256, 256), F32)
    scratch = (weights + weights + keep_attention() + keep_norm() + keep_ffn() + keep_norm() + keep_norm()
               + [low, pltpu.VMEM((256, 1024), BF16), pltpu.VMEM((256, 1024), BF16)]
               + keep_attention() + keep_norm() + [low, pltpu.VMEM((8, 256, 256), BF16), low] + keep_norm() + [low] + keep_ffn() + keep_norm()
               + [square] * 3 + [wide, low, pltpu.VMEM((256, 1536), BF16), pltpu.VMEM((256, 2048), BF16), pltpu.VMEM((8, 512), F32)]
               + [pltpu.SemaphoreType.DMA((2, 5))])
    vmem = pl.BlockSpec(memory_space=pltpu.VMEM)
    smem = pl.BlockSpec(memory_space=pltpu.SMEM)
    hbm = pl.BlockSpec(memory_space=pl.ANY)
    packed = jax.ShapeDtypeStruct((64, ROWS_OUT, 128), BF16)
    return pl.pallas_call(
        functools.partial(pair_kernel, stages),
        out_shape=[jax.ShapeDtypeStruct((256, 512), BF16)] * 2 + [jax.ShapeDtypeStruct((256, 512), F32)] * 2 + [packed, packed],
        in_specs=[smem, smem] + [vmem] * 7 + [hbm] * 10,
        out_specs=[vmem] * 6,
        scratch_shapes=scratch,
        compiler_params=pltpu.CompilerParams(vmem_limit_bytes=60 << 20),
        name=name,
    )(section, lengths, segments, source, target, cot_memory, cot_third, norm_enc, norm_dec, *own, *other)


MESH = pl.DeviceIdType.MESH
PARTS = ((0, 160, (0, 1, 2)), (160, 160, (1, 2, 0)), (320, 144, (2, 0, 1)))


def half_of(rows):
    return (rows // 32) * 16


def place():
    dp = lax.axis_index("dp")
    return [lax.div(dp, 16), lax.rem(lax.div(dp, 4), 4), lax.rem(dp, 4)]


def beside(position, axis, step):
    moved = list(position)
    moved[axis] = lax.rem(moved[axis] + (step + 4), 4)
    return {"dp": (moved[0] * 4 + moved[1]) * 4 + moved[2]}


def greet(position):
    barrier = pltpu.get_barrier_semaphore()
    for axis in range(3):
        for step in (1, -1):
            pl.semaphore_signal(barrier, inc=1, device_id=beside(position, axis, step), device_id_type=MESH)
    pl.semaphore_wait(barrier, 6)


def widened(value):
    return value.astype(jnp.float32)


class Ring:
    def __init__(self, source, dim, first, rows, position, axis, scratch, sems):
        self.source, self.dim, self.first, self.rows = source, dim, first, rows
        self.half = half_of(rows)
        self.position, self.axis = position, axis
        self.last, self.next, self.far_last, self.far_next, self.send_last, self.send_next = scratch
        self.sems = sems

    def block(self, step, low, count):
        where = lax.rem(self.position[self.axis] + (step + 4), 4)
        index = [slice(None)] * self.dim + [where]
        index += [slice(None)] * (len(self.source.shape) - 2 - len(index))
        return self.source.at[tuple(index + [pl.ds(self.first + low, count), slice(None)])]

    def copy(self, slot, source, target, step):
        return pltpu.make_async_remote_copy(
            src_ref=source, dst_ref=target, send_sem=self.sems.at[0, slot], recv_sem=self.sems.at[1, slot],
            device_id=beside(self.position, self.axis, step), device_id_type=MESH)

    def rows_of(self, ref, low, count):
        lead = [slice(None)] * (len(ref.shape) - 2)
        return ref.at[tuple(lead + [pl.ds(low, count), slice(None)])]

    def begin(self):
        h, r = self.half, self.rows
        self.copies = [
            self.copy(0, self.block(2, 0, h), self.far_last, 1),
            self.copy(1, self.block(2, h, r - h), self.far_next, -1),
            self.copy(2, self.block(1, h, r - h), self.rows_of(self.last, h, r - h), 1),
            self.copy(3, self.block(-1, 0, h), self.rows_of(self.next, 0, h), -1),
            self.copy(4, self.send_next, self.rows_of(self.last, 0, h), 1),
            self.copy(5, self.send_last, self.rows_of(self.next, h, r - h), -1),
        ]
        for copy in self.copies[:4]:
            copy.start()

    def middle(self):
        h, r = self.half, self.rows
        self.copies[0].wait_recv()
        self.send_next[...] = (widened(self.block(1, 0, h)[...]) + widened(self.far_last[...])).astype(jnp.bfloat16)
        self.copies[4].start()
        self.copies[1].wait_recv()
        self.send_last[...] = (widened(self.block(-1, h, r - h)[...]) + widened(self.far_next[...])).astype(jnp.bfloat16)
        self.copies[5].start()

    def end(self):
        for copy in self.copies[2:]:
            copy.wait_recv()
        return widened(self.block(0, 0, self.rows)[...]) + widened(self.last[...]) + widened(self.next[...])

    def close(self):
        for copy in self.copies:
            copy.wait_send()


def scratch_of(lead, rows):
    h = half_of(rows)
    return [pltpu.VMEM(lead + (n, 128), jnp.bfloat16) for n in (rows, rows, h, rows - h, rows - h, h)]


def sum_kernel(partial_ref, total_ref, *scratch):
    position = place()
    sems = scratch[-1]
    buffers = scratch[:-1]
    greet(position)
    rings = []
    at = 0
    for part, (first, rows, order) in enumerate(PARTS):
        mine = []
        for phase in range(3):
            size = 6 + (1 if phase else 0)
            mine.append(buffers[at : at + size])
            at += size
        rings.append(mine)
    active = []
    for part, (first, rows, order) in enumerate(PARTS):
        active.append(Ring(partial_ref, order[0], first, rows, position, order[0], rings[part][0], sems.at[part, 0]))
    done = []
    for phase in range(3):
        for ring in active:
            ring.begin()
        for ring in active:
            ring.middle()
        following = []
        for part, (first, rows, order) in enumerate(PARTS):
            value = active[part].end()
            done.append(active[part])
            if phase == 2:
                total_ref[first : first + rows, :] = value
                continue
            held = rings[part][phase + 1][6]
            held[...] = value.astype(jnp.bfloat16)
            left = [a for a in (0, 1, 2) if a not in order[: phase + 1]]
            axis = order[phase + 1]
            following.append(Ring(held, left.index(axis), 0, rows, position, axis, rings[part][phase + 1][:6], sems.at[part, phase + 1]))
        active = following
    for ring in done:
        ring.close()


def sum_over_dp(partial):
    shapes = []
    for first, rows, order in PARTS:
        for phase in range(3):
            shapes += scratch_of((4,) * (2 - phase), rows)
            if phase:
                shapes.append(pltpu.VMEM((4,) * (3 - phase) + (rows, 128), jnp.bfloat16))
    return pl.pallas_call(
        sum_kernel,
        out_shape=jax.ShapeDtypeStruct((ROWS_OUT, 128), jnp.float32),
        in_specs=[pl.BlockSpec(memory_space=pltpu.VMEM)],
        out_specs=pl.BlockSpec(memory_space=pltpu.VMEM),
        scratch_shapes=shapes + [pltpu.SemaphoreType.DMA((3, 3, 2, 6))],
        compiler_params=pltpu.CompilerParams(collective_id=1, has_side_effects=True, vmem_limit_bytes=40 << 20),
        name="sum_over_dp",
    )(partial)


def to_partner(value):
    return lax.ppermute(value, "section", [(0, 1), (1, 0)])


def body(tokens, cotangent, source_lengths, target_segments, self_in, self_out, cross_weight, hidden_in, hidden_out, norm_params):
    section = lax.axis_index("section")
    first = section == 0
    own = (self_in[0], self_out[0], cross_weight[0], hidden_in[0], hidden_out[0])
    other = tuple(to_partner(w) for w in own)
    other_norm = to_partner(norm_params[0])
    norm_enc, norm_dec = jnp.where(first, norm_params[0], other_norm), jnp.where(first, other_norm, norm_params[0])

    def both(array):
        held = lax.dynamic_index_in_dim(array[0, :, 0], section, 0, False)
        received = to_partner(lax.dynamic_index_in_dim(array[0, :, 0], 1 - section, 0, False))
        return jnp.where(first, held, received), jnp.where(first, received, held)

    source, target = both(tokens)
    cot_memory, cot_third = both(cotangent)
    lengths = lax.dynamic_index_in_dim(source_lengths[:, 0], section, 0, False)
    segments = lax.dynamic_index_in_dim(target_segments, section, 0, False)
    memory, third, source_grad, target_grad, packed_enc, packed_dec = run_pair(
        section.reshape(1), lengths, segments, source, target, cot_memory, cot_third, norm_enc, norm_dec, own, other)

    def split(enc, dec):
        held, sent = jnp.where(first, enc, dec), jnp.where(first, dec, enc)
        return held, to_partner(sent)

    def joined(enc, dec):
        held, received = split(enc, dec)
        return jnp.where(first, jnp.stack([held, received]), jnp.stack([received, held]))[None, :, None]

    layer_out = joined(memory, third)
    token_grads = joined(source_grad, target_grad)
    held, received = split(packed_enc, packed_dec)
    packed = (held.astype(F32) + received.astype(F32)).astype(BF16)
    total = sum_over_dp(packed.reshape(4, 4, 4, ROWS_OUT, 128))
    results = []
    at = 0
    for w in own:
        rows, columns = w.shape
        count = rows // 64 * columns // 128
        block = total[at : at + count]
        at += count
        if rows == 2048:
            block = block.reshape(4, columns // 128, 8, 128).transpose(0, 2, 1, 3)
        else:
            block = block.reshape(columns // 128, 8, 128).transpose(1, 0, 2)
        results.append(block.reshape(1, rows // 64, columns))
    results.append(total[at : at + 8, :6].T[None])
    return (layer_out, token_grads, *results)


def solution(mesh):
    return jax.shard_map(
        body,
        mesh=mesh,
        in_specs=(
            P("section", None, "dp", None, None),
            P("section", None, "dp", None, None),
            P(None, "dp", None),
            P(None, "dp", None),
            P("section", None, None),
            P("section", None, None),
            P("section", None, None),
            P("section", None, None),
            P("section", None, None),
            P("section", None, None),
        ),
        out_specs=(
            P("section", None, "dp", None, None),
            P("section", None, "dp", None, None),
            P("section", "dp", None),
            P("section", "dp", None),
            P("section", "dp", None),
            P("section", "dp", None),
            P("section", "dp", None),
            P("section", None, "dp"),
        ),
        check_vma=False,
    )
```

```python
import jax
import jax.numpy as jnp
from jax import lax
from jax.experimental import pallas as pl
from jax.experimental.pallas import tpu as pltpu
from jax.sharding import PartitionSpec as P

HEADS = 8
D = 512
ROW = 256
NSEG = 8
root_half = 0.7071067811865476
inverse_root = 0.3989422804014327
F32 = jnp.float32
BF16 = jnp.bfloat16
MESH = pl.DeviceIdType.MESH
WEIGHTS = ((512, 1536), (512, 512), (512, 1024), (512, 2048), (2048, 512))

HIDDEN_OUT, HIDDEN_IN, CROSS, SELF_OUT, SELF_IN, NORMS = 0, 8, 16, 20, 22, 28
GROUPS = (
    (1, 0, 8, (3, 3, 2), 0),
    (1, 16, 6, (2, 2, 2), 1),
    (0, 0, 10, (3, 3, 4), 0),
    (0, 20, 4, (2, 2, 1), 1),
)
BANKS = ((3, 3, 4), (2, 2, 2))
ORDERS = ((0, 1, 2), (1, 2, 0), (2, 0, 1))
STARTS = (0, 16, 28, 48)
PACKED_UNITS = 58


def unit_of(section, unit):
    if section == 1:
        return 57 if unit == NORMS else unit
    return 52 if unit == NORMS else 28 + unit + (1 if unit >= 24 else 0)


def dot(a, b):
    return lax.dot_general(a, b, (((1,), (0,)), ((), ())), preferred_element_type=F32)


def dot_nt(a, b):
    return lax.dot_general(a, b, (((1,), (1,)), ((), ())), preferred_element_type=F32)


def dot_tn(a, b):
    return lax.dot_general(a, b, (((0,), (0,)), ((), ())), preferred_element_type=F32)

def sides(factor):
    lane = lax.broadcasted_iota(jnp.int32, (1, 128), 1)
    low = jnp.where(lane < 64, factor, 0.0).astype(BF16)
    high = jnp.where(lane < 64, 0.0, factor).astype(BF16)
    return (low, high)


def attend(query, key, value, bias, shares, context):
    scaled, plain = sides(0.125), sides(1.0)
    for pair in range(HEADS // 2):
        q, k, v = query(pair), key(pair), value(pair)
        total = None
        for side in range(2):
            scores = dot_nt(q * scaled[side], k) + bias[...]
            expval = jnp.exp(scores - jnp.max(scores, -1, keepdims=True))
            share = (expval * (1.0 / jnp.sum(expval, -1, keepdims=True))).astype(BF16)
            shares[2 * pair + side] = share
            part = dot(share, v * plain[side])
            total = part if total is None else total + part
        context[:, 128 * pair : 128 * pair + 128] = total.astype(BF16)


def attend_back(query, key, value, shares, context, grad_context, put_query, put_key, put_value):
    scaled, plain = sides(0.125), sides(1.0)
    for pair in range(HEADS // 2):
        q, k, v = query(pair), key(pair), value(pair)
        columns = slice(128 * pair, 128 * pair + 128)
        g = grad_context[:, columns]
        along = g.astype(F32) * context[:, columns].astype(F32)
        grads = [None, None, None]
        for side in range(2):
            share = shares[2 * pair + side]
            mine = g * plain[side]
            delta = jnp.sum(along * plain[side].astype(F32), -1, keepdims=True)
            ds = (share.astype(F32) * (dot_nt(mine, v) - delta)).astype(BF16)
            parts = (dot(ds, k * scaled[side]), dot_tn(ds, q * scaled[side]), dot_tn(share, mine))
            grads = [p if t is None else t + p for t, p in zip(grads, parts)]
        for put, grad in zip((put_query, put_key, put_value), grads):
            put(pair, grad.astype(BF16))


def mean(values):
    return jnp.sum(values, -1, keepdims=True) * (1.0 / D)


def norm(values, params, which, normed, scale):
    center = values - mean(values)
    inverse = lax.rsqrt(mean(center * center) + 1e-05)
    result = center * inverse
    normed[...] = result
    scale[...] = inverse
    return result * params[2 * which : 2 * which + 1, :] + params[2 * which + 1 : 2 * which + 2, :]


def norm_back(gradient, params, which, normed, scale, grad_norms):
    n = normed[...]
    grad_norms[2 * which : 2 * which + 1, :] = jnp.sum(gradient * n, 0, keepdims=True)
    grad_norms[2 * which + 1 : 2 * which + 2, :] = jnp.sum(gradient, 0, keepdims=True)
    scaled = gradient * params[2 * which : 2 * which + 1, :]
    return scale[...] * (scaled - mean(scaled) - n * mean(scaled * n))


def pack(packed, section, unit, value):
    blocks = value.reshape(4, 4, 4, 8, value.shape[1])
    for i in range(value.shape[1] // 256):
        two = jnp.concatenate([blocks[..., 256 * i : 256 * i + 128], blocks[..., 256 * i + 128 : 256 * i + 256]], 3)
        at = 16 * unit_of(section, unit + i)
        packed[:, :, :, at : at + 16, :] = two.astype(BF16)


def pack_tall(packed, section, first, value):
    blocks = value.reshape(4, 4, 4, 8, 512)
    for r in range(4):
        for i in range(2):
            two = jnp.concatenate([blocks[:, :, r, :, 256 * i : 256 * i + 128], blocks[:, :, r, :, 256 * i + 128 : 256 * i + 256]], 2)
            at = 16 * unit_of(section, HIDDEN_OUT + 2 * r + i)
            packed[first, :, :, at : at + 16, :] = two.astype(BF16)


def pack_norms(packed, section, grad_norms):
    turned = jnp.concatenate([grad_norms[...], jnp.zeros((120, 512), F32)], 0).T
    tiles = turned.reshape(4, 4, 4, 8, 128)
    at = 16 * unit_of(section, NORMS)
    packed[:, :, :, at : at + 16, :] = jnp.concatenate([tiles, jnp.zeros_like(tiles)], 3).astype(BF16)

def columns_of(ref, first):
    return lambda pair: ref[:, first + 128 * pair : first + 128 * pair + 128]


def putter(ref, first):
    def put(pair, value):
        ref[:, first + 128 * pair : first + 128 * pair + 128] = value

    return put


def thirds(ref):
    return columns_of(ref, 0), columns_of(ref, 512), columns_of(ref, 1024)


def self_forward(inputs, self_in, self_out, bias, params, projected, shares, context, normed, scale):
    for i in range(3):
        projected[:, 512 * i : 512 * i + 512] = dot(inputs[...], self_in[:, 512 * i : 512 * i + 512]).astype(BF16)
    attend(*thirds(projected), bias, shares, context)
    return norm(inputs[...].astype(F32) + dot(context[...], self_out[...]), params, 0, normed, scale)


def ffn_forward(low, hidden_in, hidden_out, activated, slopes, ready_in, ready_out):
    ready_in()
    for i in range(4):
        hidden = dot(low[...], hidden_in[:, 512 * i : 512 * i + 512])
        cdf = 0.5 * (1.0 + lax.erf(hidden * root_half))
        activated[:, 512 * i : 512 * i + 512] = (hidden * cdf).astype(BF16)
        slope = cdf + hidden * jnp.exp(-0.5 * hidden * hidden) * inverse_root
        slopes[:, 512 * i : 512 * i + 512] = slope.astype(BF16)
    ready_out()
    return dot(activated[...], hidden_out[...])


def place():
    dp = lax.axis_index("dp")
    return [lax.div(dp, 16), lax.rem(lax.div(dp, 4), 4), lax.rem(dp, 4)]


def beside(position, axis, step):
    moved = list(position)
    moved[axis] = lax.rem(moved[axis] + (step + 4), 4)
    return {"dp": (moved[0] * 4 + moved[1]) * 4 + moved[2]}


def partner():
    return {"section": 1 - lax.axis_index("section")}


def remote(source, target, send, receive, device):
    return pltpu.make_async_remote_copy(
        src_ref=source, dst_ref=target, send_sem=send, recv_sem=receive, device_id=device, device_id_type=MESH
    )


def widened(ref):
    return ref[...].astype(F32)


def cut(ref, dim, where, rows):
    index = [slice(None)] * (len(ref.shape) - 2)
    index[dim] = where
    return ref.at[tuple(index + [pl.ds(*rows), slice(None)])]


def halved(ref, side):
    return ref.at[pl.ds(2 * side, 2)]


class Part:
    def __init__(self, position, packed, first, rows, order, buffers, sems):
        self.position, self.packed, self.first, self.rows, self.order = position, packed, first, rows, order
        self.buffers, self.sems = buffers, sems
        self.copies = []

    def where(self, axis, step):
        return lax.rem(self.position[axis] + (step + 4), 4)

    def copy(self, phase, slot, source, target, axis, step):
        made = remote(source, target, self.sems.at[0, phase, slot], self.sems.at[1, phase, slot], beside(self.position, axis, step))
        made.start()
        self.copies.append(made)
        return made

    def block(self, step):
        axis = self.order[0]
        return cut(self.packed, axis, self.where(axis, step), (self.first, self.rows))

    def begin(self):
        axis = self.order[0]
        self.last, self.next, self.far_last, self.far_next, self.send_last, self.send_next = [
            ref.at[:, :, pl.ds(0, self.rows), :] for ref in self.buffers[:6]
        ]
        far = self.block(2)
        self.far = [
            self.copy(0, 0, halved(far, 0), self.far_last, axis, 1),
            self.copy(0, 1, halved(far, 1), self.far_next, axis, -1),
        ]
        self.near = [
            self.copy(0, 2, halved(self.block(1), 1), halved(self.last, 1), axis, 1),
            self.copy(0, 3, halved(self.block(-1), 0), halved(self.next, 0), axis, -1),
        ]

    def middle(self):
        axis = self.order[0]
        self.far[0].wait_recv()
        self.send_next[...] = (widened(halved(self.block(1), 0)) + widened(self.far_last)).astype(BF16)
        self.near.append(self.copy(0, 4, self.send_next, halved(self.last, 0), axis, 1))
        self.far[1].wait_recv()
        self.send_last[...] = (widened(halved(self.block(-1), 1)) + widened(self.far_next)).astype(BF16)
        self.near.append(self.copy(0, 5, self.send_last, halved(self.next, 1), axis, -1))

    def end(self):
        for made in self.near:
            made.wait_recv()
        self.held = self.buffers[6]
        self.held[...] = (widened(self.block(0)) + widened(self.last) + widened(self.next)).astype(BF16)
        for made in self.copies:
            made.wait_send()
        self.copies = []

    def direct(self, phase):
        axis = self.order[phase]
        left = sorted(self.order[phase:])
        dim = left.index(axis)
        slots = self.buffers[4 + 4 * phase - 1 : 4 + 4 * phase + 2]
        self.near = [
            self.copy(phase, i, cut(self.held, dim, self.where(axis, step), (0, self.rows)), slots[i], axis, step)
            for i, step in enumerate((2, 1, -1))
        ]
        self.own = (self.held, dim, axis, slots)

    def arrived(self):
        for made in self.near:
            made.wait_recv()
        held, dim, axis, slots = self.own
        total = widened(cut(held, dim, self.where(axis, 0), (0, self.rows)))
        for slot in slots:
            total = total + widened(slot)
        return total

    def hold(self, value):
        self.held = self.buffers[10]
        self.held[...] = value.astype(BF16)

    def close(self):
        for made in self.copies:
            made.wait_send()


def bank_buffers(units):
    rows = 16 * units
    whole, half = (4, 4, rows, 128), (2, 4, rows, 128)
    return [pltpu.VMEM(shape, BF16) for shape in (whole, whole, half, half, half, half)]


def part_buffers(units):
    rows = 16 * units
    one, two = (rows, 128), (4, rows, 128)
    return [pltpu.VMEM(shape, BF16) for shape in ((4, 4, rows, 128), two, two, two, two, one, one, one)]


class Group:
    def __init__(self, which, position, packed, arrivals, totals, banks, own, sems, credits):
        self.section, self.first, self.half, self.parts, self.bank = GROUPS[which]
        self.again = which >= 2
        self.reused = which < 2
        self.position, self.packed, self.totals = position, packed, totals
        self.me = lax.axis_index("section")
        self.swap_sems, self.part_sems, self.total_sems = sems
        self.swap_credit, self.part_credit = credits
        self.units = sum(self.parts)
        self.arrival = arrivals[self.bank]
        self.offsets = [sum(self.parts[:i]) for i in range(3)]
        self.work = []
        for i in range(3):
            first = 16 * (STARTS[which] + self.offsets[i]) + self.me * (16 * self.units)
            first = pl.multiple_of(first, 16)
            buffers = list(banks[self.bank][i]) + list(own[i])
            self.work.append(Part(position, packed, first, 16 * self.parts[i], ORDERS[i], buffers, self.part_sems.at[i]))
        self.swaps = []
        for i in range(3):
            rows = 16 * self.parts[i]
            first = 16 * (STARTS[which] + self.offsets[i]) + (1 - self.me) * (16 * self.units)
            source = packed.at[:, :, :, pl.ds(pl.multiple_of(first, 16), rows), :]
            target = self.arrival.at[:, :, :, pl.ds(16 * self.offsets[i], rows), :]
            self.swaps.append(remote(source, target, self.swap_sems.at[0, i], self.swap_sems.at[1, i], partner()))

    def steps(self):
        if self.again:
            pl.semaphore_wait(self.swap_credit, 1)
        for swap in self.swaps:
            swap.start()
        yield
        for i, part in enumerate(self.work):
            self.swaps[i].wait_recv()
            mine = self.packed.at[:, :, :, pl.ds(part.first, part.rows), :]
            mine[...] = mine[...] + self.arrival[:, :, :, 16 * self.offsets[i] : 16 * self.offsets[i] + part.rows, :]
            if self.again:
                pl.semaphore_wait(self.part_credit.at[i], 2)
            part.begin()
        if self.reused:
            pl.semaphore_signal(self.swap_credit, inc=1, device_id=partner(), device_id_type=MESH)
        yield
        for part in self.work:
            part.middle()
        yield
        for i, part in enumerate(self.work):
            part.end()
            if self.reused:
                for step in (1, -1):
                    pl.semaphore_signal(self.part_credit.at[i], inc=1, device_id=beside(self.position, part.order[0], step), device_id_type=MESH)
            part.direct(1)
        yield
        for part in self.work:
            part.hold(part.arrived())
            part.direct(2)
        yield
        base = 16 * (self.first + self.me * self.half)
        for i, part in enumerate(self.work):
            total = part.arrived()
            at = pl.multiple_of(base + 16 * self.offsets[i], 16)
            if self.offsets[i] < self.half:
                self.totals[self.section, pl.ds(at, part.rows), :] = total
            else:
                self.totals[self.me, 16 * NORMS : 16 * NORMS + 16, :] = total
        mine = self.totals.at[self.section, pl.ds(pl.multiple_of(base, 16), 16 * self.half), :]
        self.handed = remote(mine, mine, self.total_sems.at[0], self.total_sems.at[1], partner())

        @pl.when(self.me != self.section)
        def _():
            self.handed.start()

        yield

    def close(self):
        for swap in self.swaps:
            swap.wait_send()
        for part in self.work:
            part.close()
        theirs = pl.multiple_of(16 * (self.first + (1 - self.me) * self.half), 16)
        other = self.totals.at[self.section, pl.ds(theirs, 16 * self.half), :]

        @pl.when(self.me != self.section)
        def _():
            self.handed.wait_send()

        @pl.when(self.me == self.section)
        def _():
            remote(other, other, self.total_sems.at[0], self.total_sems.at[1], partner()).wait_recv()


def keep_attention():
    return [pltpu.VMEM((256, 1536), BF16), pltpu.VMEM((8, 256, 256), BF16), pltpu.VMEM((256, 512), BF16)]


def keep_norm():
    return [pltpu.VMEM((256, 512), F32), pltpu.VMEM((256, 1), F32)]


def keep_ffn():
    return [pltpu.VMEM((256, 512), BF16), pltpu.VMEM((256, 2048), BF16), pltpu.VMEM((256, 2048), BF16)]


def stacked(scratch):
    return [pltpu.VMEM((2,) + tuple(s.shape), s.dtype) for s in scratch]


def scratch_shapes():
    low, wide, square = pltpu.VMEM((256, 512), BF16), pltpu.VMEM((256, 512), F32), pltpu.VMEM((256, 256), F32)
    return dict(
        weights=stacked([pltpu.VMEM(shape, BF16) for shape in WEIGHTS]),
        inputs=stacked([low, low, pltpu.VMEM((6, 512), F32)]),
        selfs=stacked(keep_attention() + keep_norm()),
        firsts=stacked([low, wide]),
        enc=keep_ffn()[1:] + keep_norm() + keep_norm() + [low, pltpu.VMEM((256, 1024), BF16)],
        cross=[low, pltpu.VMEM((8, 256, 256), BF16), low] + keep_norm(),
        dec=keep_ffn() + keep_norm(),
        bias=[pltpu.VMEM((2, 256, 256), F32), square],
        work=[wide, low, pltpu.VMEM((8, 512), F32)],
        results=[low, wide, low, wide],
        packed=pltpu.VMEM((4, 4, 4, 16 * PACKED_UNITS, 128), BF16),
        arrivals=[pltpu.VMEM((4, 4, 4, 16 * sum(units), 128), BF16) for units in BANKS],
        banks=[[bank_buffers(units) for units in bank] for bank in BANKS],
        parts=[[part_buffers(units) for units in group[3]] for group in GROUPS],
        totals=pltpu.VMEM((2, 464, 128), F32),
        in_sems=pltpu.SemaphoreType.DMA((2, 8)),
        in_sends=pltpu.SemaphoreType.DMA((8,)),
        out_sems=pltpu.SemaphoreType.DMA((3, 2)),
        swap_sems=pltpu.SemaphoreType.DMA((4, 2, 3)),
        part_sems=pltpu.SemaphoreType.DMA((4, 3, 2, 3, 6)),
        total_sems=pltpu.SemaphoreType.DMA((4, 2)),
        swap_credit=pltpu.SemaphoreType.REGULAR((2,)),
        part_credit=pltpu.SemaphoreType.REGULAR((2, 3)),
    )


def whole_kernel(tree, *refs):
    tokens, cotangent, lengths, segments = refs[:4]
    own = refs[4:9]
    norm_params = refs[9]
    layer_out, token_grads = refs[10:12]
    grad_refs, grad_norms_out = refs[12:17], refs[17]
    s = jax.tree.unflatten(tree, refs[18:])
    me = lax.axis_index("section")
    position = place()

    barrier = pltpu.get_barrier_semaphore()
    pl.semaphore_signal(barrier, inc=1, device_id=partner(), device_id_type=MESH)
    for axis in range(3):
        for step in (1, -1):
            pl.semaphore_signal(barrier, inc=1, device_id=beside(position, axis, step), device_id_type=MESH)

    held = list(s["weights"]) + list(s["inputs"])

    def given(i, micro):
        if i < 5:
            return own[i].at[0]
        if i == 7:
            return norm_params.at[0]
        return (tokens, cotangent)[i - 5].at[0, micro, 0]

    def local(i):
        return pltpu.make_async_copy(given(i, me), held[i].at[me], s["in_sems"].at[me, i])

    def sent(i):
        return remote(given(i, 1 - me), held[i].at[me], s["in_sends"].at[i], s["in_sems"].at[me, i], partner())

    def ready(j, i):
        pltpu.make_async_copy(given(i, 0), held[i].at[j], s["in_sems"].at[j, i]).wait()

    for i in (5, 0, 7, 1, 3, 4, 2, 6):
        local(i).start()

    bias, cross_bias = s["bias"]
    lane = lax.broadcasted_iota(jnp.int32, (1, ROW), 1)
    down = lax.broadcasted_iota(jnp.int32, (ROW, 1), 0)
    ids_row, ids_col = jnp.zeros((1, ROW), jnp.int32), jnp.zeros((ROW, 1), jnp.int32)
    bound = jnp.int32(0)
    for j in range(NSEG):
        bound = bound + lengths[me, 0, j]
        ids_row = ids_row + (lane >= bound).astype(jnp.int32)
        ids_col = ids_col + (down >= bound).astype(jnp.int32)
    target_row = segments[me].astype(F32)
    target_col = jnp.broadcast_to(target_row, (128, ROW)).T[:, 0:1]
    ids_row, ids_col = ids_row.astype(F32), ids_col.astype(F32)
    bias[0] = jnp.where(ids_col == ids_row, 0.0, -1e30)
    bias[1] = jnp.where(target_col == target_row, 0.0, -1e30)
    cross_bias[...] = jnp.where(target_col == ids_row, 0.0, -1e30)

    pl.semaphore_wait(barrier, 7)
    for i in (5, 7, 0, 1):
        sent(i).start()

    @pl.when(me == 0)
    def _():
        for i in (3, 4, 2):
            sent(i).start()

    @pl.when(me != 0)
    def _():
        for i in (2, 3, 4):
            sent(i).start()

    sent(6).start()

    w_self_in, w_self_out, w_cross, w_in, w_out = s["weights"]
    x, cot, norms = s["inputs"]
    first_low, first = s["firsts"]
    work, grad_context, grad_norms = s["work"]
    memory_low, source_grad, third_low, target_grad = s["results"]

    def self_block(i, carry):
        j = lax.rem(me + i, 2)
        for which in (5, 0, 7, 1):
            ready(j, which)
        projected, shares, context, normed, scale = [ref.at[j] for ref in s["selfs"]]
        result = self_forward(x.at[j], w_self_in.at[j], w_self_out.at[j], bias.at[j], norms.at[j], projected, shares, context, normed, scale)
        first[j] = result
        first_low[j] = result.astype(BF16)
        return carry

    lax.fori_loop(0, 2, self_block, 0)

    enc_active, enc_slopes, enc_normed, enc_scale, memory_normed, memory_scale, memory_keep, key_value = s["enc"]
    queries, cross_shares, cross_context, cross_normed, cross_scale = s["cross"]
    dec_low, dec_active, dec_slopes, dec_normed, dec_scale = s["dec"]
    enc_self, dec_self = [ref.at[0] for ref in s["selfs"]], [ref.at[1] for ref in s["selfs"]]
    enc_norms, dec_norms = norms.at[0], norms.at[1]

    result = ffn_forward(first_low.at[0], w_in.at[0], w_out.at[0], enc_active, enc_slopes, lambda: ready(0, 3), lambda: ready(0, 4))
    second = norm(first[0] + result, enc_norms, 1, enc_normed, enc_scale)
    memory = norm(second, enc_norms, 2, memory_normed, memory_scale).astype(BF16)
    memory_low[...] = memory
    ready(0, 2)
    for i in range(2):
        key_value[:, 512 * i : 512 * i + 512] = dot(memory, w_cross[0, :, 512 * i : 512 * i + 512]).astype(BF16)

    ready(1, 2)
    queries[...] = dot(first_low[1], w_cross[1, :, :512]).astype(BF16)
    keys_values = (columns_of(key_value, 0), columns_of(key_value, 512))
    attend(columns_of(queries, 0), *keys_values, cross_bias, cross_shares, cross_context)
    second = norm(first[1] + dot(cross_context[...], w_cross[1, :, 512:]), dec_norms, 2, cross_normed, cross_scale)
    dec_low[...] = second.astype(BF16)
    result = ffn_forward(dec_low, w_in.at[1], w_out.at[1], dec_active, dec_slopes, lambda: ready(1, 3), lambda: ready(1, 4))
    third_low[...] = norm(second + result, dec_norms, 1, dec_normed, dec_scale).astype(BF16)

    def put_out(slot, out, values):
        for j in range(2):
            here = pltpu.make_async_copy(values[j], out.at[0, me, 0], s["out_sems"].at[0, slot])
            there = remote(values[j], out.at[0, me, 0], s["out_sems"].at[1, slot], s["out_sems"].at[2, slot], partner())

            @pl.when(me == j)
            def _():
                here.start()

            @pl.when(me != j)
            def _():
                there.start()

    def out_done(slot, out, values):
        pltpu.make_async_copy(values[0], out.at[0, me, 0], s["out_sems"].at[0, slot]).wait()
        there = remote(values[0], out.at[0, me, 0], s["out_sems"].at[1, slot], s["out_sems"].at[2, slot], partner())
        there.wait_send()
        there.wait_recv()

    put_out(0, layer_out, (memory_low, third_low))

    packed = s["packed"]
    groups = [
        Group(g, position, packed, s["arrivals"], s["totals"], s["banks"], s["parts"][g],
              (s["swap_sems"].at[g], s["part_sems"].at[g], s["total_sems"].at[g]),
              (s["swap_credit"].at[GROUPS[g][4]], s["part_credit"].at[GROUPS[g][4]]))
        for g in range(4)
    ]
    running = [group.steps() for group in groups]

    def pump(*which):
        for g in which:
            next(running[g])

    def ffn_back(gradient, low, section, activated, slopes):
        result = gradient.astype(BF16)
        for i in range(4):
            rows = slice(512 * i, 512 * i + 512)
            slopes[:, rows] = (dot_nt(result, w_out[section, rows, :]) * slopes[:, rows].astype(F32)).astype(BF16)
            pack_tall(packed, section, i, dot_tn(activated[:, rows], result))
        for i in range(4):
            pack(packed, section, HIDDEN_IN + 2 * i, dot_tn(low[...], slopes[:, 512 * i : 512 * i + 512]))
        return dot_nt(slopes[...], w_in[section])

    def self_back_a(gradient, section, kept):
        projected, shares, context, normed, scale = kept
        low = gradient.astype(BF16)
        pack(packed, section, SELF_OUT, dot_tn(context[...], low))
        grad_context[...] = dot_nt(low, w_self_out[section]).astype(BF16)

    def self_back_b(section, kept):
        projected, shares, context, normed, scale = kept
        attend_back(*thirds(projected), shares, context, grad_context, *[putter(projected, 512 * i) for i in range(3)])

    def self_back_c(section, kept):
        projected = kept[0]
        for i in range(3):
            pack(packed, section, SELF_IN + 2 * i, dot_tn(x[section], projected[:, 512 * i : 512 * i + 512]))
        pack_norms(packed, section, grad_norms)

    grad_norms[...] = jnp.zeros_like(grad_norms)
    ready(1, 6)
    gradient = norm_back(cot[1].astype(F32), dec_norms, 1, dec_normed, dec_scale, grad_norms)
    gradient = gradient + ffn_back(gradient, dec_low, 1, dec_active, dec_slopes)
    pump(0)
    gradient = norm_back(gradient, dec_norms, 2, cross_normed, cross_scale, grad_norms)
    work[...] = gradient
    low = gradient.astype(BF16)
    pack(packed, 1, CROSS + 2, dot_tn(cross_context[...], low))
    grad_context[...] = dot_nt(low, w_cross[1, :, 512:]).astype(BF16)
    attend_back(columns_of(queries, 0), *keys_values, cross_shares, cross_context, grad_context,
                putter(queries, 0), putter(key_value, 0), putter(key_value, 512))
    pump(0)
    pack(packed, 1, CROSS, dot_tn(first_low[1], queries[...]))
    gradient = work[...] + dot_nt(queries[...], w_cross[1, :, :512])
    gradient = norm_back(gradient, dec_norms, 0, *dec_self[3:], grad_norms)
    work[...] = gradient
    self_back_a(gradient, 1, dec_self)
    pump(0)
    self_back_b(1, dec_self)
    self_back_c(1, dec_self)
    pump(1, 0)
    target_grad[...] = work[...] + dot_nt(dec_self[0][...], w_self_in[1])

    for i in range(2):
        pack(packed, 0, CROSS + 2 * i, dot_tn(memory_low[...], key_value[:, 512 * i : 512 * i + 512]))
    ready(0, 6)
    gradient = cot[0].astype(F32) + dot_nt(key_value[...], w_cross[0])
    gradient = norm_back(gradient, enc_norms, 2, memory_normed, memory_scale, grad_norms)
    gradient = norm_back(gradient, enc_norms, 1, enc_normed, enc_scale, grad_norms)
    pump(1, 0)
    gradient = gradient + ffn_back(gradient, first_low.at[0], 0, enc_active, enc_slopes)
    pump(2, 1, 0)
    gradient = norm_back(gradient, enc_norms, 0, *enc_self[3:], grad_norms)
    work[...] = gradient
    self_back_a(gradient, 0, enc_self)
    pump(1)
    self_back_b(0, enc_self)
    pump(2, 1)
    self_back_c(0, enc_self)
    pump(3, 1)
    source_grad[...] = work[...] + dot_nt(enc_self[0][...], w_self_in[0])
    put_out(1, token_grads, (source_grad, target_grad))
    pump(2, 3, 2, 3, 2, 3, 2, 3, 3)

    for group in groups:
        group.close()
    totals = s["totals"]

    def tile(t):
        return totals[me, 8 * t : 8 * t + 8, :]

    for which, unit, columns in ((0, SELF_IN, 1536), (1, SELF_OUT, 512), (2, CROSS, 1024), (3, HIDDEN_IN, 2048)):
        for i in range(columns // 128):
            grad_refs[which][0, :, 128 * i : 128 * i + 128] = tile(2 * unit + i)
    for r in range(4):
        for i in range(4):
            grad_refs[4][0, 8 * r : 8 * r + 8, 128 * i : 128 * i + 128] = tile(2 * HIDDEN_OUT + 4 * r + i)
    turned = jnp.concatenate([tile(2 * NORMS), jnp.zeros((120, 128), F32)], 0).T
    grad_norms_out[0] = turned[:6, :8]
    for i in range(8):
        sent(i).wait_send()
    out_done(0, layer_out, (memory_low, third_low))
    out_done(1, token_grads, (source_grad, target_grad))


def body(tokens, cotangent, source_lengths, target_segments, self_in, self_out, cross_weight, hidden_in, hidden_out, norm_params):
    shapes, tree = jax.tree.flatten(scratch_shapes())
    vmem, smem, hbm = [pl.BlockSpec(memory_space=space) for space in (pltpu.VMEM, pltpu.SMEM, pl.ANY)]
    f32 = [(1, 8, 1536), (1, 8, 512), (1, 8, 1024), (1, 8, 2048), (1, 32, 512), (1, 6, 8)]
    return tuple(pl.pallas_call(
        lambda *refs: whole_kernel(tree, *refs),
        out_shape=[jax.ShapeDtypeStruct(tokens.shape, BF16), jax.ShapeDtypeStruct(tokens.shape, F32)]
        + [jax.ShapeDtypeStruct(shape, F32) for shape in f32],
        in_specs=[hbm, hbm, smem, vmem] + [hbm] * 6,
        out_specs=[hbm, hbm] + [vmem] * 6,
        scratch_shapes=shapes,
        compiler_params=pltpu.CompilerParams(collective_id=0, has_side_effects=True, vmem_limit_bytes=64 << 20),
        name="layer_pair",
    )(tokens, cotangent, source_lengths, target_segments, self_in, self_out, cross_weight, hidden_in, hidden_out, norm_params))


def solution(mesh):
    return jax.shard_map(
        body,
        mesh=mesh,
        in_specs=(
            P("section", None, "dp", None, None),
            P("section", None, "dp", None, None),
            P(None, "dp", None),
            P(None, "dp", None),
            P("section", None, None),
            P("section", None, None),
            P("section", None, None),
            P("section", None, None),
            P("section", None, None),
            P("section", None, None),
        ),
        out_specs=(
            P("section", None, "dp", None, None),
            P("section", None, "dp", None, None),
            P("section", "dp", None),
            P("section", "dp", None),
            P("section", "dp", None),
            P("section", "dp", None),
            P("section", "dp", None),
            P("section", None, "dp"),
        ),
        check_vma=False,
    )
```

```python
import jax
import jax.numpy as jnp
from jax import lax
from jax.experimental import pallas as pl
from jax.experimental.pallas import tpu as pltpu
from jax.sharding import PartitionSpec as P

HEADS = 8
D = 512
ROW = 256
NSEG = 8
root_half = 0.7071067811865476
inverse_root = 0.3989422804014327
F32 = jnp.float32
BF16 = jnp.bfloat16
MESH = pl.DeviceIdType.MESH
WEIGHTS = ((512, 1536), (512, 512), (512, 1024), (512, 2048), (2048, 512))

HIDDEN_OUT, HIDDEN_IN, CROSS, SELF_OUT, SELF_IN, NORMS = 0, 8, 16, 20, 22, 28
GROUPS = (
    (1, 0, 8, (3, 3, 2), 0),
    (1, 16, 6, (2, 2, 2), 1),
    (0, 0, 10, (3, 3, 4), 0),
    (0, 20, 4, (2, 2, 1), 1),
)
BANKS = ((3, 3, 4), (2, 2, 2))
ORDERS = ((0, 1, 2), (1, 2, 0), (2, 0, 1))
STARTS = (0, 16, 28, 48)
SCHEDULE = dict(
    dec_in3="0s",
    dec_attend="0b 0a",
    dec_end="0c",
    memory_start="1s",
    enc_in0="0b 0a 0c 1a 1b",
    enc_in3="2s 1c",
    enc_start="0b 0c 0a",
    enc_attend="1c 1b 1a 2a",
    enc_end="2b 2c 3s",
    last="1c 1a 3a 0a 2b 3c 2c 1b 3b 2a 1c 0c 3a 3b 3c 2c 2a 2b 3a 3b 3c 0c 2a 2b 0b 1a 2c 1b 3a 3c 3b 1a 0b 1c 1b 2b 2a 0a 3a 2c 3c 3b",
)
PACKED_UNITS = 58


def unit_of(section, unit):
    if section == 1:
        return 57 if unit == NORMS else unit
    return 52 if unit == NORMS else 28 + unit + (1 if unit >= 24 else 0)


def dot(a, b):
    return lax.dot_general(a, b, (((1,), (0,)), ((), ())), preferred_element_type=F32)


def dot_nt(a, b):
    return lax.dot_general(a, b, (((1,), (1,)), ((), ())), preferred_element_type=F32)


def dot_tn(a, b):
    return lax.dot_general(a, b, (((0,), (0,)), ((), ())), preferred_element_type=F32)

def sides(factor):
    lane = lax.broadcasted_iota(jnp.int32, (1, 128), 1)
    low = jnp.where(lane < 64, factor, 0.0).astype(BF16)
    high = jnp.where(lane < 64, 0.0, factor).astype(BF16)
    return (low, high)


def attend(query, key, value, bias, shares, context):
    scaled, plain = sides(0.125), sides(1.0)
    heads = [(pair, side) for pair in range(HEADS // 2) for side in range(2)]
    scores = [dot_nt(query(pair) * scaled[side], key(pair)) + bias[...] for pair, side in heads]
    expvals = [jnp.exp(score - jnp.max(score, -1, keepdims=True)) for score in scores]
    low = [(expval * (1.0 / jnp.sum(expval, -1, keepdims=True))).astype(BF16) for expval in expvals]
    for head in range(HEADS):
        shares[head] = low[head]
    for pair in range(HEADS // 2):
        parts = [dot(low[2 * pair + side], value(pair) * plain[side]) for side in range(2)]
        context[:, 128 * pair : 128 * pair + 128] = (parts[0] + parts[1]).astype(BF16)


def attend_back(query, key, value, shares, context, grad_context, put_query, put_key, put_value):
    scaled, plain = sides(0.125), sides(1.0)
    heads = [(pair, side) for pair in range(HEADS // 2) for side in range(2)]
    given = [grad_context[:, 128 * pair : 128 * pair + 128] for pair in range(HEADS // 2)]
    along = [given[pair].astype(F32) * context[:, 128 * pair : 128 * pair + 128].astype(F32) for pair in range(HEADS // 2)]
    grad_shares = [dot_nt(given[pair] * plain[side], value(pair)) for pair, side in heads]
    deltas = [jnp.sum(along[pair] * plain[side].astype(F32), -1, keepdims=True) for pair, side in heads]
    low = [(shares[i].astype(F32) * (grad_shares[i] - deltas[i])).astype(BF16) for i in range(HEADS)]
    for pair in range(HEADS // 2):
        q, k, g = query(pair), key(pair), given[pair]
        one, two = low[2 * pair], low[2 * pair + 1]
        grad_query = dot(one, k * scaled[0]) + dot(two, k * scaled[1])
        grad_key = dot_tn(one, q * scaled[0]) + dot_tn(two, q * scaled[1])
        grad_value = dot_tn(shares[2 * pair], g * plain[0]) + dot_tn(shares[2 * pair + 1], g * plain[1])
        put_query(pair, grad_query.astype(BF16))
        put_key(pair, grad_key.astype(BF16))
        put_value(pair, grad_value.astype(BF16))


def mean(values):
    return jnp.sum(values, -1, keepdims=True) * (1.0 / D)


def norm(values, params, which, normed, scale):
    center = values - mean(values)
    inverse = lax.rsqrt(mean(center * center) + 1e-05)
    result = center * inverse
    normed[...] = result
    scale[...] = inverse
    return result * params[2 * which] + params[2 * which + 1]


def norm_back(gradient, params, which, normed, scale, grad_norms):
    n = normed[...]
    grad_norms[2 * which : 2 * which + 1, :] = jnp.sum(gradient * n, 0, keepdims=True)
    grad_norms[2 * which + 1 : 2 * which + 2, :] = jnp.sum(gradient, 0, keepdims=True)
    scaled = gradient * params[2 * which]
    return scale[...] * (scaled - mean(scaled) - n * mean(scaled * n))


def pack(packed, section, unit, value):
    blocks = value.reshape(4, 4, 4, 8, value.shape[1])
    for i in range(value.shape[1] // 256):
        two = jnp.concatenate([blocks[..., 256 * i : 256 * i + 128], blocks[..., 256 * i + 128 : 256 * i + 256]], 3)
        at = 16 * unit_of(section, unit + i)
        packed[:, :, :, at : at + 16, :] = two.astype(BF16)


def pack_tall(packed, section, first, value):
    blocks = value.reshape(4, 4, 4, 8, 512)
    for r in range(4):
        for i in range(2):
            two = jnp.concatenate([blocks[:, :, r, :, 256 * i : 256 * i + 128], blocks[:, :, r, :, 256 * i + 128 : 256 * i + 256]], 2)
            at = 16 * unit_of(section, HIDDEN_OUT + 2 * r + i)
            packed[first, :, :, at : at + 16, :] = two.astype(BF16)


def pack_norms(packed, section, grad_norms):
    turned = jnp.concatenate([grad_norms[...], jnp.zeros((120, 512), F32)], 0).T
    tiles = turned.reshape(4, 4, 4, 8, 128)
    at = 16 * unit_of(section, NORMS)
    packed[:, :, :, at : at + 16, :] = jnp.concatenate([tiles, jnp.zeros_like(tiles)], 3).astype(BF16)

def columns_of(ref, first):
    return lambda pair: ref[:, first + 128 * pair : first + 128 * pair + 128]


def putter(ref, first):
    def put(pair, value):
        ref[:, first + 128 * pair : first + 128 * pair + 128] = value

    return put


def thirds(ref):
    return columns_of(ref, 0), columns_of(ref, 512), columns_of(ref, 1024)


def self_forward(inputs, self_in, self_out, bias, params, projected, shares, context, normed, scale):
    for i in range(3):
        projected[:, 512 * i : 512 * i + 512] = dot(inputs[...], self_in[:, 512 * i : 512 * i + 512]).astype(BF16)
    attend(*thirds(projected), bias, shares, context)
    return norm(inputs[...].astype(F32) + dot(context[...], self_out[...]), params, 0, normed, scale)


def ffn_forward(low, hidden_in, hidden_out, activated, slopes, ready_in, ready_out):
    ready_in()
    for i in range(4):
        hidden = dot(low[...], hidden_in[:, 512 * i : 512 * i + 512])
        cdf = 0.5 * (1.0 + lax.erf(hidden * root_half))
        activated[:, 512 * i : 512 * i + 512] = (hidden * cdf).astype(BF16)
        slope = cdf + hidden * jnp.exp(-0.5 * hidden * hidden) * inverse_root
        slopes[:, 512 * i : 512 * i + 512] = slope.astype(BF16)
    ready_out()
    return dot(activated[...], hidden_out[...])


def place():
    dp = lax.axis_index("dp")
    return [lax.div(dp, 16), lax.rem(lax.div(dp, 4), 4), lax.rem(dp, 4)]


def beside(position, axis, step):
    moved = list(position)
    moved[axis] = lax.rem(moved[axis] + (step + 4), 4)
    return {"dp": (moved[0] * 4 + moved[1]) * 4 + moved[2]}


def across(position, axis, step):
    return dict(beside(position, axis, step), section=1 - lax.axis_index("section"))


def partner():
    return {"section": 1 - lax.axis_index("section")}


def remote(source, target, send, receive, device):
    return pltpu.make_async_remote_copy(
        src_ref=source, dst_ref=target, send_sem=send, recv_sem=receive, device_id=device, device_id_type=MESH
    )


def widened(ref):
    return ref[...].astype(F32)


def cut(ref, dim, where, rows):
    index = [slice(None)] * (len(ref.shape) - 2)
    index[dim] = where
    return ref.at[tuple(index + [pl.ds(*rows), slice(None)])]


def halved(ref, side):
    return ref.at[pl.ds(2 * side, 2)]


class Part:
    def __init__(self, group, which, first, rows, at):
        self.group, self.which, self.first = group, which, first
        self.position, self.order = group.position, ORDERS[which]
        self.rows = (at, rows)

    def where(self, axis, step):
        return lax.rem(self.position[axis] + (step + 4), 4)

    def copy(self, receive, source, target, axis, step):
        remote(source, target, self.group.send_sems.at[self.which], receive, beside(self.position, axis, step)).start()

    def block(self, step):
        axis = self.order[0]
        return cut(self.group.packed, axis, self.where(axis, step), (self.first, self.rows[1]))

    def inbox(self, which, side=None):
        rows = [pl.ds(*self.rows), slice(None)]
        middle = [slice(None) if side is None else pl.ds(2 * side, 2), slice(None)]
        return self.group.inbox.at[tuple([which] + middle + rows)]

    def outbox(self, side):
        return self.group.outbox.at[pl.ds(2 * side, 2), :, pl.ds(*self.rows), :]

    def steps(self):
        group, axis, rows = self.group, self.order[0], pl.ds(*self.rows)
        far_sem, near_sem = group.far_sems.at[self.which], group.near_sems.at[self.which]
        group.add_swapped(self.which)
        far = self.block(2)
        self.copy(far_sem, halved(far, 0), self.inbox(2, 0), axis, 1)
        self.copy(far_sem, halved(far, 1), self.inbox(2, 1), axis, -1)
        self.copy(near_sem, halved(self.block(1), 1), self.inbox(0, 1), axis, 1)
        self.copy(near_sem, halved(self.block(-1), 0), self.inbox(1, 0), axis, -1)
        yield
        landed(self.inbox(2), far_sem)
        for side, step in ((0, 1), (1, -1)):
            box = self.outbox(side)
            box[...] = (widened(halved(self.block(step), side)) + widened(self.inbox(2, side))).astype(BF16)
            self.copy(near_sem, box, self.inbox(0 if step == 1 else 1, side), axis, step)
        yield
        landed(group.inbox.at[pl.ds(0, 2), :, :, rows, :], near_sem)
        total = widened(self.block(0)) + widened(self.inbox(0)) + widened(self.inbox(1))
        group.held[0][:, :, self.rows[0] : self.rows[0] + self.rows[1], :] = total.astype(BF16)
        landed(group.inbox.at[:, :, :, rows, :], group.send_sems.at[self.which])
        group.free(self.which)
        self.direct(1)
        yield
        group.held[1][:, self.rows[0] : self.rows[0] + self.rows[1], :] = self.summed(1).astype(BF16)
        self.direct(2)
        yield
        group.total(self.which, self.summed(2))
        yield

    def direct(self, phase):
        axis = self.order[phase]
        dim = sorted(self.order[phase:]).index(axis)
        held, slots = self.group.held[phase - 1], self.group.slots[phase - 1]
        for i, step in enumerate((2, 1, -1)):
            remote(cut(held, dim, self.where(axis, step), self.rows), cut(slots, 0, i, self.rows), self.group.send_sems.at[2 + phase],
                   self.group.direct_sems.at[phase - 1, self.which], beside(self.position, axis, step)).start()

    def summed(self, phase):
        axis = self.order[phase]
        dim = sorted(self.order[phase:]).index(axis)
        held, slots = self.group.held[phase - 1], self.group.slots[phase - 1]
        whole = slots.at[tuple([slice(None)] * (len(slots.shape) - 2) + [pl.ds(*self.rows), slice(None)])]
        landed(whole, self.group.direct_sems.at[phase - 1, self.which])
        total = widened(cut(held, dim, self.where(axis, 0), self.rows))
        for i in range(3):
            total = total + widened(cut(slots, 0, i, self.rows))
        return total


def landed(ref, semaphore):
    pltpu.make_async_copy(ref, ref, semaphore).wait()


def bank_buffers(units):
    rows = 16 * sum(units)
    return [pltpu.VMEM((3, 4, 4, rows, 128), BF16), pltpu.VMEM((4, 4, rows, 128), BF16)]


def group_buffers(units):
    rows = 16 * sum(units)
    return [pltpu.VMEM(shape + (rows, 128), BF16) for shape in ((4, 4), (4,), (3, 4), (3,))]


class Group:
    def __init__(self, which, position, packed, arrivals, totals, banks, own, sems, credits):
        self.section, self.first, self.half, self.parts, self.bank = GROUPS[which]
        self.again, self.reused = which >= 2, which < 2
        self.position, self.packed, self.totals = position, packed, totals
        self.me = lax.axis_index("section")
        self.swap_sems, self.far_sems, self.near_sems, self.direct_sems, self.send_sems, self.total_sems = sems
        self.swap_credit, self.part_credit = credits
        self.units = sum(self.parts)
        rows = 16 * self.units
        self.arrival = arrivals[self.bank]
        self.inbox, self.outbox = banks[self.bank]
        self.inbox = self.inbox.at[:, :, :, pl.ds(0, rows), :]
        self.held, self.slots = own[:2], own[2:]
        self.offsets = [sum(self.parts[:i]) for i in range(3)]
        self.start, self.other = [
            pl.multiple_of(16 * STARTS[which] + side * rows, 16) for side in (self.me, 1 - self.me)
        ]
        self.work = [Part(self, i, self.start + 16 * self.offsets[i], 16 * self.parts[i], 16 * self.offsets[i]) for i in range(3)]

    def swap(self, i):
        rows = 16 * self.parts[i]
        source = self.packed.at[:, :, :, pl.ds(self.other + 16 * self.offsets[i], rows), :]
        target = self.arrival.at[:, :, :, pl.ds(16 * self.offsets[i], rows), :]
        return remote(source, target, self.swap_sems.at[3], self.swap_sems.at[i], partner())

    def start_swap(self):
        self.begun = self.ended = 0
        if self.again:
            pl.semaphore_wait(self.swap_credit, 1)
        for i in range(3):
            self.swap(i).start()
        self.steps = [part.steps() for part in self.work]

    def add_swapped(self, i):
        part = self.work[i]
        self.swap(i).wait_recv()
        mine = self.packed.at[:, :, :, pl.ds(part.first, part.rows[1]), :]
        mine[...] = mine[...] + self.arrival[:, :, :, part.rows[0] : part.rows[0] + part.rows[1], :]
        self.begun += 1
        if self.reused and self.begun == 3:
            pl.semaphore_signal(self.swap_credit, inc=1, device_id=partner(), device_id_type=MESH)
        if self.again:
            pl.semaphore_wait(self.part_credit.at[i], 2)

    def free(self, i):
        if self.reused:
            for step in (1, -1):
                pl.semaphore_signal(self.part_credit.at[i], inc=1, device_id=beside(self.position, ORDERS[i][0], step), device_id_type=MESH)

    def total(self, i, total):
        base = 16 * (self.first + self.me * self.half)
        if self.offsets[i] < self.half:
            at = pl.multiple_of(base + 16 * self.offsets[i], 16)
            self.totals[self.section, pl.ds(at, 16 * self.parts[i]), :] = total
        else:
            self.totals[self.me, 16 * NORMS : 16 * NORMS + 16, :] = total
        self.ended += 1
        if self.ended < 3:
            return
        mine = self.totals.at[self.section, pl.ds(pl.multiple_of(base, 16), 16 * self.half), :]
        self.handed = remote(mine, mine, self.total_sems.at[0], self.total_sems.at[1], partner())

        @pl.when(self.me != self.section)
        def _():
            self.handed.start()

    def close(self):
        landed(self.packed.at[:, :, :, pl.ds(self.other, 16 * self.units), :], self.swap_sems.at[3])
        landed(self.slots[0], self.send_sems.at[3])
        landed(self.slots[1], self.send_sems.at[4])
        theirs = pl.multiple_of(16 * (self.first + (1 - self.me) * self.half), 16)

        @pl.when(self.me != self.section)
        def _():
            self.handed.wait_send()

        @pl.when(self.me == self.section)
        def _():
            landed(self.totals.at[self.section, pl.ds(theirs, 16 * self.half), :], self.total_sems.at[1])


def keep_attention():
    return [pltpu.VMEM((256, 1536), BF16), pltpu.VMEM((8, 256, 256), BF16), pltpu.VMEM((256, 512), BF16)]


def keep_norm():
    return [pltpu.VMEM((256, 512), F32), pltpu.VMEM((256, 1), F32)]


def keep_ffn():
    return [pltpu.VMEM((256, 512), BF16), pltpu.VMEM((256, 2048), BF16), pltpu.VMEM((256, 2048), BF16)]


def stacked(scratch):
    return [pltpu.VMEM((2,) + tuple(s.shape), s.dtype) for s in scratch]


def scratch_shapes():
    low, wide, square = pltpu.VMEM((256, 512), BF16), pltpu.VMEM((256, 512), F32), pltpu.VMEM((256, 256), F32)
    return dict(
        weights=stacked([pltpu.VMEM(shape, BF16) for shape in WEIGHTS]),
        inputs=stacked([low, low, pltpu.VMEM((6, 1, 512), F32)]),
        selfs=stacked(keep_attention() + keep_norm()),
        firsts=stacked([low, wide]),
        enc=keep_ffn()[1:] + keep_norm() + keep_norm() + [low, pltpu.VMEM((256, 1024), BF16)],
        cross=[low, pltpu.VMEM((8, 256, 256), BF16), low] + keep_norm(),
        dec=keep_ffn() + keep_norm(),
        bias=[pltpu.VMEM((2, 256, 256), F32), square],
        work=[wide, low, pltpu.VMEM((8, 512), F32)],
        results=[low, low],
        packed=pltpu.VMEM((4, 4, 4, 16 * PACKED_UNITS, 128), BF16),
        arrivals=[pltpu.VMEM((4, 4, 4, 16 * sum(units), 128), BF16) for units in BANKS],
        banks=[bank_buffers(units) for units in BANKS],
        groups=[group_buffers(group[3]) for group in GROUPS],
        places=[pltpu.VMEM((2, 1, ROW), jnp.int32), pltpu.SMEM((2, 1, NSEG), jnp.int32)],
        totals=pltpu.VMEM((2, 464, 128), F32),
        in_sems=pltpu.SemaphoreType.DMA((2, 8)),
        in_sends=pltpu.SemaphoreType.DMA((8,)),
        place_sems=pltpu.SemaphoreType.DMA((2,)),
        out_sems=pltpu.SemaphoreType.DMA((3, 2)),
        group_sems=[
            [pltpu.SemaphoreType.DMA(shape) for shape in ((4,), (3,), (3,), (2, 3), (5,), (2,))]
            for _ in GROUPS
        ],
        swap_credit=pltpu.SemaphoreType.REGULAR((2,)),
        part_credit=pltpu.SemaphoreType.REGULAR((2, 3)),
    )


def whole_kernel(tree, *refs):
    tokens, cotangent, lengths_in, segments_in = refs[:4]
    own = refs[4:9]
    norm_params = refs[9]
    layer_out, token_grads = refs[10:12]
    totals_out = refs[12]
    s = jax.tree.unflatten(tree, refs[13:])
    me = lax.axis_index("section")
    position = place()

    barrier = pltpu.get_barrier_semaphore()
    pl.semaphore_signal(barrier, inc=1, device_id=partner(), device_id_type=MESH)
    for axis in range(3):
        for step in (1, -1):
            pl.semaphore_signal(barrier, inc=1, device_id=beside(position, axis, step), device_id_type=MESH)
            pl.semaphore_signal(barrier, inc=1, device_id=across(position, axis, step), device_id_type=MESH)

    held = list(s["weights"]) + list(s["inputs"])

    def given(i, micro):
        if i < 5:
            return own[i].at[0]
        if i == 7:
            return norm_params
        return (tokens, cotangent)[i - 5].at[0, micro, 0]

    def local(i):
        return pltpu.make_async_copy(given(i, me), held[i].at[me], s["in_sems"].at[me, i])

    def sent(i):
        return remote(given(i, 1 - me), held[i].at[me], s["in_sends"].at[i], s["in_sems"].at[me, i], partner())

    def ready(j, i):
        pltpu.make_async_copy(given(i, 0), held[i].at[j], s["in_sems"].at[j, i]).wait()

    segments, lengths = s["places"]
    places = [pltpu.make_async_copy((segments_in, lengths_in)[i], s["places"][i], s["place_sems"].at[i]) for i in range(2)]
    for copy in places:
        copy.start()
    for i in (5, 0, 7, 1, 3, 4, 2, 6):
        local(i).start()
    for copy in places:
        copy.wait()

    bias, cross_bias = s["bias"]
    lane = lax.broadcasted_iota(jnp.int32, (1, ROW), 1)
    down = lax.broadcasted_iota(jnp.int32, (ROW, 1), 0)
    ids_row, ids_col = jnp.zeros((1, ROW), jnp.int32), jnp.zeros((ROW, 1), jnp.int32)
    bound = jnp.int32(0)
    for j in range(NSEG):
        bound = bound + lengths[me, 0, j]
        ids_row = ids_row + (lane >= bound).astype(jnp.int32)
        ids_col = ids_col + (down >= bound).astype(jnp.int32)
    target_row = segments[me].astype(F32)
    target_col = jnp.broadcast_to(target_row, (128, ROW)).T[:, 0:1]
    ids_row, ids_col = ids_row.astype(F32), ids_col.astype(F32)
    bias[0] = jnp.where(ids_col == ids_row, 0.0, -1e30)
    bias[1] = jnp.where(target_col == target_row, 0.0, -1e30)
    cross_bias[...] = jnp.where(target_col == ids_row, 0.0, -1e30)

    pl.semaphore_wait(barrier, 13)
    for i in (5, 7, 0, 1):
        sent(i).start()
    first = 0
    for k, rows in enumerate((352, 352, 336, 336, 336, 336)):
        piece = pl.ds(first, rows)
        remote(own[4].at[0, piece], held[4].at[me, piece], s["in_sends"].at[4], s["in_sems"].at[me, 4],
               across(position, k // 2, 1 - 2 * (k % 2))).start()
        first += rows

    @pl.when(me == 0)
    def _():
        for i in (3, 2):
            sent(i).start()

    @pl.when(me != 0)
    def _():
        for i in (2, 3):
            sent(i).start()

    sent(6).start()

    w_self_in, w_self_out, w_cross, w_in, w_out = s["weights"]
    x, cot, norms = s["inputs"]
    first_low, first = s["firsts"]
    work, grad_context, grad_norms = s["work"]
    memory_low, third_low = s["results"]
    source_grad, target_grad = first.at[0], first.at[1]

    def self_block(i, carry):
        j = lax.rem(me + i, 2)
        for which in (5, 0, 7, 1):
            ready(j, which)
        projected, shares, context, normed, scale = [ref.at[j] for ref in s["selfs"]]
        result = self_forward(x.at[j], w_self_in.at[j], w_self_out.at[j], bias.at[j], norms.at[j], projected, shares, context, normed, scale)
        first[j] = result
        first_low[j] = result.astype(BF16)
        return carry

    lax.fori_loop(0, 2, self_block, 0)

    enc_active, enc_slopes, enc_normed, enc_scale, memory_normed, memory_scale, memory_keep, key_value = s["enc"]
    queries, cross_shares, cross_context, cross_normed, cross_scale = s["cross"]
    dec_low, dec_active, dec_slopes, dec_normed, dec_scale = s["dec"]
    enc_self, dec_self = [ref.at[0] for ref in s["selfs"]], [ref.at[1] for ref in s["selfs"]]
    enc_norms, dec_norms = norms.at[0], norms.at[1]

    result = ffn_forward(first_low.at[0], w_in.at[0], w_out.at[0], enc_active, enc_slopes, lambda: ready(0, 3), lambda: ready(0, 4))
    second = norm(first[0] + result, enc_norms, 1, enc_normed, enc_scale)
    memory = norm(second, enc_norms, 2, memory_normed, memory_scale).astype(BF16)
    memory_low[...] = memory
    ready(0, 2)
    for i in range(2):
        key_value[:, 512 * i : 512 * i + 512] = dot(memory, w_cross[0, :, 512 * i : 512 * i + 512]).astype(BF16)

    ready(1, 2)
    queries[...] = dot(first_low[1], w_cross[1, :, :512]).astype(BF16)
    keys_values = (columns_of(key_value, 0), columns_of(key_value, 512))
    attend(columns_of(queries, 0), *keys_values, cross_bias, cross_shares, cross_context)
    second = norm(first[1] + dot(cross_context[...], w_cross[1, :, 512:]), dec_norms, 2, cross_normed, cross_scale)
    dec_low[...] = second.astype(BF16)
    result = ffn_forward(dec_low, w_in.at[1], w_out.at[1], dec_active, dec_slopes, lambda: ready(1, 3), lambda: ready(1, 4))
    third_low[...] = norm(second + result, dec_norms, 1, dec_normed, dec_scale).astype(BF16)

    def put_out(slot, out, values):
        for j in range(2):
            here = pltpu.make_async_copy(values[j], out.at[0, me, 0], s["out_sems"].at[0, slot])
            there = remote(values[j], out.at[0, me, 0], s["out_sems"].at[1, slot], s["out_sems"].at[2, slot], partner())

            @pl.when(me == j)
            def _():
                here.start()

            @pl.when(me != j)
            def _():
                there.start()

    def out_done(slot, out, values):
        pltpu.make_async_copy(values[0], out.at[0, me, 0], s["out_sems"].at[0, slot]).wait()
        there = remote(values[0], out.at[0, me, 0], s["out_sems"].at[1, slot], s["out_sems"].at[2, slot], partner())
        there.wait_send()
        there.wait_recv()

    put_out(0, layer_out, (memory_low, third_low))

    packed = s["packed"]
    groups = [
        Group(g, position, packed, s["arrivals"], s["totals"], s["banks"], s["groups"][g], s["group_sems"][g],
              (s["swap_credit"].at[GROUPS[g][4]], s["part_credit"].at[GROUPS[g][4]]))
        for g in range(4)
    ]
    def at(moment, which=None):
        for step in SCHEDULE.get(moment if which is None else moment + str(which), "").split():
            group = groups[int(step[0])]
            if step[1] == "s":
                group.start_swap()
            else:
                next(group.steps["abc".index(step[1])])

    def ffn_back(gradient, low, section, activated, slopes, moment):
        result = gradient.astype(BF16)
        for i in range(4):
            rows = slice(512 * i, 512 * i + 512)
            slopes[:, rows] = (dot_nt(result, w_out[section, rows, :]) * slopes[:, rows].astype(F32)).astype(BF16)
            pack_tall(packed, section, i, dot_tn(activated[:, rows], result))
            at(moment + "_out", i)
        for i in range(4):
            pack(packed, section, HIDDEN_IN + 2 * i, dot_tn(low[...], slopes[:, 512 * i : 512 * i + 512]))
            at(moment + "_in", i)
        return dot_nt(slopes[...], w_in[section])

    def self_back_a(gradient, section, kept):
        projected, shares, context, normed, scale = kept
        low = gradient.astype(BF16)
        pack(packed, section, SELF_OUT, dot_tn(context[...], low))
        grad_context[...] = dot_nt(low, w_self_out[section]).astype(BF16)

    def self_back_b(section, kept, moment):
        projected, shares, context, normed, scale = kept
        attend_back(*thirds(projected), shares, context, grad_context, *[putter(projected, 512 * i) for i in range(3)])
        at(moment + "_attend")

    def self_back_c(section, kept):
        projected = kept[0]
        for i in range(3):
            pack(packed, section, SELF_IN + 2 * i, dot_tn(x[section], projected[:, 512 * i : 512 * i + 512]))
        pack_norms(packed, section, grad_norms)

    grad_norms[...] = jnp.zeros_like(grad_norms)
    ready(1, 6)
    gradient = norm_back(cot[1].astype(F32), dec_norms, 1, dec_normed, dec_scale, grad_norms)
    gradient = gradient + ffn_back(gradient, dec_low, 1, dec_active, dec_slopes, "dec")
    gradient = norm_back(gradient, dec_norms, 2, cross_normed, cross_scale, grad_norms)
    work[...] = gradient
    low = gradient.astype(BF16)
    pack(packed, 1, CROSS + 2, dot_tn(cross_context[...], low))
    grad_context[...] = dot_nt(low, w_cross[1, :, 512:]).astype(BF16)
    at("cross_start")
    attend_back(columns_of(queries, 0), *keys_values, cross_shares, cross_context, grad_context,
                putter(queries, 0), putter(key_value, 0), putter(key_value, 512))
    at("cross_attend")
    pack(packed, 1, CROSS, dot_tn(first_low[1], queries[...]))
    gradient = work[...] + dot_nt(queries[...], w_cross[1, :, :512])
    gradient = norm_back(gradient, dec_norms, 0, *dec_self[3:], grad_norms)
    work[...] = gradient
    at("cross_end")
    self_back_a(gradient, 1, dec_self)
    at("dec_start")
    self_back_b(1, dec_self, "dec")
    self_back_c(1, dec_self)
    at("dec_end")
    target_grad[...] = work[...] + dot_nt(dec_self[0][...], w_self_in[1])

    for i in range(2):
        pack(packed, 0, CROSS + 2 * i, dot_tn(memory_low[...], key_value[:, 512 * i : 512 * i + 512]))
    at("memory_start")
    ready(0, 6)
    gradient = cot[0].astype(F32) + dot_nt(key_value[...], w_cross[0])
    gradient = norm_back(gradient, enc_norms, 2, memory_normed, memory_scale, grad_norms)
    gradient = norm_back(gradient, enc_norms, 1, enc_normed, enc_scale, grad_norms)
    at("memory_end")
    gradient = gradient + ffn_back(gradient, first_low.at[0], 0, enc_active, enc_slopes, "enc")
    gradient = norm_back(gradient, enc_norms, 0, *enc_self[3:], grad_norms)
    work[...] = gradient
    self_back_a(gradient, 0, enc_self)
    at("enc_start")
    self_back_b(0, enc_self, "enc")
    self_back_c(0, enc_self)
    at("enc_end")
    source_grad[...] = work[...] + dot_nt(enc_self[0][...], w_self_in[0])
    put_out(1, token_grads, (source_grad, target_grad))
    at("last")

    for group in groups:
        group.close()
    copy = pltpu.make_async_copy(s["totals"].at[me], totals_out, s["place_sems"].at[0])
    copy.start()
    for i in range(8):
        sent(i).wait_send()
    out_done(0, layer_out, (memory_low, third_low))
    out_done(1, token_grads, (source_grad, target_grad))
    copy.wait()


def finish_kernel(layer_in, grads_in, totals, layer_out, token_grads, *refs):
    grad_refs, grad_norms = refs[:5], refs[5]
    layer_out[...] = layer_in[...]
    token_grads[...] = grads_in[...]

    def tile(t):
        return totals[8 * t : 8 * t + 8, :]

    for which, unit, columns in ((0, SELF_IN, 1536), (1, SELF_OUT, 512), (2, CROSS, 1024), (3, HIDDEN_IN, 2048)):
        for i in range(columns // 128):
            grad_refs[which][0, :, 128 * i : 128 * i + 128] = tile(2 * unit + i)
    for r in range(4):
        for i in range(4):
            grad_refs[4][0, 8 * r : 8 * r + 8, 128 * i : 128 * i + 128] = tile(2 * HIDDEN_OUT + 4 * r + i)
    turned = jnp.concatenate([tile(2 * NORMS), jnp.zeros((120, 128), F32)], 0).T
    for i in range(6):
        grad_norms[i] = turned[i : i + 1, :8]


def body(tokens, cotangent, source_lengths, target_segments, self_in, self_out, cross_weight, hidden_in, hidden_out, norm_params):
    shapes, tree = jax.tree.flatten(scratch_shapes())
    vmem, hbm = [pl.BlockSpec(memory_space=space) for space in (pltpu.VMEM, pl.ANY)]
    large = [jax.ShapeDtypeStruct(tokens.shape, BF16), jax.ShapeDtypeStruct(tokens.shape, F32)]
    layer, grads, totals = pl.pallas_call(
        lambda *refs: whole_kernel(tree, *refs),
        out_shape=large + [jax.ShapeDtypeStruct((464, 128), F32)],
        in_specs=[hbm] * 10,
        out_specs=[hbm] * 3,
        scratch_shapes=shapes,
        compiler_params=pltpu.CompilerParams(collective_id=0, has_side_effects=True, vmem_limit_bytes=64 << 20),
        name="layer_pair",
    )(tokens, cotangent, source_lengths, target_segments, self_in, self_out, cross_weight, hidden_in, hidden_out,
      norm_params.transpose(1, 0, 2))
    small = [(1, 8, 1536), (1, 8, 512), (1, 8, 1024), (1, 8, 2048), (1, 32, 512), (6, 1, 8)]
    results = pl.pallas_call(
        finish_kernel,
        out_shape=large + [jax.ShapeDtypeStruct(shape, F32) for shape in small],
        in_specs=[vmem] * 3,
        out_specs=[vmem] * 8,
        name="finish",
    )(layer, grads, totals)
    return (*results[:7], results[7].transpose(1, 0, 2))


def solution(mesh):
    return jax.shard_map(
        body,
        mesh=mesh,
        in_specs=(
            P("section", None, "dp", None, None),
            P("section", None, "dp", None, None),
            P(None, "dp", None),
            P(None, "dp", None),
            P("section", None, None),
            P("section", None, None),
            P("section", None, None),
            P("section", None, None),
            P("section", None, None),
            P("section", None, None),
        ),
        out_specs=(
            P("section", None, "dp", None, None),
            P("section", None, "dp", None, None),
            P("section", "dp", None),
            P("section", "dp", None),
            P("section", "dp", None),
            P("section", "dp", None),
            P("section", "dp", None),
            P("section", None, "dp"),
        ),
        check_vma=False,
    )
```

```python
import jax
import jax.numpy as jnp
from jax import lax
from jax.experimental import pallas as pl
from jax.experimental.pallas import tpu as pltpu
from jax.sharding import PartitionSpec as P

HEADS = 8
D = 512
ROW = 256
NSEG = 8
root_half = 0.7071067811865476
inverse_root = 0.3989422804014327
F32 = jnp.float32
BF16 = jnp.bfloat16
MESH = pl.DeviceIdType.MESH
WEIGHTS = ((512, 1536), (512, 512), (512, 1024), (512, 2048), (2048, 512))

HIDDEN_OUT, HIDDEN_IN, CROSS, SELF_OUT, SELF_IN, NORMS = 0, 8, 16, 20, 22, 28
GROUPS = (
    (1, 0, 4, (2, 1, 1), 0),
    (1, 8, 4, (1, 2, 1), 1),
    (1, 16, 6, (2, 2, 2), 2),
    (0, 0, 4, (1, 1, 2), 0),
    (0, 8, 6, (2, 2, 2), 1),
    (0, 20, 4, (2, 2, 1), 2),
)
BANKS = ((2, 1, 2), (2, 2, 2), (2, 2, 2))
FIRST_USERS = 3
ORDERS = ((0, 1, 2), (1, 2, 0), (2, 0, 1))
STARTS = (0, 8, 16, 28, 36, 48)
SCHEDULE = dict(
    dec_in3="1s 0s",
    dec_start="1b 1a",
    dec_end="2s 0a 0c 1c",
    memory_start="0b",
    memory_end="1a 1b",
    enc_out="3s 2a",
    enc_in0="0c 2b",
    enc_in1="2c",
    enc_in3="0a 4s 0b",
    enc_start="1a 1b 0c",
    enc_attend="2b 2a 2c",
    enc_end="4b",
    last="5s 1c 4a 3c 0a 0b 2a 3a 1c 2b 5a 2c 3b 3c 5b 4c 5a 4a 5c 0b 4b 3a 0c 3b 4c 3c 5b 5c 5a 4b 2b 3b 1c 4a 4c 0c 5b 3a 2c 5c 3c 2a 1b 4b 0a 0b 2b 1a 3b 5a 4c 4a 5b 3a 5c 2c 3c 2a 4b 4a 3b 1b 5a 1a 4c 1c 5b 3a 0a 5c",
)
PACKED_UNITS = 58


def unit_of(section, unit):
    if section == 1:
        return 57 if unit == NORMS else unit
    return 52 if unit == NORMS else 28 + unit + (1 if unit >= 24 else 0)


def dot(a, b):
    return lax.dot_general(a, b, (((1,), (0,)), ((), ())), preferred_element_type=F32)


def dot_nt(a, b):
    return lax.dot_general(a, b, (((1,), (1,)), ((), ())), preferred_element_type=F32)


def dot_tn(a, b):
    return lax.dot_general(a, b, (((0,), (0,)), ((), ())), preferred_element_type=F32)

def sides(factor):
    lane = lax.broadcasted_iota(jnp.int32, (1, 128), 1)
    low = jnp.where(lane < 64, factor, 0.0).astype(BF16)
    high = jnp.where(lane < 64, 0.0, factor).astype(BF16)
    return (low, high)


def attend(query, key, value, bias, shares, context):
    scaled, plain = sides(0.125), sides(1.0)
    heads = [(pair, side) for pair in range(HEADS // 2) for side in range(2)]
    masked = bias[...].astype(F32)
    scores = [dot_nt(query(pair) * scaled[side], key(pair)) + masked for pair, side in heads]
    expvals = [jnp.exp(score - jnp.max(score, -1, keepdims=True)) for score in scores]
    low = [(expval * (1.0 / jnp.sum(expval, -1, keepdims=True))).astype(BF16) for expval in expvals]
    for head in range(HEADS):
        shares[head] = low[head]
    for pair in range(HEADS // 2):
        parts = [dot(low[2 * pair + side], value(pair) * plain[side]) for side in range(2)]
        context[:, 128 * pair : 128 * pair + 128] = (parts[0] + parts[1]).astype(BF16)


def attend_back(query, key, value, shares, context, grad_context, put_query, put_key, put_value):
    scaled, plain = sides(0.125), sides(1.0)
    heads = [(pair, side) for pair in range(HEADS // 2) for side in range(2)]
    given = [grad_context[:, 128 * pair : 128 * pair + 128] for pair in range(HEADS // 2)]
    along = [given[pair].astype(F32) * context[:, 128 * pair : 128 * pair + 128].astype(F32) for pair in range(HEADS // 2)]
    grad_shares = [dot_nt(given[pair] * plain[side], value(pair)) for pair, side in heads]
    deltas = [jnp.sum(along[pair] * plain[side].astype(F32), -1, keepdims=True) for pair, side in heads]
    low = [(shares[i].astype(F32) * (grad_shares[i] - deltas[i])).astype(BF16) for i in range(HEADS)]
    for pair in range(HEADS // 2):
        q, k, g = query(pair), key(pair), given[pair]
        one, two = low[2 * pair], low[2 * pair + 1]
        grad_query = dot(one, k * scaled[0]) + dot(two, k * scaled[1])
        grad_key = dot_tn(one, q * scaled[0]) + dot_tn(two, q * scaled[1])
        grad_value = dot_tn(shares[2 * pair], g * plain[0]) + dot_tn(shares[2 * pair + 1], g * plain[1])
        put_query(pair, grad_query.astype(BF16))
        put_key(pair, grad_key.astype(BF16))
        put_value(pair, grad_value.astype(BF16))


def mean(values):
    return jnp.sum(values, -1, keepdims=True) * (1.0 / D)


def norm(values, params, which, normed, scale):
    center = values - mean(values)
    inverse = lax.rsqrt(mean(center * center) + 1e-05)
    result = center * inverse
    normed[...] = result
    scale[...] = inverse
    return result * params[2 * which] + params[2 * which + 1]


def norm_back(gradient, params, which, normed, scale, grad_norms):
    n = normed[...]
    grad_norms[2 * which : 2 * which + 1, :] = jnp.sum(gradient * n, 0, keepdims=True)
    grad_norms[2 * which + 1 : 2 * which + 2, :] = jnp.sum(gradient, 0, keepdims=True)
    scaled = gradient * params[2 * which]
    return scale[...] * (scaled - mean(scaled) - n * mean(scaled * n))


def pack(packed, section, unit, value):
    blocks = value.reshape(4, 4, 4, 8, value.shape[1])
    for i in range(value.shape[1] // 256):
        two = jnp.concatenate([blocks[..., 256 * i : 256 * i + 128], blocks[..., 256 * i + 128 : 256 * i + 256]], 3)
        at = 16 * unit_of(section, unit + i)
        packed[:, :, :, at : at + 16, :] = two.astype(BF16)


def pack_tall(packed, section, first, value):
    blocks = value.reshape(4, 4, 4, 8, 512)
    for r in range(4):
        for i in range(2):
            two = jnp.concatenate([blocks[:, :, r, :, 256 * i : 256 * i + 128], blocks[:, :, r, :, 256 * i + 128 : 256 * i + 256]], 2)
            at = 16 * unit_of(section, HIDDEN_OUT + 2 * r + i)
            packed[first, :, :, at : at + 16, :] = two.astype(BF16)


def pack_norms(packed, section, grad_norms):
    turned = jnp.concatenate([grad_norms[...], jnp.zeros((120, 512), F32)], 0).T
    tiles = turned.reshape(4, 4, 4, 8, 128)
    at = 16 * unit_of(section, NORMS)
    packed[:, :, :, at : at + 16, :] = jnp.concatenate([tiles, jnp.zeros_like(tiles)], 3).astype(BF16)

def columns_of(ref, first):
    return lambda pair: ref[:, first + 128 * pair : first + 128 * pair + 128]


def putter(ref, first):
    def put(pair, value):
        ref[:, first + 128 * pair : first + 128 * pair + 128] = value

    return put


def thirds(ref):
    return columns_of(ref, 0), columns_of(ref, 512), columns_of(ref, 1024)


def self_forward(inputs, self_in, self_out, bias, params, projected, shares, context, normed, scale):
    for i in range(3):
        projected[:, 512 * i : 512 * i + 512] = dot(inputs[...], self_in[:, 512 * i : 512 * i + 512]).astype(BF16)
    attend(*thirds(projected), bias, shares, context)
    return norm(inputs[...].astype(F32) + dot(context[...], self_out[...]), params, 0, normed, scale)


def ffn_forward(low, hidden_in, hidden_out, activated, slopes, ready_in, ready_out):
    ready_in()
    for i in range(4):
        hidden = dot(low[...], hidden_in[:, 512 * i : 512 * i + 512])
        cdf = 0.5 * (1.0 + lax.erf(hidden * root_half))
        activated[:, 512 * i : 512 * i + 512] = (hidden * cdf).astype(BF16)
        slope = cdf + hidden * jnp.exp(-0.5 * hidden * hidden) * inverse_root
        slopes[:, 512 * i : 512 * i + 512] = slope.astype(BF16)
    ready_out()
    return dot(activated[...], hidden_out[...])


def place():
    dp = lax.axis_index("dp")
    return [lax.div(dp, 16), lax.rem(lax.div(dp, 4), 4), lax.rem(dp, 4)]


def beside(position, axis, step):
    moved = list(position)
    moved[axis] = lax.rem(moved[axis] + (step + 4), 4)
    return {"dp": (moved[0] * 4 + moved[1]) * 4 + moved[2]}


def across(position, axis, step):
    return dict(beside(position, axis, step), section=1 - lax.axis_index("section"))


def partner():
    return {"section": 1 - lax.axis_index("section")}


def remote(source, target, send, receive, device):
    return pltpu.make_async_remote_copy(
        src_ref=source, dst_ref=target, send_sem=send, recv_sem=receive, device_id=device, device_id_type=MESH
    )


def widened(ref):
    return ref[...].astype(F32)


def cut(ref, dim, where, rows):
    index = [slice(None)] * (len(ref.shape) - 2)
    index[dim] = where
    return ref.at[tuple(index + [pl.ds(*rows), slice(None)])]


def halved(ref, side):
    return ref.at[pl.ds(2 * side, 2)]


class Part:
    def __init__(self, group, which, first, rows, at, bank_at):
        self.group, self.which, self.first = group, which, first
        self.position, self.order = group.position, ORDERS[which]
        self.rows, self.bank_rows = (at, rows), (bank_at, rows)

    def where(self, axis, step):
        return lax.rem(self.position[axis] + (step + 4), 4)

    def copy(self, receive, source, target, axis, step):
        remote(source, target, self.group.first_sends.at[self.which], receive, beside(self.position, axis, step)).start()

    def block(self, step):
        axis = self.order[0]
        return cut(self.group.packed, axis, self.where(axis, step), (self.first, self.rows[1]))

    def inbox(self, which, side=None):
        rows = [pl.ds(*self.bank_rows), slice(None)]
        middle = [slice(None) if side is None else pl.ds(2 * side, 2), slice(None)]
        return self.group.inbox.at[tuple([which] + middle + rows)]

    def outbox(self, side):
        return self.group.outbox.at[pl.ds(2 * side, 2), :, pl.ds(*self.bank_rows), :]

    def steps(self):
        group, axis, rows = self.group, self.order[0], pl.ds(*self.bank_rows)
        far_sem, near_sem = group.far_sems.at[self.which], group.near_sems.at[self.which]
        group.add_swapped(self.which)
        far = self.block(2)
        self.copy(far_sem, halved(far, 0), self.inbox(2, 0), axis, 1)
        self.copy(far_sem, halved(far, 1), self.inbox(2, 1), axis, -1)
        self.copy(near_sem, halved(self.block(1), 1), self.inbox(0, 1), axis, 1)
        self.copy(near_sem, halved(self.block(-1), 0), self.inbox(1, 0), axis, -1)
        yield
        landed(self.inbox(2), far_sem)
        for side, step in ((0, 1), (1, -1)):
            box = self.outbox(side)
            box[...] = (widened(halved(self.block(step), side)) + widened(self.inbox(2, side))).astype(BF16)
            self.copy(near_sem, box, self.inbox(0 if step == 1 else 1, side), axis, step)
        yield
        landed(group.inbox.at[pl.ds(0, 2), :, :, rows, :], near_sem)
        total = widened(self.block(0)) + widened(self.inbox(0)) + widened(self.inbox(1))
        group.held[0][:, :, self.rows[0] : self.rows[0] + self.rows[1], :] = total.astype(BF16)
        landed(group.inbox.at[:, :, :, rows, :], group.first_sends.at[self.which])
        group.free(self.which)
        self.direct(1)
        yield
        group.held[1][:, self.rows[0] : self.rows[0] + self.rows[1], :] = self.summed(1).astype(BF16)
        if group.owner(self.which) is None:
            self.direct(2)
        else:
            pl.when(group.me == group.section)(lambda: self.direct(2))
            pl.when(group.me != group.section)(self.give)
        yield
        if group.owner(self.which) is None:
            group.totals[16 * NORMS : 16 * NORMS + 16, :] = self.summed(2)
        else:
            pl.when(group.me == group.section)(self.finish)
        yield

    def direct(self, phase):
        axis = self.order[phase]
        dim = sorted(self.order[phase:]).index(axis)
        held, slots = self.group.held[phase - 1], self.group.slots[phase - 1]
        for i, step in enumerate((2, 1, -1)):
            remote(cut(held, dim, self.where(axis, step), self.rows), cut(slots, 0, i, self.rows), self.group.late_sends.at[phase - 1],
                   self.group.direct_sems.at[phase - 1, self.which], beside(self.position, axis, step)).start()

    def give(self):
        axis = self.order[2]
        held, slots = self.group.held[1], self.group.slots[2]
        for i, step in enumerate((2, 1, -1, 0)):
            remote(cut(held, 0, self.where(axis, step), self.rows), cut(slots, 0, i, self.rows), self.group.late_sends.at[1],
                   self.group.direct_sems.at[2, self.which], across(self.position, axis, step)).start()

    def finish(self):
        group = self.group
        at = 16 * (group.first + self.group.me * group.half) + self.rows[0]
        group.totals[pl.ds(pl.multiple_of(at, 16), self.rows[1]), :] = self.summed(2)
        at = 16 * (group.first + (1 - self.group.me) * group.half) + self.rows[0]
        landed(group.slots[2].at[:, pl.ds(*self.rows), :], group.direct_sems.at[2, self.which])
        group.totals[pl.ds(pl.multiple_of(at, 16), self.rows[1]), :] = sum(
            [widened(cut(group.slots[2], 0, i, self.rows)) for i in range(1, 4)], widened(cut(group.slots[2], 0, 0, self.rows)))

    def summed(self, phase):
        axis = self.order[phase]
        dim = sorted(self.order[phase:]).index(axis)
        held, slots = self.group.held[phase - 1], self.group.slots[phase - 1]
        whole = slots.at[tuple([slice(None)] * (len(slots.shape) - 2) + [pl.ds(*self.rows), slice(None)])]
        landed(whole, self.group.direct_sems.at[phase - 1, self.which])
        total = widened(cut(held, dim, self.where(axis, 0), self.rows))
        for i in range(3):
            total = total + widened(cut(slots, 0, i, self.rows))
        return total


def landed(ref, semaphore):
    pltpu.make_async_copy(ref, ref, semaphore).wait()


def bank_buffers(units):
    rows = 16 * sum(units)
    return [pltpu.VMEM((3, 4, 4, rows, 128), BF16), pltpu.VMEM((4, 4, rows, 128), BF16)]


def group_buffers(units):
    rows = 16 * sum(units)
    return [pltpu.VMEM(shape + (rows, 128), BF16) for shape in ((4, 4), (4,), (3, 4), (3,), (4,))]


class Group:
    def __init__(self, which, position, packed, arrivals, totals, banks, own, sems, credits):
        self.section, self.first, self.half, self.parts, self.bank = GROUPS[which]
        self.again, self.reused = which >= FIRST_USERS, which < FIRST_USERS
        self.position, self.packed, self.totals = position, packed, totals
        self.me = lax.axis_index("section")
        self.swap_sems, self.far_sems, self.near_sems, self.first_sends, self.direct_sems, self.late_sends = sems
        self.swap_credit, self.part_credit = credits
        self.units = sum(self.parts)
        rows = 16 * self.units
        self.arrival = arrivals[self.bank]
        self.inbox, self.outbox = banks[self.bank]
        self.held, self.slots = own[:2], own[2:]
        self.offsets = [sum(self.parts[:i]) for i in range(3)]
        self.bank_offsets = [sum(BANKS[self.bank][:i]) for i in range(3)]
        self.start, self.other = [
            pl.multiple_of(16 * STARTS[which] + side * rows, 16) for side in (self.me, 1 - self.me)
        ]
        self.work = [
            Part(self, i, self.start + 16 * self.offsets[i], 16 * self.parts[i], 16 * self.offsets[i], 16 * self.bank_offsets[i])
            for i in range(3)
        ]

    def owner(self, i):
        return self.section if self.offsets[i] < self.half else None

    def swap(self, i):
        rows = 16 * self.parts[i]
        source = self.packed.at[:, :, :, pl.ds(self.other + 16 * self.offsets[i], rows), :]
        target = self.arrival.at[:, :, :, pl.ds(16 * self.bank_offsets[i], rows), :]
        return remote(source, target, self.swap_sems.at[3], self.swap_sems.at[i], partner())

    def start_swap(self):
        self.begun = 0
        if self.again:
            self.before.swapped()
            pl.semaphore_wait(self.swap_credit, 1)
        for i in range(3):
            self.swap(i).start()
        self.steps = [part.steps() for part in self.work]

    def add_swapped(self, i):
        part = self.work[i]
        self.swap(i).wait_recv()
        mine = self.packed.at[:, :, :, pl.ds(part.first, part.rows[1]), :]
        mine[...] = mine[...] + self.arrival[:, :, :, part.bank_rows[0] : part.bank_rows[0] + part.rows[1], :]
        self.begun += 1
        if self.reused and self.begun == 3:
            pl.semaphore_signal(self.swap_credit, inc=1, device_id=partner(), device_id_type=MESH)
        if self.again:
            pl.semaphore_wait(self.part_credit.at[i], 2)

    def free(self, i):
        if self.reused:
            for step in (1, -1):
                pl.semaphore_signal(self.part_credit.at[i], inc=1, device_id=beside(self.position, ORDERS[i][0], step), device_id_type=MESH)

    def swapped(self):
        landed(self.packed.at[:, :, :, pl.ds(self.other, 16 * self.units), :], self.swap_sems.at[3])

    def close(self):
        if self.again:
            self.swapped()
        landed(self.slots[0], self.late_sends.at[0])
        given = 16 * self.half
        rest = 16 * self.units - given

        @pl.when(self.me == self.section)
        def _():
            landed(self.slots[1], self.late_sends.at[1])

        @pl.when(self.me != self.section)
        def _():
            if rest:
                landed(self.packed.at[0, 0, 0, pl.ds(0, 4 * given + 3 * rest), :], self.late_sends.at[1])
            else:
                landed(self.slots[2], self.late_sends.at[1])


def keep_attention():
    return [pltpu.VMEM((256, 1536), BF16), pltpu.VMEM((8, 256, 256), BF16), pltpu.VMEM((256, 512), BF16)]


def keep_norm():
    return [pltpu.VMEM((256, 512), F32)]


def keep_ffn():
    return [pltpu.VMEM((256, 512), BF16), pltpu.VMEM((256, 2048), BF16), pltpu.VMEM((256, 2048), BF16)]


def stacked(scratch):
    return [pltpu.VMEM((2,) + tuple(s.shape), s.dtype) for s in scratch]


def scratch_shapes():
    low, wide, square = pltpu.VMEM((256, 512), BF16), pltpu.VMEM((256, 512), F32), pltpu.VMEM((256, 256), BF16)
    return dict(
        weights=stacked([pltpu.VMEM(shape, BF16) for shape in WEIGHTS]),
        inputs=stacked([low, low, pltpu.VMEM((6, 1, 512), F32)]),
        selfs=stacked(keep_attention() + keep_norm() + [pltpu.VMEM((256, 1), F32)]),
        scales=pltpu.VMEM((256, 128), F32),
        firsts=stacked([low, wide]),
        enc=keep_ffn()[1:] + keep_norm() + keep_norm() + [pltpu.VMEM((256, 1024), BF16)],
        cross=[low, pltpu.VMEM((8, 256, 256), BF16), low] + keep_norm(),
        dec=keep_ffn() + keep_norm(),
        bias=[pltpu.VMEM((2, 256, 256), BF16), square],
        work=[wide, low, pltpu.VMEM((8, 512), F32)],
        results=[low, low],
        packed=pltpu.VMEM((4, 4, 4, 16 * PACKED_UNITS, 128), BF16),
        arrivals=[pltpu.VMEM((4, 4, 4, 16 * sum(units), 128), BF16) for units in BANKS],
        banks=[bank_buffers(units) for units in BANKS],
        groups=[group_buffers(group[3]) for group in GROUPS],
        places=[pltpu.VMEM((2, 1, ROW), jnp.int32), pltpu.SMEM((2, 1, NSEG), jnp.int32)],
        totals=pltpu.VMEM((464, 128), F32),
        in_sems=pltpu.SemaphoreType.DMA((2, 8)),
        in_sends=pltpu.SemaphoreType.DMA((8,)),
        place_sems=pltpu.SemaphoreType.DMA((2,)),
        out_sems=pltpu.SemaphoreType.DMA((3, 2)),
        group_sems=[
            [pltpu.SemaphoreType.DMA(shape) for shape in ((3, 3), (2,))]
            for _ in GROUPS
        ],
        bank_sems=[[pltpu.SemaphoreType.DMA(shape) for shape in ((4,), (3,), (3,), (3,))] for _ in BANKS],
        swap_credit=pltpu.SemaphoreType.REGULAR((3,)),
        part_credit=pltpu.SemaphoreType.REGULAR((3, 3)),
    )


def whole_kernel(tree, *refs):
    tokens, cotangent, lengths_in, segments_in = refs[:4]
    own = refs[4:9]
    norm_params = refs[9]
    layer_out, token_grads = refs[10:12]
    totals_out = refs[12]
    s = jax.tree.unflatten(tree, refs[13:])
    me = lax.axis_index("section")
    position = place()

    barrier = pltpu.get_barrier_semaphore()
    pl.semaphore_signal(barrier, inc=1, device_id=partner(), device_id_type=MESH)
    for axis in range(3):
        for step in (1, -1):
            pl.semaphore_signal(barrier, inc=1, device_id=beside(position, axis, step), device_id_type=MESH)
            pl.semaphore_signal(barrier, inc=1, device_id=across(position, axis, step), device_id_type=MESH)

    held = list(s["weights"]) + list(s["inputs"])

    def given(i, micro):
        if i < 5:
            return own[i].at[0]
        if i == 7:
            return norm_params
        return (tokens, cotangent)[i - 5].at[0, micro, 0]

    def local(i):
        return pltpu.make_async_copy(given(i, me), held[i].at[me], s["in_sems"].at[me, i])

    def sent(i):
        return remote(given(i, 1 - me), held[i].at[me], s["in_sends"].at[i], s["in_sems"].at[me, i], partner())

    def ready(j, i):
        pltpu.make_async_copy(given(i, 0), held[i].at[j], s["in_sems"].at[j, i]).wait()

    segments, lengths = s["places"]
    places = [pltpu.make_async_copy((segments_in, lengths_in)[i], s["places"][i], s["place_sems"].at[i]) for i in range(2)]
    for copy in places:
        copy.start()
    for i in (5, 0, 7, 1, 3, 4, 2, 6):
        local(i).start()

    pl.semaphore_wait(barrier, 13)
    for i in (5, 7, 0, 1):
        sent(i).start()
    def pieces(i):
        first = 0
        for k, rows in enumerate((352, 352, 336, 336, 336, 336)):
            piece = pl.ds(first, rows)
            remote(own[i].at[0, piece], held[i].at[me, piece], s["in_sends"].at[i], s["in_sems"].at[me, i],
                   across(position, k // 2, 1 - 2 * (k % 2))).start()
            first += rows

    @pl.when(me == 0)
    def _():
        pieces(4)
        for i in (3, 2):
            sent(i).start()

    @pl.when(me != 0)
    def _():
        for i in (2, 3):
            sent(i).start()

    sent(6).start()

    for copy in places:
        copy.wait()

    bias, cross_bias = s["bias"]
    lane = lax.broadcasted_iota(jnp.int32, (1, ROW), 1)
    down = lax.broadcasted_iota(jnp.int32, (ROW, 1), 0)
    ids_row, ids_col = jnp.zeros((1, ROW), jnp.int32), jnp.zeros((ROW, 1), jnp.int32)
    bound = jnp.int32(0)
    for j in range(NSEG):
        bound = bound + lengths[me, 0, j]
        ids_row = ids_row + (lane >= bound).astype(jnp.int32)
        ids_col = ids_col + (down >= bound).astype(jnp.int32)
    target_row = segments[me].astype(F32)
    target_col = jnp.broadcast_to(target_row, (128, ROW)).T[:, 0:1]
    ids_row, ids_col = ids_row.astype(F32), ids_col.astype(F32)
    bias[0] = jnp.where(ids_col == ids_row, 0.0, -1e30).astype(BF16)
    bias[1] = jnp.where(target_col == target_row, 0.0, -1e30).astype(BF16)
    cross_bias[...] = jnp.where(target_col == ids_row, 0.0, -1e30).astype(BF16)

    w_self_in, w_self_out, w_cross, w_in, w_out = s["weights"]
    x, cot, norms = s["inputs"]
    first_low, first = s["firsts"]
    work, grad_context, grad_norms = s["work"]
    memory_low, third_low = s["results"]
    source_grad, target_grad = first.at[0], first.at[1]

    def self_block(i, carry):
        j = lax.rem(me + i, 2)
        for which in (5, 0, 7, 1):
            ready(j, which)
        @pl.when((me != 0) & (i == 1))
        def _():
            pieces(4)

        projected, shares, context, normed, scale = [ref.at[j] for ref in s["selfs"]]
        result = self_forward(x.at[j], w_self_in.at[j], w_self_out.at[j], bias.at[j], norms.at[j], projected, shares, context, normed, scale)
        first[j] = result
        first_low[j] = result.astype(BF16)
        return carry

    lax.fori_loop(0, 2, self_block, 0)

    enc_active, enc_slopes, enc_normed, memory_normed, key_value = s["enc"]
    queries, cross_shares, cross_context, cross_normed = s["cross"]
    dec_low, dec_active, dec_slopes, dec_normed = s["dec"]
    enc_scale, memory_scale, cross_scale, dec_scale = [s["scales"].at[:, i : i + 1] for i in range(4)]
    enc_self, dec_self = [ref.at[0] for ref in s["selfs"]], [ref.at[1] for ref in s["selfs"]]
    enc_norms, dec_norms = norms.at[0], norms.at[1]

    result = ffn_forward(first_low.at[0], w_in.at[0], w_out.at[0], enc_active, enc_slopes, lambda: ready(0, 3), lambda: ready(0, 4))
    second = norm(first[0] + result, enc_norms, 1, enc_normed, enc_scale)
    memory = norm(second, enc_norms, 2, memory_normed, memory_scale).astype(BF16)
    memory_low[...] = memory
    ready(0, 2)
    for i in range(2):
        key_value[:, 512 * i : 512 * i + 512] = dot(memory, w_cross[0, :, 512 * i : 512 * i + 512]).astype(BF16)

    ready(1, 2)
    queries[...] = dot(first_low[1], w_cross[1, :, :512]).astype(BF16)
    keys_values = (columns_of(key_value, 0), columns_of(key_value, 512))
    attend(columns_of(queries, 0), *keys_values, cross_bias, cross_shares, cross_context)
    second = norm(first[1] + dot(cross_context[...], w_cross[1, :, 512:]), dec_norms, 2, cross_normed, cross_scale)
    dec_low[...] = second.astype(BF16)
    result = ffn_forward(dec_low, w_in.at[1], w_out.at[1], dec_active, dec_slopes, lambda: ready(1, 3), lambda: ready(1, 4))
    third_low[...] = norm(second + result, dec_norms, 1, dec_normed, dec_scale).astype(BF16)

    def put_out(slot, out, values):
        for j in range(2):
            here = pltpu.make_async_copy(values[j], out.at[0, me, 0], s["out_sems"].at[0, slot])
            there = remote(values[j], out.at[0, me, 0], s["out_sems"].at[1, slot], s["out_sems"].at[2, slot], partner())

            @pl.when(me == j)
            def _():
                here.start()

            @pl.when(me != j)
            def _():
                there.start()

    def out_done(slot, out, values):
        pltpu.make_async_copy(values[0], out.at[0, me, 0], s["out_sems"].at[0, slot]).wait()
        there = remote(values[0], out.at[0, me, 0], s["out_sems"].at[1, slot], s["out_sems"].at[2, slot], partner())
        there.wait_send()
        there.wait_recv()

    put_out(0, layer_out, (memory_low, third_low))

    packed = s["packed"]
    groups = [
        Group(g, position, packed, s["arrivals"], s["totals"], s["banks"], s["groups"][g], s["bank_sems"][GROUPS[g][4]] + s["group_sems"][g],
              (s["swap_credit"].at[GROUPS[g][4]], s["part_credit"].at[GROUPS[g][4]]))
        for g in range(len(GROUPS))
    ]
    for group in groups[FIRST_USERS:]:
        group.before = next(other for other in groups if other.bank == group.bank)

    def at(moment, which=None):
        for step in SCHEDULE.get(moment if which is None else moment + str(which), "").split():
            group = groups[int(step[0])]
            if step[1] == "s":
                group.start_swap()
            else:
                next(group.steps["abc".index(step[1])])

    def ffn_back(gradient, low, section, activated, slopes, moment):
        result = gradient.astype(BF16)
        for i in range(4):
            pack_tall(packed, section, i, dot_tn(activated[:, 512 * i : 512 * i + 512], result))
        at(moment + "_out")
        for i in range(4):
            rows = slice(512 * i, 512 * i + 512)
            slopes[:, rows] = (dot_nt(result, w_out[section, rows, :]) * slopes[:, rows].astype(F32)).astype(BF16)
            pack(packed, section, HIDDEN_IN + 2 * i, dot_tn(low[...], slopes[:, rows]))
            at(moment + "_in", i)
        return dot_nt(slopes[...], w_in[section])

    def self_back_a(gradient, section, kept):
        projected, shares, context, normed, scale = kept
        low = gradient.astype(BF16)
        pack(packed, section, SELF_OUT, dot_tn(context[...], low))
        grad_context[...] = dot_nt(low, w_self_out[section]).astype(BF16)

    def self_back_b(section, kept, moment):
        projected, shares, context, normed, scale = kept
        attend_back(*thirds(projected), shares, context, grad_context, *[putter(projected, 512 * i) for i in range(3)])
        at(moment + "_attend")

    def self_back_c(section, kept):
        projected = kept[0]
        for i in range(3):
            pack(packed, section, SELF_IN + 2 * i, dot_tn(x[section], projected[:, 512 * i : 512 * i + 512]))
        pack_norms(packed, section, grad_norms)

    grad_norms[...] = jnp.zeros_like(grad_norms)
    ready(1, 6)
    gradient = norm_back(cot[1].astype(F32), dec_norms, 1, dec_normed, dec_scale, grad_norms)
    gradient = gradient + ffn_back(gradient, dec_low, 1, dec_active, dec_slopes, "dec")
    gradient = norm_back(gradient, dec_norms, 2, cross_normed, cross_scale, grad_norms)
    work[...] = gradient
    low = gradient.astype(BF16)
    pack(packed, 1, CROSS + 2, dot_tn(cross_context[...], low))
    grad_context[...] = dot_nt(low, w_cross[1, :, 512:]).astype(BF16)
    at("cross_start")
    attend_back(columns_of(queries, 0), *keys_values, cross_shares, cross_context, grad_context,
                putter(queries, 0), putter(key_value, 0), putter(key_value, 512))
    at("cross_attend")
    pack(packed, 1, CROSS, dot_tn(first_low[1], queries[...]))
    gradient = work[...] + dot_nt(queries[...], w_cross[1, :, :512])
    gradient = norm_back(gradient, dec_norms, 0, *dec_self[3:], grad_norms)
    work[...] = gradient
    at("cross_end")
    self_back_a(gradient, 1, dec_self)
    at("dec_start")
    self_back_b(1, dec_self, "dec")
    self_back_c(1, dec_self)
    at("dec_end")
    target_grad[...] = work[...] + dot_nt(dec_self[0][...], w_self_in[1])

    for i in range(2):
        pack(packed, 0, CROSS + 2 * i, dot_tn(memory_low[...], key_value[:, 512 * i : 512 * i + 512]))
    at("memory_start")
    ready(0, 6)
    gradient = cot[0].astype(F32) + dot_nt(key_value[...], w_cross[0])
    gradient = norm_back(gradient, enc_norms, 2, memory_normed, memory_scale, grad_norms)
    gradient = norm_back(gradient, enc_norms, 1, enc_normed, enc_scale, grad_norms)
    at("memory_end")
    gradient = gradient + ffn_back(gradient, first_low.at[0], 0, enc_active, enc_slopes, "enc")
    gradient = norm_back(gradient, enc_norms, 0, *enc_self[3:], grad_norms)
    work[...] = gradient
    self_back_a(gradient, 0, enc_self)
    at("enc_start")
    self_back_b(0, enc_self, "enc")
    self_back_c(0, enc_self)
    at("enc_end")
    source_grad[...] = work[...] + dot_nt(enc_self[0][...], w_self_in[0])
    put_out(1, token_grads, (source_grad, target_grad))
    at("last")

    for group in groups:
        group.close()
    copy = pltpu.make_async_copy(s["totals"], totals_out, s["place_sems"].at[0])
    copy.start()
    for i in range(8):
        sent(i).wait_send()
    out_done(0, layer_out, (memory_low, third_low))
    out_done(1, token_grads, (source_grad, target_grad))
    copy.wait()


def finish_kernel(layer_in, grads_in, totals, layer_out, token_grads, *refs):
    grad_refs, grad_norms = refs[:5], refs[5]
    layer_out[...] = layer_in[...]
    token_grads[...] = grads_in[...]

    def tile(t):
        return totals[8 * t : 8 * t + 8, :]

    for which, unit, columns in ((0, SELF_IN, 1536), (1, SELF_OUT, 512), (2, CROSS, 1024), (3, HIDDEN_IN, 2048)):
        for i in range(columns // 128):
            grad_refs[which][0, :, 128 * i : 128 * i + 128] = tile(2 * unit + i)
    for r in range(4):
        for i in range(4):
            grad_refs[4][0, 8 * r : 8 * r + 8, 128 * i : 128 * i + 128] = tile(2 * HIDDEN_OUT + 4 * r + i)
    turned = jnp.concatenate([tile(2 * NORMS), jnp.zeros((120, 128), F32)], 0).T
    for i in range(6):
        grad_norms[i] = turned[i : i + 1, :8]


def body(tokens, cotangent, source_lengths, target_segments, self_in, self_out, cross_weight, hidden_in, hidden_out, norm_params):
    shapes, tree = jax.tree.flatten(scratch_shapes())
    vmem, hbm = [pl.BlockSpec(memory_space=space) for space in (pltpu.VMEM, pl.ANY)]
    large = [jax.ShapeDtypeStruct(tokens.shape, BF16), jax.ShapeDtypeStruct(tokens.shape, F32)]
    layer, grads, totals = pl.pallas_call(
        lambda *refs: whole_kernel(tree, *refs),
        out_shape=large + [jax.ShapeDtypeStruct((464, 128), F32)],
        in_specs=[hbm] * 10,
        out_specs=[hbm] * 3,
        scratch_shapes=shapes,
        compiler_params=pltpu.CompilerParams(collective_id=0, has_side_effects=True, vmem_limit_bytes=64 << 20),
        name="layer_pair",
    )(tokens, cotangent, source_lengths, target_segments, self_in, self_out, cross_weight, hidden_in, hidden_out,
      norm_params.transpose(1, 0, 2))
    small = [(1, 8, 1536), (1, 8, 512), (1, 8, 1024), (1, 8, 2048), (1, 32, 512), (6, 1, 8)]
    results = pl.pallas_call(
        finish_kernel,
        out_shape=large + [jax.ShapeDtypeStruct(shape, F32) for shape in small],
        in_specs=[vmem] * 3,
        out_specs=[vmem] * 8,
        name="finish",
    )(layer, grads, totals)
    return (*results[:7], results[7].transpose(1, 0, 2))


def solution(mesh):
    return jax.shard_map(
        body,
        mesh=mesh,
        in_specs=(
            P("section", None, "dp", None, None),
            P("section", None, "dp", None, None),
            P(None, "dp", None),
            P(None, "dp", None),
            P("section", None, None),
            P("section", None, None),
            P("section", None, None),
            P("section", None, None),
            P("section", None, None),
            P("section", None, None),
        ),
        out_specs=(
            P("section", None, "dp", None, None),
            P("section", None, "dp", None, None),
            P("section", "dp", None),
            P("section", "dp", None),
            P("section", "dp", None),
            P("section", "dp", None),
            P("section", "dp", None),
            P("section", None, "dp"),
        ),
        check_vma=False,
    )
```

```python
import jax
import jax.numpy as jnp
from jax import lax
from jax.experimental import pallas as pl
from jax.experimental.pallas import tpu as pltpu
from jax.sharding import PartitionSpec as P

HEADS = 8
D = 512
ROW = 256
NSEG = 8
root_half = 0.7071067811865476
inverse_root = 0.3989422804014327
F32 = jnp.float32
BF16 = jnp.bfloat16
MESH = pl.DeviceIdType.MESH
WEIGHTS = ((512, 1536), (512, 512), (512, 1024), (512, 2048), (2048, 512))

HIDDEN_OUT, HIDDEN_IN, CROSS, SELF_OUT, SELF_IN, NORMS = 0, 8, 16, 20, 22, 28
GROUPS = (
    (1, 0, 4, (2, 1, 1), 0),
    (1, 8, 4, (1, 2, 1), 1),
    (1, 16, 6, (2, 2, 2), 2),
    (0, 0, 4, (1, 1, 2), 0),
    (0, 8, 6, (2, 2, 2), 1),
    (0, 20, 4, (2, 2, 1), 2),
)
BANKS = ((2, 1, 2), (2, 2, 2), (2, 2, 2))
FIRST_USERS = 3
ORDERS = ((0, 1, 2), (1, 2, 0), (2, 0, 1))
STARTS = (0, 8, 16, 28, 36, 48)
SCHEDULE = dict(
    dec_in3="1s 0s",
    dec_start="1b 1a",
    dec_end="2s 0a 0c 1c",
    memory_start="0b",
    memory_end="1a 1b",
    enc_out="3s 2a",
    enc_in0="0c 2b",
    enc_in1="2c",
    enc_in3="0a 4s 0b",
    enc_start="1a 1b 0c",
    enc_attend="2b 2a 2c",
    enc_end="4b",
    last="5s 1c 4a 3c 0a 0b 2a 3a 1c 2b 5a 2c 3b 3c 5b 4c 5a 4a 5c 0b 4b 3a 0c 3b 4c 3c 5b 5c 5a 4b 2b 3b 1c 4a 4c 0c 5b 3a 2c 5c 3c 2a 1b 4b 0a 0b 2b 1a 3b 5a 4c 4a 5b 3a 5c 2c 3c 2a 4b 4a 3b 1b 5a 1a 4c 1c 5b 3a 0a 5c",
)
PACKED_UNITS = 58


def unit_of(section, unit):
    if section == 1:
        return 57 if unit == NORMS else unit
    return 52 if unit == NORMS else 28 + unit + (1 if unit >= 24 else 0)


def dot(a, b):
    return lax.dot_general(a, b, (((1,), (0,)), ((), ())), preferred_element_type=F32)


def dot_nt(a, b):
    return lax.dot_general(a, b, (((1,), (1,)), ((), ())), preferred_element_type=F32)


def dot_tn(a, b):
    return lax.dot_general(a, b, (((0,), (0,)), ((), ())), preferred_element_type=F32)

def sides(factor):
    lane = lax.broadcasted_iota(jnp.int32, (1, 128), 1)
    low = jnp.where(lane < 64, factor, 0.0).astype(BF16)
    high = jnp.where(lane < 64, 0.0, factor).astype(BF16)
    return (low, high)


def attend(query, key, value, bias, shares, context):
    scaled, plain = sides(0.125), sides(1.0)
    heads = [(pair, side) for pair in range(HEADS // 2) for side in range(2)]
    masked = bias[...].astype(F32)
    scores = [dot_nt(query(pair) * scaled[side], key(pair)) + masked for pair, side in heads]
    expvals = [jnp.exp(score - jnp.max(score, -1, keepdims=True)) for score in scores]
    low = [(expval * (1.0 / jnp.sum(expval, -1, keepdims=True))).astype(BF16) for expval in expvals]
    for head in range(HEADS):
        shares[head] = low[head]
    for pair in range(HEADS // 2):
        parts = [dot(low[2 * pair + side], value(pair) * plain[side]) for side in range(2)]
        context[:, 128 * pair : 128 * pair + 128] = (parts[0] + parts[1]).astype(BF16)


def attend_back(query, key, value, shares, context, grad_context, put_query, put_key, put_value):
    scaled, plain = sides(0.125), sides(1.0)
    heads = [(pair, side) for pair in range(HEADS // 2) for side in range(2)]
    given = [grad_context[:, 128 * pair : 128 * pair + 128] for pair in range(HEADS // 2)]
    along = [given[pair].astype(F32) * context[:, 128 * pair : 128 * pair + 128].astype(F32) for pair in range(HEADS // 2)]
    grad_shares = [dot_nt(given[pair] * plain[side], value(pair)) for pair, side in heads]
    deltas = [jnp.sum(along[pair] * plain[side].astype(F32), -1, keepdims=True) for pair, side in heads]
    low = [(shares[i].astype(F32) * (grad_shares[i] - deltas[i])).astype(BF16) for i in range(HEADS)]
    for pair in range(HEADS // 2):
        q, k, g = query(pair), key(pair), given[pair]
        one, two = low[2 * pair], low[2 * pair + 1]
        grad_query = dot(one, k * scaled[0]) + dot(two, k * scaled[1])
        grad_key = dot_tn(one, q * scaled[0]) + dot_tn(two, q * scaled[1])
        grad_value = dot_tn(shares[2 * pair], g * plain[0]) + dot_tn(shares[2 * pair + 1], g * plain[1])
        put_query(pair, grad_query.astype(BF16))
        put_key(pair, grad_key.astype(BF16))
        put_value(pair, grad_value.astype(BF16))


def mean(values):
    return jnp.sum(values, -1, keepdims=True) * (1.0 / D)


def norm(values, params, which, normed, scale):
    center = values - mean(values)
    inverse = lax.rsqrt(mean(center * center) + 1e-05)
    result = center * inverse
    normed[...] = result
    scale[...] = inverse
    return result * params[2 * which] + params[2 * which + 1]


def norm_back(gradient, params, which, normed, scale, grad_norms):
    n = normed[...]
    grad_norms[2 * which : 2 * which + 1, :] = jnp.sum(gradient * n, 0, keepdims=True)
    grad_norms[2 * which + 1 : 2 * which + 2, :] = jnp.sum(gradient, 0, keepdims=True)
    scaled = gradient * params[2 * which]
    return scale[...] * (scaled - mean(scaled) - n * mean(scaled * n))


def pack(packed, section, unit, value):
    blocks = value.reshape(4, 4, 4, 8, value.shape[1])
    for i in range(value.shape[1] // 256):
        two = jnp.concatenate([blocks[..., 256 * i : 256 * i + 128], blocks[..., 256 * i + 128 : 256 * i + 256]], 3)
        at = 16 * unit_of(section, unit + i)
        packed[:, :, :, at : at + 16, :] = two.astype(BF16)


def pack_tall(packed, section, first, value):
    blocks = value.reshape(4, 4, 4, 8, 512)
    for r in range(4):
        for i in range(2):
            two = jnp.concatenate([blocks[:, :, r, :, 256 * i : 256 * i + 128], blocks[:, :, r, :, 256 * i + 128 : 256 * i + 256]], 2)
            at = 16 * unit_of(section, HIDDEN_OUT + 2 * r + i)
            packed[first, :, :, at : at + 16, :] = two.astype(BF16)


def pack_norms(packed, section, grad_norms):
    turned = jnp.concatenate([grad_norms[...], jnp.zeros((120, 512), F32)], 0).T
    tiles = turned.reshape(4, 4, 4, 8, 128)
    at = 16 * unit_of(section, NORMS)
    packed[:, :, :, at : at + 16, :] = jnp.concatenate([tiles, jnp.zeros_like(tiles)], 3).astype(BF16)

def columns_of(ref, first):
    return lambda pair: ref[:, first + 128 * pair : first + 128 * pair + 128]


def putter(ref, first):
    def put(pair, value):
        ref[:, first + 128 * pair : first + 128 * pair + 128] = value

    return put


def thirds(ref):
    return columns_of(ref, 0), columns_of(ref, 512), columns_of(ref, 1024)


def project(inputs, self_in, projected):
    for i in range(3):
        projected[:, 512 * i : 512 * i + 512] = dot(inputs[...], self_in[:, 512 * i : 512 * i + 512]).astype(BF16)


def self_forward(inputs, self_out, bias, params, projected, shares, context, normed, scale):
    attend(*thirds(projected), bias, shares, context)
    return norm(inputs[...].astype(F32) + dot(context[...], self_out[...]), params, 0, normed, scale)


def ffn_forward(low, hidden_in, hidden_out, activated, slopes, ready_in, ready_out):
    ready_in()
    for i in range(4):
        hidden = dot(low[...], hidden_in[:, 512 * i : 512 * i + 512])
        cdf = 0.5 * (1.0 + lax.erf(hidden * root_half))
        activated[:, 512 * i : 512 * i + 512] = (hidden * cdf).astype(BF16)
        slope = cdf + hidden * jnp.exp(-0.5 * hidden * hidden) * inverse_root
        slopes[:, 512 * i : 512 * i + 512] = slope.astype(BF16)
    ready_out()
    return dot(activated[...], hidden_out[...])


def place():
    dp = lax.axis_index("dp")
    return [lax.div(dp, 16), lax.rem(lax.div(dp, 4), 4), lax.rem(dp, 4)]


def beside(position, axis, step):
    moved = list(position)
    moved[axis] = lax.rem(moved[axis] + (step + 4), 4)
    return {"dp": (moved[0] * 4 + moved[1]) * 4 + moved[2]}


def across(position, axis, step):
    return dict(beside(position, axis, step), section=1 - lax.axis_index("section"))


def partner():
    return {"section": 1 - lax.axis_index("section")}


def remote(source, target, send, receive, device):
    return pltpu.make_async_remote_copy(
        src_ref=source, dst_ref=target, send_sem=send, recv_sem=receive, device_id=device, device_id_type=MESH
    )


def widened(ref):
    return ref[...].astype(F32)


def cut(ref, dim, where, rows):
    index = [slice(None)] * (len(ref.shape) - 2)
    index[dim] = where
    return ref.at[tuple(index + [pl.ds(*rows), slice(None)])]


def halved(ref, side):
    return ref.at[pl.ds(2 * side, 2)]


class Part:
    def __init__(self, group, which, first, rows, at, bank_at):
        self.group, self.which, self.first = group, which, first
        self.position, self.order = group.position, ORDERS[which]
        self.rows, self.bank_rows = (at, rows), (bank_at, rows)

    def where(self, axis, step):
        return lax.rem(self.position[axis] + (step + 4), 4)

    def copy(self, receive, source, target, axis, step):
        remote(source, target, self.group.first_sends.at[self.which], receive, beside(self.position, axis, step)).start()

    def block(self, step):
        axis = self.order[0]
        return cut(self.group.packed, axis, self.where(axis, step), (self.first, self.rows[1]))

    def inbox(self, which, side=None):
        rows = [pl.ds(*self.bank_rows), slice(None)]
        middle = [slice(None) if side is None else pl.ds(2 * side, 2), slice(None)]
        return self.group.inbox.at[tuple([which] + middle + rows)]

    def outbox(self, side):
        return self.group.outbox.at[pl.ds(2 * side, 2), :, pl.ds(*self.bank_rows), :]

    def steps(self):
        group, axis, rows = self.group, self.order[0], pl.ds(*self.bank_rows)
        far_sem, near_sem = group.far_sems.at[self.which], group.near_sems.at[self.which]
        group.add_swapped(self.which)
        far = self.block(2)
        self.copy(far_sem, halved(far, 0), self.inbox(2, 0), axis, 1)
        self.copy(far_sem, halved(far, 1), self.inbox(2, 1), axis, -1)
        self.copy(near_sem, halved(self.block(1), 1), self.inbox(0, 1), axis, 1)
        self.copy(near_sem, halved(self.block(-1), 0), self.inbox(1, 0), axis, -1)
        yield
        landed(self.inbox(2), far_sem)
        for side, step in ((0, 1), (1, -1)):
            box = self.outbox(side)
            box[...] = (widened(halved(self.block(step), side)) + widened(self.inbox(2, side))).astype(BF16)
            self.copy(near_sem, box, self.inbox(0 if step == 1 else 1, side), axis, step)
        yield
        landed(group.inbox.at[pl.ds(0, 2), :, :, rows, :], near_sem)
        total = widened(self.block(0)) + widened(self.inbox(0)) + widened(self.inbox(1))
        group.held[0][:, :, self.rows[0] : self.rows[0] + self.rows[1], :] = total.astype(BF16)
        landed(group.inbox.at[:, :, :, rows, :], group.first_sends.at[self.which])
        group.free(self.which)
        self.direct(1)
        yield
        group.held[1][:, self.rows[0] : self.rows[0] + self.rows[1], :] = self.summed(1).astype(BF16)
        if group.owner(self.which) is None:
            self.direct(2)
        else:
            pl.when(group.me == group.section)(lambda: self.direct(2))
            pl.when(group.me != group.section)(self.give)
        yield
        if group.owner(self.which) is None:
            group.totals[16 * NORMS : 16 * NORMS + 16, :] = self.summed(2)
        else:
            pl.when(group.me == group.section)(self.finish)
        yield

    def direct(self, phase):
        axis = self.order[phase]
        dim = sorted(self.order[phase:]).index(axis)
        held, slots = self.group.held[phase - 1], self.group.slots[phase - 1]
        for i, step in enumerate((2, 1, -1)):
            remote(cut(held, dim, self.where(axis, step), self.rows), cut(slots, 0, i, self.rows), self.group.late_sends.at[phase - 1],
                   self.group.direct_sems.at[phase - 1, self.which], beside(self.position, axis, step)).start()

    def give(self):
        axis = self.order[2]
        held, slots = self.group.held[1], self.group.slots[2]
        for i, step in enumerate((2, 1, -1, 0)):
            remote(cut(held, 0, self.where(axis, step), self.rows), cut(slots, 0, i, self.rows), self.group.late_sends.at[1],
                   self.group.direct_sems.at[2, self.which], across(self.position, axis, step)).start()

    def finish(self):
        group = self.group
        at = 16 * (group.first + self.group.me * group.half) + self.rows[0]
        group.totals[pl.ds(pl.multiple_of(at, 16), self.rows[1]), :] = self.summed(2)
        at = 16 * (group.first + (1 - self.group.me) * group.half) + self.rows[0]
        landed(group.slots[2].at[:, pl.ds(*self.rows), :], group.direct_sems.at[2, self.which])
        group.totals[pl.ds(pl.multiple_of(at, 16), self.rows[1]), :] = sum(
            [widened(cut(group.slots[2], 0, i, self.rows)) for i in range(1, 4)], widened(cut(group.slots[2], 0, 0, self.rows)))

    def summed(self, phase):
        axis = self.order[phase]
        dim = sorted(self.order[phase:]).index(axis)
        held, slots = self.group.held[phase - 1], self.group.slots[phase - 1]
        whole = slots.at[tuple([slice(None)] * (len(slots.shape) - 2) + [pl.ds(*self.rows), slice(None)])]
        landed(whole, self.group.direct_sems.at[phase - 1, self.which])
        total = widened(cut(held, dim, self.where(axis, 0), self.rows))
        for i in range(3):
            total = total + widened(cut(slots, 0, i, self.rows))
        return total


def landed(ref, semaphore):
    pltpu.make_async_copy(ref, ref, semaphore).wait()


def bank_buffers(units):
    rows = 16 * sum(units)
    return [pltpu.VMEM((3, 4, 4, rows, 128), BF16), pltpu.VMEM((4, 4, rows, 128), BF16)]


def group_buffers(units):
    rows = 16 * sum(units)
    return [pltpu.VMEM(shape + (rows, 128), BF16) for shape in ((4, 4), (4,), (3, 4), (3,), (4,))]


class Group:
    def __init__(self, which, position, packed, arrivals, totals, banks, own, sems, credits):
        self.section, self.first, self.half, self.parts, self.bank = GROUPS[which]
        self.again, self.reused = which >= FIRST_USERS, which < FIRST_USERS
        self.position, self.packed, self.totals = position, packed, totals
        self.me = lax.axis_index("section")
        self.swap_sems, self.far_sems, self.near_sems, self.first_sends, self.direct_sems, self.late_sends = sems
        self.swap_credit, self.part_credit = credits
        self.units = sum(self.parts)
        rows = 16 * self.units
        self.arrival = arrivals[self.bank]
        self.inbox, self.outbox = banks[self.bank]
        self.held, self.slots = own[:2], own[2:]
        self.offsets = [sum(self.parts[:i]) for i in range(3)]
        self.bank_offsets = [sum(BANKS[self.bank][:i]) for i in range(3)]
        self.start, self.other = [
            pl.multiple_of(16 * STARTS[which] + side * rows, 16) for side in (self.me, 1 - self.me)
        ]
        self.work = [
            Part(self, i, self.start + 16 * self.offsets[i], 16 * self.parts[i], 16 * self.offsets[i], 16 * self.bank_offsets[i])
            for i in range(3)
        ]

    def owner(self, i):
        return self.section if self.offsets[i] < self.half else None

    def swap(self, i):
        rows = 16 * self.parts[i]
        source = self.packed.at[:, :, :, pl.ds(self.other + 16 * self.offsets[i], rows), :]
        target = self.arrival.at[:, :, :, pl.ds(16 * self.bank_offsets[i], rows), :]
        return remote(source, target, self.swap_sems.at[3], self.swap_sems.at[i], partner())

    def start_swap(self):
        self.begun = 0
        if self.again:
            self.before.swapped()
            pl.semaphore_wait(self.swap_credit, 1)
        for i in range(3):
            self.swap(i).start()
        self.steps = [part.steps() for part in self.work]

    def add_swapped(self, i):
        part = self.work[i]
        self.swap(i).wait_recv()
        mine = self.packed.at[:, :, :, pl.ds(part.first, part.rows[1]), :]
        mine[...] = mine[...] + self.arrival[:, :, :, part.bank_rows[0] : part.bank_rows[0] + part.rows[1], :]
        self.begun += 1
        if self.reused and self.begun == 3:
            pl.semaphore_signal(self.swap_credit, inc=1, device_id=partner(), device_id_type=MESH)
        if self.again:
            pl.semaphore_wait(self.part_credit.at[i], 2)

    def free(self, i):
        if self.reused:
            for step in (1, -1):
                pl.semaphore_signal(self.part_credit.at[i], inc=1, device_id=beside(self.position, ORDERS[i][0], step), device_id_type=MESH)

    def swapped(self):
        landed(self.packed.at[:, :, :, pl.ds(self.other, 16 * self.units), :], self.swap_sems.at[3])

    def close(self):
        if self.again:
            self.swapped()
        landed(self.slots[0], self.late_sends.at[0])
        given = 16 * self.half
        rest = 16 * self.units - given

        @pl.when(self.me == self.section)
        def _():
            landed(self.slots[1], self.late_sends.at[1])

        @pl.when(self.me != self.section)
        def _():
            if rest:
                landed(self.packed.at[0, 0, 0, pl.ds(0, 4 * given + 3 * rest), :], self.late_sends.at[1])
            else:
                landed(self.slots[2], self.late_sends.at[1])


def keep_attention():
    return [pltpu.VMEM((256, 1536), BF16), pltpu.VMEM((8, 256, 256), BF16), pltpu.VMEM((256, 512), BF16)]


def keep_norm():
    return [pltpu.VMEM((256, 512), F32)]


def keep_ffn():
    return [pltpu.VMEM((256, 512), BF16), pltpu.VMEM((256, 2048), BF16), pltpu.VMEM((256, 2048), BF16)]


def stacked(scratch):
    return [pltpu.VMEM((2,) + tuple(s.shape), s.dtype) for s in scratch]


def scratch_shapes():
    low, wide, square = pltpu.VMEM((256, 512), BF16), pltpu.VMEM((256, 512), F32), pltpu.VMEM((256, 256), BF16)
    return dict(
        weights=stacked([pltpu.VMEM(shape, BF16) for shape in WEIGHTS]),
        inputs=stacked([low, low, pltpu.VMEM((6, 1, 512), F32)]),
        selfs=stacked(keep_attention() + keep_norm() + [pltpu.VMEM((256, 1), F32)]),
        scales=pltpu.VMEM((256, 128), F32),
        firsts=stacked([low, wide]),
        enc=keep_ffn()[1:] + keep_norm() + keep_norm() + [pltpu.VMEM((256, 1024), BF16)],
        cross=[low, pltpu.VMEM((8, 256, 256), BF16), low] + keep_norm(),
        dec=keep_ffn() + keep_norm(),
        bias=[pltpu.VMEM((2, 256, 256), BF16), square],
        work=[wide, low, pltpu.VMEM((8, 512), F32)],
        results=[low, low],
        packed=pltpu.VMEM((4, 4, 4, 16 * PACKED_UNITS, 128), BF16),
        arrivals=[pltpu.VMEM((4, 4, 4, 16 * sum(units), 128), BF16) for units in BANKS],
        banks=[bank_buffers(units) for units in BANKS],
        groups=[group_buffers(group[3]) for group in GROUPS],
        places=[pltpu.VMEM((2, 1, ROW), jnp.int32), pltpu.SMEM((2, 1, NSEG), jnp.int32)],
        totals=pltpu.VMEM((464, 128), F32),
        in_sems=pltpu.SemaphoreType.DMA((2, 8)),
        in_sends=pltpu.SemaphoreType.DMA((8,)),
        place_sems=pltpu.SemaphoreType.DMA((3,)),
        project_sems=pltpu.SemaphoreType.DMA((2,)),
        out_sems=pltpu.SemaphoreType.DMA((3, 2)),
        group_sems=[
            [pltpu.SemaphoreType.DMA(shape) for shape in ((3, 3), (2,))]
            for _ in GROUPS
        ],
        bank_sems=[[pltpu.SemaphoreType.DMA(shape) for shape in ((4,), (3,), (3,), (3,))] for _ in BANKS],
        swap_credit=pltpu.SemaphoreType.REGULAR((3,)),
        part_credit=pltpu.SemaphoreType.REGULAR((3, 3)),
    )


def whole_kernel(tree, *refs):
    tokens, cotangent, lengths_in, segments_in = refs[:4]
    own = refs[4:9]
    norm_params = refs[9]
    layer_out, token_grads = refs[10:12]
    totals_out = refs[12]
    s = jax.tree.unflatten(tree, refs[13:])
    me = lax.axis_index("section")
    position = place()

    barrier = pltpu.get_barrier_semaphore()
    pl.semaphore_signal(barrier, inc=1, device_id=partner(), device_id_type=MESH)
    for axis in range(3):
        for step in (1, -1):
            pl.semaphore_signal(barrier, inc=1, device_id=beside(position, axis, step), device_id_type=MESH)
            pl.semaphore_signal(barrier, inc=1, device_id=across(position, axis, step), device_id_type=MESH)

    held = list(s["weights"]) + list(s["inputs"])

    def given(i, micro):
        if i < 5:
            return own[i].at[0]
        if i == 7:
            return norm_params
        return (tokens, cotangent)[i - 5].at[0, micro, 0]

    def local(i):
        return pltpu.make_async_copy(given(i, me), held[i].at[me], s["in_sems"].at[me, i])

    def sent(i):
        return remote(given(i, 1 - me), held[i].at[me], s["in_sends"].at[i], s["in_sems"].at[me, i], partner())

    def ready(j, i):
        pltpu.make_async_copy(given(i, 0), held[i].at[j], s["in_sems"].at[j, i]).wait()

    segments, lengths = s["places"]
    places = [pltpu.make_async_copy((segments_in, lengths_in)[i], s["places"][i], s["place_sems"].at[i]) for i in range(2)]
    others = pltpu.make_async_copy(given(5, 1 - me), s["dec"][0], s["place_sems"].at[2])
    for copy in places:
        copy.start()
    others.start()
    for i in (0, 5, 7, 1, 3, 4, 2, 6):
        local(i).start()

    pl.semaphore_wait(barrier, 13)
    for i in (5, 7, 1):
        sent(i).start()

    def pieces(i):
        first = 0
        for k, rows in enumerate((352, 352, 336, 336, 336, 336)):
            piece = pl.ds(first, rows)
            remote(own[i].at[0, piece], held[i].at[me, piece], s["in_sends"].at[i], s["in_sems"].at[me, i],
                   across(position, k // 2, 1 - 2 * (k % 2))).start()
            first += rows

    @pl.when(me == 0)
    def _():
        pieces(4)


    for copy in places:
        copy.wait()

    bias, cross_bias = s["bias"]
    lane = lax.broadcasted_iota(jnp.int32, (1, ROW), 1)
    down = lax.broadcasted_iota(jnp.int32, (ROW, 1), 0)
    ids_row, ids_col = jnp.zeros((1, ROW), jnp.int32), jnp.zeros((ROW, 1), jnp.int32)
    bound = jnp.int32(0)
    for j in range(NSEG):
        bound = bound + lengths[me, 0, j]
        ids_row = ids_row + (lane >= bound).astype(jnp.int32)
        ids_col = ids_col + (down >= bound).astype(jnp.int32)
    target_row = segments[me].astype(F32)
    target_col = jnp.broadcast_to(target_row, (128, ROW)).T[:, 0:1]
    ids_row, ids_col = ids_row.astype(F32), ids_col.astype(F32)
    bias[0] = jnp.where(ids_col == ids_row, 0.0, -1e30).astype(BF16)
    bias[1] = jnp.where(target_col == target_row, 0.0, -1e30).astype(BF16)
    cross_bias[...] = jnp.where(target_col == ids_row, 0.0, -1e30).astype(BF16)

    w_self_in, w_self_out, w_cross, w_in, w_out = s["weights"]
    x, cot, norms = s["inputs"]
    first_low, first = s["firsts"]
    work, grad_context, grad_norms = s["work"]
    memory_low, third_low = s["results"]
    source_grad, target_grad = first.at[0], first.at[1]

    others.wait()
    ready(me, 0)
    staged = s["enc"][0].at[:, pl.ds(0, 1536)]
    project(s["dec"][0], w_self_in.at[me], staged)
    given_projection = remote(staged, s["selfs"][0].at[me], s["project_sems"].at[0], s["project_sems"].at[1], partner())
    given_projection.start()

    @pl.when(me == 0)
    def _():
        for i in (3, 2, 6, 0):
            sent(i).start()

    @pl.when(me != 0)
    def _():
        for i in (2, 3, 4, 6, 0):
            sent(i).start()

    for i in range(2):
        j = lax.rem(me + i, 2)
        for which in (5, 7, 1):
            ready(j, which)
        projected, shares, context, normed, scale = [ref.at[j] for ref in s["selfs"]]
        if i == 0:
            project(x.at[j], w_self_in.at[j], projected)
        else:
            landed(projected, s["project_sems"].at[1])
        result = self_forward(x.at[j], w_self_out.at[j], bias.at[j], norms.at[j], projected, shares, context, normed, scale)
        first[j] = result
        first_low[j] = result.astype(BF16)

    enc_active, enc_slopes, enc_normed, memory_normed, key_value = s["enc"]
    queries, cross_shares, cross_context, cross_normed = s["cross"]
    dec_low, dec_active, dec_slopes, dec_normed = s["dec"]
    enc_scale, memory_scale, cross_scale, dec_scale = [s["scales"].at[:, i : i + 1] for i in range(4)]
    enc_self, dec_self = [ref.at[0] for ref in s["selfs"]], [ref.at[1] for ref in s["selfs"]]
    enc_norms, dec_norms = norms.at[0], norms.at[1]

    given_projection.wait_send()
    result = ffn_forward(first_low.at[0], w_in.at[0], w_out.at[0], enc_active, enc_slopes, lambda: ready(0, 3), lambda: ready(0, 4))
    second = norm(first[0] + result, enc_norms, 1, enc_normed, enc_scale)
    memory = norm(second, enc_norms, 2, memory_normed, memory_scale).astype(BF16)
    memory_low[...] = memory
    ready(0, 2)
    for i in range(2):
        key_value[:, 512 * i : 512 * i + 512] = dot(memory, w_cross[0, :, 512 * i : 512 * i + 512]).astype(BF16)

    ready(1, 2)
    queries[...] = dot(first_low[1], w_cross[1, :, :512]).astype(BF16)
    keys_values = (columns_of(key_value, 0), columns_of(key_value, 512))
    attend(columns_of(queries, 0), *keys_values, cross_bias, cross_shares, cross_context)
    second = norm(first[1] + dot(cross_context[...], w_cross[1, :, 512:]), dec_norms, 2, cross_normed, cross_scale)
    dec_low[...] = second.astype(BF16)
    result = ffn_forward(dec_low, w_in.at[1], w_out.at[1], dec_active, dec_slopes, lambda: ready(1, 3), lambda: ready(1, 4))
    third_low[...] = norm(second + result, dec_norms, 1, dec_normed, dec_scale).astype(BF16)

    def put_out(slot, out, values):
        for j in range(2):
            here = pltpu.make_async_copy(values[j], out.at[0, me, 0], s["out_sems"].at[0, slot])
            there = remote(values[j], out.at[0, me, 0], s["out_sems"].at[1, slot], s["out_sems"].at[2, slot], partner())

            @pl.when(me == j)
            def _():
                here.start()

            @pl.when(me != j)
            def _():
                there.start()

    def out_done(slot, out, values):
        pltpu.make_async_copy(values[0], out.at[0, me, 0], s["out_sems"].at[0, slot]).wait()
        there = remote(values[0], out.at[0, me, 0], s["out_sems"].at[1, slot], s["out_sems"].at[2, slot], partner())
        there.wait_send()
        there.wait_recv()

    put_out(0, layer_out, (memory_low, third_low))

    packed = s["packed"]
    groups = [
        Group(g, position, packed, s["arrivals"], s["totals"], s["banks"], s["groups"][g], s["bank_sems"][GROUPS[g][4]] + s["group_sems"][g],
              (s["swap_credit"].at[GROUPS[g][4]], s["part_credit"].at[GROUPS[g][4]]))
        for g in range(len(GROUPS))
    ]
    for group in groups[FIRST_USERS:]:
        group.before = next(other for other in groups if other.bank == group.bank)

    def at(moment, which=None):
        for step in SCHEDULE.get(moment if which is None else moment + str(which), "").split():
            group = groups[int(step[0])]
            if step[1] == "s":
                group.start_swap()
            else:
                next(group.steps["abc".index(step[1])])

    def ffn_back(gradient, low, section, activated, slopes, moment):
        result = gradient.astype(BF16)
        for i in range(4):
            pack_tall(packed, section, i, dot_tn(activated[:, 512 * i : 512 * i + 512], result))
        at(moment + "_out")
        for i in range(4):
            rows = slice(512 * i, 512 * i + 512)
            slopes[:, rows] = (dot_nt(result, w_out[section, rows, :]) * slopes[:, rows].astype(F32)).astype(BF16)
        for i in range(4):
            pack(packed, section, HIDDEN_IN + 2 * i, dot_tn(low[...], slopes[:, 512 * i : 512 * i + 512]))
            at(moment + "_in", i)
        return dot_nt(slopes[...], w_in[section])

    def self_back_a(gradient, section, kept):
        projected, shares, context, normed, scale = kept
        low = gradient.astype(BF16)
        pack(packed, section, SELF_OUT, dot_tn(context[...], low))
        grad_context[...] = dot_nt(low, w_self_out[section]).astype(BF16)

    def self_back_b(section, kept, moment):
        projected, shares, context, normed, scale = kept
        attend_back(*thirds(projected), shares, context, grad_context, *[putter(projected, 512 * i) for i in range(3)])
        at(moment + "_attend")

    def self_back_c(section, kept):
        projected = kept[0]
        for i in range(3):
            pack(packed, section, SELF_IN + 2 * i, dot_tn(x[section], projected[:, 512 * i : 512 * i + 512]))
        pack_norms(packed, section, grad_norms)

    grad_norms[...] = jnp.zeros_like(grad_norms)
    ready(1, 6)
    gradient = norm_back(cot[1].astype(F32), dec_norms, 1, dec_normed, dec_scale, grad_norms)
    gradient = gradient + ffn_back(gradient, dec_low, 1, dec_active, dec_slopes, "dec")
    gradient = norm_back(gradient, dec_norms, 2, cross_normed, cross_scale, grad_norms)
    work[...] = gradient
    low = gradient.astype(BF16)
    pack(packed, 1, CROSS + 2, dot_tn(cross_context[...], low))
    grad_context[...] = dot_nt(low, w_cross[1, :, 512:]).astype(BF16)
    at("cross_start")
    attend_back(columns_of(queries, 0), *keys_values, cross_shares, cross_context, grad_context,
                putter(queries, 0), putter(key_value, 0), putter(key_value, 512))
    at("cross_attend")
    pack(packed, 1, CROSS, dot_tn(first_low[1], queries[...]))
    gradient = work[...] + dot_nt(queries[...], w_cross[1, :, :512])
    gradient = norm_back(gradient, dec_norms, 0, *dec_self[3:], grad_norms)
    work[...] = gradient
    at("cross_end")
    self_back_a(gradient, 1, dec_self)
    at("dec_start")
    self_back_b(1, dec_self, "dec")
    self_back_c(1, dec_self)
    at("dec_end")
    pl.when(me != 1)(lambda: ready(1, 0))
    target_grad[...] = work[...] + dot_nt(dec_self[0][...], w_self_in[1])

    for i in range(2):
        pack(packed, 0, CROSS + 2 * i, dot_tn(memory_low[...], key_value[:, 512 * i : 512 * i + 512]))
    at("memory_start")
    ready(0, 6)
    gradient = cot[0].astype(F32) + dot_nt(key_value[...], w_cross[0])
    gradient = norm_back(gradient, enc_norms, 2, memory_normed, memory_scale, grad_norms)
    gradient = norm_back(gradient, enc_norms, 1, enc_normed, enc_scale, grad_norms)
    at("memory_end")
    gradient = gradient + ffn_back(gradient, first_low.at[0], 0, enc_active, enc_slopes, "enc")
    gradient = norm_back(gradient, enc_norms, 0, *enc_self[3:], grad_norms)
    work[...] = gradient
    self_back_a(gradient, 0, enc_self)
    at("enc_start")
    self_back_b(0, enc_self, "enc")
    self_back_c(0, enc_self)
    at("enc_end")
    pl.when(me != 0)(lambda: ready(0, 0))
    source_grad[...] = work[...] + dot_nt(enc_self[0][...], w_self_in[0])
    put_out(1, token_grads, (source_grad, target_grad))
    at("last")

    for group in groups:
        group.close()
    copy = pltpu.make_async_copy(s["totals"], totals_out, s["place_sems"].at[0])
    copy.start()
    for i in range(8):
        sent(i).wait_send()
    out_done(0, layer_out, (memory_low, third_low))
    out_done(1, token_grads, (source_grad, target_grad))
    copy.wait()


def finish_kernel(layer_in, grads_in, totals, layer_out, token_grads, *refs):
    grad_refs, grad_norms = refs[:5], refs[5]
    layer_out[...] = layer_in[...]
    token_grads[...] = grads_in[...]

    def tile(t):
        return totals[8 * t : 8 * t + 8, :]

    for which, unit, columns in ((0, SELF_IN, 1536), (1, SELF_OUT, 512), (2, CROSS, 1024), (3, HIDDEN_IN, 2048)):
        for i in range(columns // 128):
            grad_refs[which][0, :, 128 * i : 128 * i + 128] = tile(2 * unit + i)
    for r in range(4):
        for i in range(4):
            grad_refs[4][0, 8 * r : 8 * r + 8, 128 * i : 128 * i + 128] = tile(2 * HIDDEN_OUT + 4 * r + i)
    turned = jnp.concatenate([tile(2 * NORMS), jnp.zeros((120, 128), F32)], 0).T
    for i in range(6):
        grad_norms[i] = turned[i : i + 1, :8]


def body(tokens, cotangent, source_lengths, target_segments, self_in, self_out, cross_weight, hidden_in, hidden_out, norm_params):
    shapes, tree = jax.tree.flatten(scratch_shapes())
    vmem, hbm = [pl.BlockSpec(memory_space=space) for space in (pltpu.VMEM, pl.ANY)]
    large = [jax.ShapeDtypeStruct(tokens.shape, BF16), jax.ShapeDtypeStruct(tokens.shape, F32)]
    layer, grads, totals = pl.pallas_call(
        lambda *refs: whole_kernel(tree, *refs),
        out_shape=large + [jax.ShapeDtypeStruct((464, 128), F32)],
        in_specs=[hbm] * 10,
        out_specs=[hbm] * 3,
        scratch_shapes=shapes,
        compiler_params=pltpu.CompilerParams(collective_id=0, has_side_effects=True, vmem_limit_bytes=64 << 20),
        name="layer_pair",
    )(tokens, cotangent, source_lengths, target_segments, self_in, self_out, cross_weight, hidden_in, hidden_out,
      norm_params.transpose(1, 0, 2))
    small = [(1, 8, 1536), (1, 8, 512), (1, 8, 1024), (1, 8, 2048), (1, 32, 512), (6, 1, 8)]
    results = pl.pallas_call(
        finish_kernel,
        out_shape=large + [jax.ShapeDtypeStruct(shape, F32) for shape in small],
        in_specs=[vmem] * 3,
        out_specs=[vmem] * 8,
        name="finish",
    )(layer, grads, totals)
    return (*results[:7], results[7].transpose(1, 0, 2))


def solution(mesh):
    return jax.shard_map(
        body,
        mesh=mesh,
        in_specs=(
            P("section", None, "dp", None, None),
            P("section", None, "dp", None, None),
            P(None, "dp", None),
            P(None, "dp", None),
            P("section", None, None),
            P("section", None, None),
            P("section", None, None),
            P("section", None, None),
            P("section", None, None),
            P("section", None, None),
        ),
        out_specs=(
            P("section", None, "dp", None, None),
            P("section", None, "dp", None, None),
            P("section", "dp", None),
            P("section", "dp", None),
            P("section", "dp", None),
            P("section", "dp", None),
            P("section", "dp", None),
            P("section", None, "dp"),
        ),
        check_vma=False,
    )
```

```python
import jax
import jax.numpy as jnp
from jax import lax
from jax.experimental import pallas as pl
from jax.experimental.pallas import tpu as pltpu
from jax.sharding import PartitionSpec as P

HEADS = 8
D = 512
ROW = 256
NSEG = 8
root_half = 0.7071067811865476
inverse_root = 0.3989422804014327
F32 = jnp.float32
BF16 = jnp.bfloat16
MESH = pl.DeviceIdType.MESH
WEIGHTS = ((512, 1536), (512, 512), (512, 1024), (512, 2048), (2048, 512))

HIDDEN_OUT, HIDDEN_IN, CROSS, SELF_OUT, SELF_IN, NORMS = 0, 8, 16, 20, 22, 28
GROUPS = (
    (1, 0, 4, (2, 1, 1), 0),
    (1, 8, 4, (1, 2, 1), 1),
    (1, 16, 6, (2, 2, 2), 2),
    (0, 0, 4, (1, 1, 2), 0),
    (0, 8, 6, (2, 2, 2), 1),
    (0, 20, 4, (2, 2, 1), 2),
)
BANKS = ((2, 1, 2), (2, 2, 2), (2, 2, 2))
FIRST_USERS = 3
ORDERS = ((0, 1, 2), (1, 2, 0), (2, 0, 1))
STARTS = (0, 8, 16, 28, 36, 48)
SCHEDULE = dict(
    dec_in3="1s 0s",
    dec_start="1b 1a",
    dec_end="2s 0a 0c 1c",
    memory_start="0b",
    memory_end="1a 1b",
    enc_out="3s 2a",
    enc_in0="0c 2b",
    enc_in1="2c",
    enc_in3="0a 4s 0b",
    enc_start="1a 1b 0c",
    enc_attend="2b 2a 2c",
    enc_end="4b",
    last="5s 1c 4a 3c 0a 0b 2a 3a 1c 2b 5a 2c 3b 3c 5b 4c 5a 4a 5c 0b 4b 3a 0c 3b 4c 3c 5b 5c 5a 4b 2b 3b 1c 4a 4c 0c 5b 3a 2c 5c 3c 2a 1b 4b 0a 0b 2b 1a 3b 5a 4c 4a 5b 3a 5c 2c 3c 2a 4b 4a 3b 1b 5a 1a 4c 1c 5b 3a 0a 5c",
)
PACKED_UNITS = 58


def unit_of(section, unit):
    if section == 1:
        return 57 if unit == NORMS else unit
    return 52 if unit == NORMS else 28 + unit + (1 if unit >= 24 else 0)


def dot(a, b):
    return lax.dot_general(a, b, (((1,), (0,)), ((), ())), preferred_element_type=F32)


def dot_nt(a, b):
    return lax.dot_general(a, b, (((1,), (1,)), ((), ())), preferred_element_type=F32)


def dot_tn(a, b):
    return lax.dot_general(a, b, (((0,), (0,)), ((), ())), preferred_element_type=F32)

def sides(factor):
    lane = lax.broadcasted_iota(jnp.int32, (1, 128), 1)
    low = jnp.where(lane < 64, factor, 0.0).astype(BF16)
    high = jnp.where(lane < 64, 0.0, factor).astype(BF16)
    return (low, high)


def attend(query, key, value, bias, shares, context):
    scaled, plain = sides(0.125), sides(1.0)
    heads = [(pair, side) for pair in range(HEADS // 2) for side in range(2)]
    masked = bias[...].astype(F32)
    scores = [dot_nt(query(pair) * scaled[side], key(pair)) + masked for pair, side in heads]
    expvals = [jnp.exp(score - jnp.max(score, -1, keepdims=True)) for score in scores]
    low = [(expval * (1.0 / jnp.sum(expval, -1, keepdims=True))).astype(BF16) for expval in expvals]
    for head in range(HEADS):
        shares[head] = low[head]
    for pair in range(HEADS // 2):
        parts = [dot(low[2 * pair + side], value(pair) * plain[side]) for side in range(2)]
        context[:, 128 * pair : 128 * pair + 128] = (parts[0] + parts[1]).astype(BF16)


def attend_back(query, key, value, shares, context, grad_context, put_query, put_key, put_value):
    scaled, plain = sides(0.125), sides(1.0)
    heads = [(pair, side) for pair in range(HEADS // 2) for side in range(2)]
    given = [grad_context[:, 128 * pair : 128 * pair + 128] for pair in range(HEADS // 2)]
    along = [given[pair].astype(F32) * context[:, 128 * pair : 128 * pair + 128].astype(F32) for pair in range(HEADS // 2)]
    grad_shares = [dot_nt(given[pair] * plain[side], value(pair)) for pair, side in heads]
    deltas = [jnp.sum(along[pair] * plain[side].astype(F32), -1, keepdims=True) for pair, side in heads]
    low = [(shares[i].astype(F32) * (grad_shares[i] - deltas[i])).astype(BF16) for i in range(HEADS)]
    for pair in range(HEADS // 2):
        q, k, g = query(pair), key(pair), given[pair]
        one, two = low[2 * pair], low[2 * pair + 1]
        grad_query = dot(one, k * scaled[0]) + dot(two, k * scaled[1])
        grad_key = dot_tn(one, q * scaled[0]) + dot_tn(two, q * scaled[1])
        grad_value = dot_tn(shares[2 * pair], g * plain[0]) + dot_tn(shares[2 * pair + 1], g * plain[1])
        put_query(pair, grad_query.astype(BF16))
        put_key(pair, grad_key.astype(BF16))
        put_value(pair, grad_value.astype(BF16))


def mean(values):
    return jnp.sum(values, -1, keepdims=True) * (1.0 / D)


def norm(values, params, which, normed, scale):
    center = values - mean(values)
    inverse = lax.rsqrt(mean(center * center) + 1e-05)
    result = center * inverse
    normed[...] = result
    scale[...] = inverse
    return result * params[2 * which] + params[2 * which + 1]


def norm_back(gradient, params, which, normed, scale, grad_norms):
    n = normed[...]
    grad_norms[2 * which : 2 * which + 1, :] = jnp.sum(gradient * n, 0, keepdims=True)
    grad_norms[2 * which + 1 : 2 * which + 2, :] = jnp.sum(gradient, 0, keepdims=True)
    scaled = gradient * params[2 * which]
    return scale[...] * (scaled - mean(scaled) - n * mean(scaled * n))


def pack(packed, section, unit, value):
    blocks = value.reshape(4, 4, 4, 8, value.shape[1])
    for i in range(value.shape[1] // 256):
        two = jnp.concatenate([blocks[..., 256 * i : 256 * i + 128], blocks[..., 256 * i + 128 : 256 * i + 256]], 3)
        at = 16 * unit_of(section, unit + i)
        packed[:, :, :, at : at + 16, :] = two.astype(BF16)


def pack_tall(packed, section, first, value):
    blocks = value.reshape(4, 4, 4, 8, 512)
    for r in range(4):
        for i in range(2):
            two = jnp.concatenate([blocks[:, :, r, :, 256 * i : 256 * i + 128], blocks[:, :, r, :, 256 * i + 128 : 256 * i + 256]], 2)
            at = 16 * unit_of(section, HIDDEN_OUT + 2 * r + i)
            packed[first, :, :, at : at + 16, :] = two.astype(BF16)


def pack_norms(packed, section, grad_norms):
    turned = jnp.concatenate([grad_norms[...], jnp.zeros((120, 512), F32)], 0).T
    tiles = turned.reshape(4, 4, 4, 8, 128)
    at = 16 * unit_of(section, NORMS)
    packed[:, :, :, at : at + 16, :] = jnp.concatenate([tiles, jnp.zeros_like(tiles)], 3).astype(BF16)

def columns_of(ref, first):
    return lambda pair: ref[:, first + 128 * pair : first + 128 * pair + 128]


def putter(ref, first):
    def put(pair, value):
        ref[:, first + 128 * pair : first + 128 * pair + 128] = value

    return put


def thirds(ref):
    return columns_of(ref, 0), columns_of(ref, 512), columns_of(ref, 1024)


def project(inputs, self_in, projected):
    for i in range(3):
        projected[:, 512 * i : 512 * i + 512] = dot(inputs[...], self_in[:, 512 * i : 512 * i + 512]).astype(BF16)


def self_forward(inputs, self_out, bias, params, projected, shares, context, normed, scale):
    attend(*thirds(projected), bias, shares, context)
    return norm(inputs[...].astype(F32) + dot(context[...], self_out[...]), params, 0, normed, scale)


def ffn_forward(low, hidden_in, hidden_out, activated, slopes, ready_in, ready_out):
    ready_in()
    for i in range(4):
        hidden = dot(low[...], hidden_in[:, 512 * i : 512 * i + 512])
        cdf = 0.5 * (1.0 + lax.erf(hidden * root_half))
        activated[:, 512 * i : 512 * i + 512] = (hidden * cdf).astype(BF16)
        slope = cdf + hidden * jnp.exp(-0.5 * hidden * hidden) * inverse_root
        slopes[:, 512 * i : 512 * i + 512] = slope.astype(BF16)
    ready_out()
    return dot(activated[...], hidden_out[...])


def place():
    dp = lax.axis_index("dp")
    return [lax.div(dp, 16), lax.rem(lax.div(dp, 4), 4), lax.rem(dp, 4)]


def beside(position, axis, step):
    moved = list(position)
    moved[axis] = lax.rem(moved[axis] + (step + 4), 4)
    return {"dp": (moved[0] * 4 + moved[1]) * 4 + moved[2]}


def across(position, axis, step):
    return dict(beside(position, axis, step), section=1 - lax.axis_index("section"))


def partner():
    return {"section": 1 - lax.axis_index("section")}


def remote(source, target, send, receive, device):
    return pltpu.make_async_remote_copy(
        src_ref=source, dst_ref=target, send_sem=send, recv_sem=receive, device_id=device, device_id_type=MESH
    )


def widened(ref):
    return ref[...].astype(F32)


def cut(ref, dim, where, rows):
    index = [slice(None)] * (len(ref.shape) - 2)
    index[dim] = where
    return ref.at[tuple(index + [pl.ds(*rows), slice(None)])]


def halved(ref, side):
    return ref.at[pl.ds(2 * side, 2)]


class Part:
    def __init__(self, group, which, first, rows, at, bank_at):
        self.group, self.which, self.first = group, which, first
        self.position, self.order = group.position, ORDERS[which]
        self.rows, self.bank_rows = (at, rows), (bank_at, rows)

    def where(self, axis, step):
        return lax.rem(self.position[axis] + (step + 4), 4)

    def copy(self, receive, source, target, axis, step):
        remote(source, target, self.group.first_sends.at[self.which], receive, beside(self.position, axis, step)).start()

    def block(self, step):
        axis = self.order[0]
        return cut(self.group.packed, axis, self.where(axis, step), (self.first, self.rows[1]))

    def inbox(self, which, side=None):
        rows = [pl.ds(*self.bank_rows), slice(None)]
        middle = [slice(None) if side is None else pl.ds(2 * side, 2), slice(None)]
        return self.group.inbox.at[tuple([which] + middle + rows)]

    def outbox(self, side):
        return self.group.outbox.at[pl.ds(2 * side, 2), :, pl.ds(*self.bank_rows), :]

    def steps(self):
        group, axis, rows = self.group, self.order[0], pl.ds(*self.bank_rows)
        far_sem, near_sem = group.far_sems.at[self.which], group.near_sems.at[self.which]
        group.add_swapped(self.which)
        far = self.block(2)
        self.copy(far_sem, halved(far, 0), self.inbox(2, 0), axis, 1)
        self.copy(far_sem, halved(far, 1), self.inbox(2, 1), axis, -1)
        self.copy(near_sem, halved(self.block(1), 1), self.inbox(0, 1), axis, 1)
        self.copy(near_sem, halved(self.block(-1), 0), self.inbox(1, 0), axis, -1)
        yield
        landed(self.inbox(2), far_sem)
        for side, step in ((0, 1), (1, -1)):
            box = self.outbox(side)
            box[...] = (widened(halved(self.block(step), side)) + widened(self.inbox(2, side))).astype(BF16)
            self.copy(near_sem, box, self.inbox(0 if step == 1 else 1, side), axis, step)
        yield
        landed(group.inbox.at[pl.ds(0, 2), :, :, rows, :], near_sem)
        total = widened(self.block(0)) + widened(self.inbox(0)) + widened(self.inbox(1))
        group.held[0][:, :, self.rows[0] : self.rows[0] + self.rows[1], :] = total.astype(BF16)
        landed(group.inbox.at[:, :, :, rows, :], group.first_sends.at[self.which])
        group.free(self.which)
        self.direct(1)
        yield
        group.held[1][:, self.rows[0] : self.rows[0] + self.rows[1], :] = self.summed(1).astype(BF16)
        if group.owner(self.which) is None:
            self.direct(2)
        else:
            pl.when(group.me == group.section)(lambda: self.direct(2))
            pl.when(group.me != group.section)(self.give)
        yield
        if group.owner(self.which) is None:
            group.totals[16 * NORMS : 16 * NORMS + 16, :] = self.summed(2)
        else:
            pl.when(group.me == group.section)(self.finish)
        yield

    def direct(self, phase):
        axis = self.order[phase]
        dim = sorted(self.order[phase:]).index(axis)
        held, slots = self.group.held[phase - 1], self.group.slots[phase - 1]
        for i, step in enumerate((2, 1, -1)):
            remote(cut(held, dim, self.where(axis, step), self.rows), cut(slots, 0, i, self.rows), self.group.late_sends.at[phase - 1],
                   self.group.direct_sems.at[phase - 1, self.which], beside(self.position, axis, step)).start()

    def give(self):
        axis = self.order[2]
        held, slots = self.group.held[1], self.group.slots[2]
        for i, step in enumerate((2, 1, -1, 0)):
            remote(cut(held, 0, self.where(axis, step), self.rows), cut(slots, 0, i, self.rows), self.group.late_sends.at[1],
                   self.group.direct_sems.at[2, self.which], across(self.position, axis, step)).start()

    def finish(self):
        group = self.group
        at = 16 * (group.first + self.group.me * group.half) + self.rows[0]
        group.totals[pl.ds(pl.multiple_of(at, 16), self.rows[1]), :] = self.summed(2)
        at = 16 * (group.first + (1 - self.group.me) * group.half) + self.rows[0]
        landed(group.slots[2].at[:, pl.ds(*self.rows), :], group.direct_sems.at[2, self.which])
        group.totals[pl.ds(pl.multiple_of(at, 16), self.rows[1]), :] = sum(
            [widened(cut(group.slots[2], 0, i, self.rows)) for i in range(1, 4)], widened(cut(group.slots[2], 0, 0, self.rows)))

    def summed(self, phase):
        axis = self.order[phase]
        dim = sorted(self.order[phase:]).index(axis)
        held, slots = self.group.held[phase - 1], self.group.slots[phase - 1]
        whole = slots.at[tuple([slice(None)] * (len(slots.shape) - 2) + [pl.ds(*self.rows), slice(None)])]
        landed(whole, self.group.direct_sems.at[phase - 1, self.which])
        total = widened(cut(held, dim, self.where(axis, 0), self.rows))
        for i in range(3):
            total = total + widened(cut(slots, 0, i, self.rows))
        return total


def landed(ref, semaphore):
    pltpu.make_async_copy(ref, ref, semaphore).wait()


def bank_buffers(units):
    rows = 16 * sum(units)
    return [pltpu.VMEM((3, 4, 4, rows, 128), BF16), pltpu.VMEM((4, 4, rows, 128), BF16)]


def group_buffers(units):
    rows = 16 * sum(units)
    return [pltpu.VMEM(shape + (rows, 128), BF16) for shape in ((4, 4), (4,), (3, 4), (3,), (4,))]


class Group:
    def __init__(self, which, position, packed, arrivals, totals, banks, own, sems, credits):
        self.section, self.first, self.half, self.parts, self.bank = GROUPS[which]
        self.again, self.reused = which >= FIRST_USERS, which < FIRST_USERS
        self.position, self.packed, self.totals = position, packed, totals
        self.me = lax.axis_index("section")
        self.swap_sems, self.far_sems, self.near_sems, self.first_sends, self.direct_sems, self.late_sends = sems
        self.swap_credit, self.part_credit = credits
        self.units = sum(self.parts)
        rows = 16 * self.units
        self.arrival = arrivals[self.bank]
        self.inbox, self.outbox = banks[self.bank]
        self.held, self.slots = own[:2], own[2:]
        self.offsets = [sum(self.parts[:i]) for i in range(3)]
        self.bank_offsets = [sum(BANKS[self.bank][:i]) for i in range(3)]
        self.start, self.other = [
            pl.multiple_of(16 * STARTS[which] + side * rows, 16) for side in (self.me, 1 - self.me)
        ]
        self.work = [
            Part(self, i, self.start + 16 * self.offsets[i], 16 * self.parts[i], 16 * self.offsets[i], 16 * self.bank_offsets[i])
            for i in range(3)
        ]

    def owner(self, i):
        return self.section if self.offsets[i] < self.half else None

    def swap(self, i):
        rows = 16 * self.parts[i]
        source = self.packed.at[:, :, :, pl.ds(self.other + 16 * self.offsets[i], rows), :]
        target = self.arrival.at[:, :, :, pl.ds(16 * self.bank_offsets[i], rows), :]
        return remote(source, target, self.swap_sems.at[3], self.swap_sems.at[i], partner())

    def start_swap(self):
        self.begun = 0
        if self.again:
            self.before.swapped()
            pl.semaphore_wait(self.swap_credit, 1)
        for i in range(3):
            self.swap(i).start()
        self.steps = [part.steps() for part in self.work]

    def add_swapped(self, i):
        part = self.work[i]
        self.swap(i).wait_recv()
        mine = self.packed.at[:, :, :, pl.ds(part.first, part.rows[1]), :]
        mine[...] = mine[...] + self.arrival[:, :, :, part.bank_rows[0] : part.bank_rows[0] + part.rows[1], :]
        self.begun += 1
        if self.reused and self.begun == 3:
            pl.semaphore_signal(self.swap_credit, inc=1, device_id=partner(), device_id_type=MESH)
        if self.again:
            pl.semaphore_wait(self.part_credit.at[i], 2)

    def free(self, i):
        if self.reused:
            for step in (1, -1):
                pl.semaphore_signal(self.part_credit.at[i], inc=1, device_id=beside(self.position, ORDERS[i][0], step), device_id_type=MESH)

    def swapped(self):
        landed(self.packed.at[:, :, :, pl.ds(self.other, 16 * self.units), :], self.swap_sems.at[3])

    def close(self):
        if self.again:
            self.swapped()
        landed(self.slots[0], self.late_sends.at[0])
        given = 16 * self.half
        rest = 16 * self.units - given

        @pl.when(self.me == self.section)
        def _():
            landed(self.slots[1], self.late_sends.at[1])

        @pl.when(self.me != self.section)
        def _():
            if rest:
                landed(self.packed.at[0, 0, 0, pl.ds(0, 4 * given + 3 * rest), :], self.late_sends.at[1])
            else:
                landed(self.slots[2], self.late_sends.at[1])


def keep_attention():
    return [pltpu.VMEM((256, 1536), BF16), pltpu.VMEM((8, 256, 256), BF16), pltpu.VMEM((256, 512), BF16)]


def keep_norm():
    return [pltpu.VMEM((256, 512), F32)]


def keep_ffn():
    return [pltpu.VMEM((256, 512), BF16), pltpu.VMEM((256, 2048), BF16), pltpu.VMEM((256, 2048), BF16)]


def stacked(scratch):
    return [pltpu.VMEM((2,) + tuple(s.shape), s.dtype) for s in scratch]


def scratch_shapes():
    low, wide, square = pltpu.VMEM((256, 512), BF16), pltpu.VMEM((256, 512), F32), pltpu.VMEM((256, 256), BF16)
    return dict(
        weights=stacked([pltpu.VMEM(shape, BF16) for shape in WEIGHTS]),
        inputs=stacked([low, low, pltpu.VMEM((6, 1, 512), F32)]),
        selfs=stacked(keep_attention() + keep_norm() + [pltpu.VMEM((256, 1), F32)]),
        scales=pltpu.VMEM((256, 128), F32),
        firsts=stacked([low, wide]),
        enc=keep_ffn()[1:] + keep_norm() + keep_norm() + [pltpu.VMEM((256, 1024), BF16)],
        cross=[low, pltpu.VMEM((8, 256, 256), BF16), low] + keep_norm(),
        dec=keep_ffn() + keep_norm(),
        bias=[pltpu.VMEM((2, 256, 256), BF16), square],
        work=[wide, low, pltpu.VMEM((8, 512), F32)],
        results=[low, low],
        packed=pltpu.VMEM((4, 4, 4, 16 * PACKED_UNITS, 128), BF16),
        arrivals=[pltpu.VMEM((4, 4, 4, 16 * sum(units), 128), BF16) for units in BANKS],
        banks=[bank_buffers(units) for units in BANKS],
        groups=[group_buffers(group[3]) for group in GROUPS],
        places=[pltpu.VMEM((2, 1, ROW), jnp.int32), pltpu.SMEM((2, 1, NSEG), jnp.int32)],
        totals=pltpu.VMEM((464, 128), F32),
        in_sems=pltpu.SemaphoreType.DMA((2, 8)),
        in_sends=pltpu.SemaphoreType.DMA((2,)),
        place_sems=pltpu.SemaphoreType.DMA((3,)),
        project_sems=pltpu.SemaphoreType.DMA((2,)),
        out_sems=pltpu.SemaphoreType.DMA((3, 2)),
        group_sems=[
            [pltpu.SemaphoreType.DMA(shape) for shape in ((3, 3), (2,))]
            for _ in GROUPS
        ],
        bank_sems=[[pltpu.SemaphoreType.DMA(shape) for shape in ((4,), (3,), (3,), (3,))] for _ in BANKS],
        swap_credit=pltpu.SemaphoreType.REGULAR((3,)),
        part_credit=pltpu.SemaphoreType.REGULAR((3, 3)),
    )


def whole_kernel(tree, *refs):
    tokens, cotangent, lengths_in, segments_in = refs[:4]
    own = refs[4:9]
    norm_params = refs[9]
    layer_out, token_grads = refs[10:12]
    totals_out = refs[12]
    s = jax.tree.unflatten(tree, refs[13:])
    me = lax.axis_index("section")
    position = place()

    barrier = pltpu.get_barrier_semaphore()
    pl.semaphore_signal(barrier, inc=1, device_id=partner(), device_id_type=MESH)
    for axis in range(3):
        for step in (1, -1):
            pl.semaphore_signal(barrier, inc=1, device_id=beside(position, axis, step), device_id_type=MESH)
            pl.semaphore_signal(barrier, inc=1, device_id=across(position, axis, step), device_id_type=MESH)

    held = list(s["weights"]) + list(s["inputs"])

    def given(i, micro):
        if i < 5:
            return own[i].at[0]
        if i == 7:
            return norm_params
        return (tokens, cotangent)[i - 5].at[0, micro, 0]

    def local(i):
        return pltpu.make_async_copy(given(i, me), held[i].at[me], s["in_sems"].at[me, i])

    def sent(i):
        return remote(given(i, 1 - me), held[i].at[me], s["in_sends"].at[1 if i == 7 else 0], s["in_sems"].at[me, i], partner())

    def ready(j, i):
        pltpu.make_async_copy(given(i, 0), held[i].at[j], s["in_sems"].at[j, i]).wait()

    segments, lengths = s["places"]
    places = [pltpu.make_async_copy((segments_in, lengths_in)[i], s["places"][i], s["place_sems"].at[i]) for i in range(2)]
    others = pltpu.make_async_copy(given(5, 1 - me), s["dec"][0], s["place_sems"].at[2])
    for copy in places:
        copy.start()
    others.start()
    for i in (0, 5, 7, 1, 3, 4, 2, 6):
        local(i).start()

    pl.semaphore_wait(barrier, 13)
    for i in (5, 7, 1):
        sent(i).start()

    def pieces(i):
        first = 0
        for k, rows in enumerate((352, 352, 336, 336, 336, 336)):
            piece = pl.ds(first, rows)
            remote(own[i].at[0, piece], held[i].at[me, piece], s["in_sends"].at[1 if i == 7 else 0], s["in_sems"].at[me, i],
                   across(position, k // 2, 1 - 2 * (k % 2))).start()
            first += rows

    @pl.when(me == 0)
    def _():
        pieces(4)


    for copy in places:
        copy.wait()

    bias, cross_bias = s["bias"]
    lane = lax.broadcasted_iota(jnp.int32, (1, ROW), 1)
    down = lax.broadcasted_iota(jnp.int32, (ROW, 1), 0)
    ids_row, ids_col = jnp.zeros((1, ROW), jnp.int32), jnp.zeros((ROW, 1), jnp.int32)
    bound = jnp.int32(0)
    for j in range(NSEG):
        bound = bound + lengths[me, 0, j]
        ids_row = ids_row + (lane >= bound).astype(jnp.int32)
        ids_col = ids_col + (down >= bound).astype(jnp.int32)
    target_row = segments[me].astype(F32)
    target_col = jnp.broadcast_to(target_row, (128, ROW)).T[:, 0:1]
    ids_row, ids_col = ids_row.astype(F32), ids_col.astype(F32)
    bias[0] = jnp.where(ids_col == ids_row, 0.0, -1e30).astype(BF16)
    bias[1] = jnp.where(target_col == target_row, 0.0, -1e30).astype(BF16)
    cross_bias[...] = jnp.where(target_col == ids_row, 0.0, -1e30).astype(BF16)

    w_self_in, w_self_out, w_cross, w_in, w_out = s["weights"]
    x, cot, norms = s["inputs"]
    first_low, first = s["firsts"]
    work, grad_context, grad_norms = s["work"]
    memory_low, third_low = s["results"]
    source_grad, target_grad = first.at[0], first.at[1]

    others.wait()
    ready(me, 0)
    staged = s["enc"][0].at[:, pl.ds(0, 1536)]
    project(s["dec"][0], w_self_in.at[me], staged)
    given_projection = remote(staged, s["selfs"][0].at[me], s["project_sems"].at[0], s["project_sems"].at[1], partner())
    given_projection.start()

    @pl.when(me == 0)
    def _():
        for i in (3, 2, 6, 0):
            sent(i).start()

    @pl.when(me != 0)
    def _():
        for i in (2, 3, 4, 6, 0):
            sent(i).start()

    for i in range(2):
        j = lax.rem(me + i, 2)
        for which in (5, 7, 1):
            ready(j, which)
        projected, shares, context, normed, scale = [ref.at[j] for ref in s["selfs"]]
        if i == 0:
            project(x.at[j], w_self_in.at[j], projected)
        else:
            landed(projected, s["project_sems"].at[1])
        result = self_forward(x.at[j], w_self_out.at[j], bias.at[j], norms.at[j], projected, shares, context, normed, scale)
        first[j] = result
        first_low[j] = result.astype(BF16)

    enc_active, enc_slopes, enc_normed, memory_normed, key_value = s["enc"]
    queries, cross_shares, cross_context, cross_normed = s["cross"]
    dec_low, dec_active, dec_slopes, dec_normed = s["dec"]
    enc_scale, memory_scale, cross_scale, dec_scale = [s["scales"].at[:, i : i + 1] for i in range(4)]
    enc_self, dec_self = [ref.at[0] for ref in s["selfs"]], [ref.at[1] for ref in s["selfs"]]
    enc_norms, dec_norms = norms.at[0], norms.at[1]

    given_projection.wait_send()
    result = ffn_forward(first_low.at[0], w_in.at[0], w_out.at[0], enc_active, enc_slopes, lambda: ready(0, 3), lambda: ready(0, 4))
    second = norm(first[0] + result, enc_norms, 1, enc_normed, enc_scale)
    memory = norm(second, enc_norms, 2, memory_normed, memory_scale).astype(BF16)
    memory_low[...] = memory
    ready(0, 2)
    for i in range(2):
        key_value[:, 512 * i : 512 * i + 512] = dot(memory, w_cross[0, :, 512 * i : 512 * i + 512]).astype(BF16)

    ready(1, 2)
    queries[...] = dot(first_low[1], w_cross[1, :, :512]).astype(BF16)
    keys_values = (columns_of(key_value, 0), columns_of(key_value, 512))
    attend(columns_of(queries, 0), *keys_values, cross_bias, cross_shares, cross_context)
    second = norm(first[1] + dot(cross_context[...], w_cross[1, :, 512:]), dec_norms, 2, cross_normed, cross_scale)
    dec_low[...] = second.astype(BF16)
    result = ffn_forward(dec_low, w_in.at[1], w_out.at[1], dec_active, dec_slopes, lambda: ready(1, 3), lambda: ready(1, 4))
    third_low[...] = norm(second + result, dec_norms, 1, dec_normed, dec_scale).astype(BF16)

    def put_out(slot, out, values):
        for j in range(2):
            here = pltpu.make_async_copy(values[j], out.at[0, me, 0], s["out_sems"].at[0, slot])
            there = remote(values[j], out.at[0, me, 0], s["out_sems"].at[1, slot], s["out_sems"].at[2, slot], partner())

            @pl.when(me == j)
            def _():
                here.start()

            @pl.when(me != j)
            def _():
                there.start()

    def out_done(slot, out, values):
        pltpu.make_async_copy(values[0], out.at[0, me, 0], s["out_sems"].at[0, slot]).wait()
        there = remote(values[0], out.at[0, me, 0], s["out_sems"].at[1, slot], s["out_sems"].at[2, slot], partner())
        there.wait_send()
        there.wait_recv()

    put_out(0, layer_out, (memory_low, third_low))

    packed = s["packed"]
    groups = [
        Group(g, position, packed, s["arrivals"], s["totals"], s["banks"], s["groups"][g], s["bank_sems"][GROUPS[g][4]] + s["group_sems"][g],
              (s["swap_credit"].at[GROUPS[g][4]], s["part_credit"].at[GROUPS[g][4]]))
        for g in range(len(GROUPS))
    ]
    for group in groups[FIRST_USERS:]:
        group.before = next(other for other in groups if other.bank == group.bank)

    def at(moment, which=None):
        for step in SCHEDULE.get(moment if which is None else moment + str(which), "").split():
            group = groups[int(step[0])]
            if step[1] == "s":
                group.start_swap()
            else:
                next(group.steps["abc".index(step[1])])

    def ffn_back(gradient, low, section, activated, slopes, moment):
        result = gradient.astype(BF16)
        for i in range(4):
            pack_tall(packed, section, i, dot_tn(activated[:, 512 * i : 512 * i + 512], result))
        at(moment + "_out")
        for i in range(4):
            rows = slice(512 * i, 512 * i + 512)
            slopes[:, rows] = (dot_nt(result, w_out[section, rows, :]) * slopes[:, rows].astype(F32)).astype(BF16)
        for i in range(4):
            pack(packed, section, HIDDEN_IN + 2 * i, dot_tn(low[...], slopes[:, 512 * i : 512 * i + 512]))
            at(moment + "_in", i)
        return dot_nt(slopes[...], w_in[section])

    def self_back_a(gradient, section, kept):
        projected, shares, context, normed, scale = kept
        low = gradient.astype(BF16)
        pack(packed, section, SELF_OUT, dot_tn(context[...], low))
        grad_context[...] = dot_nt(low, w_self_out[section]).astype(BF16)

    def self_back_b(section, kept, moment):
        projected, shares, context, normed, scale = kept
        attend_back(*thirds(projected), shares, context, grad_context, *[putter(projected, 512 * i) for i in range(3)])
        at(moment + "_attend")

    def self_back_c(section, kept):
        projected = kept[0]
        for i in range(3):
            pack(packed, section, SELF_IN + 2 * i, dot_tn(x[section], projected[:, 512 * i : 512 * i + 512]))
        pack_norms(packed, section, grad_norms)

    grad_norms[...] = jnp.zeros_like(grad_norms)
    ready(1, 6)
    gradient = norm_back(cot[1].astype(F32), dec_norms, 1, dec_normed, dec_scale, grad_norms)
    gradient = gradient + ffn_back(gradient, dec_low, 1, dec_active, dec_slopes, "dec")
    gradient = norm_back(gradient, dec_norms, 2, cross_normed, cross_scale, grad_norms)
    work[...] = gradient
    low = gradient.astype(BF16)
    pack(packed, 1, CROSS + 2, dot_tn(cross_context[...], low))
    grad_context[...] = dot_nt(low, w_cross[1, :, 512:]).astype(BF16)
    at("cross_start")
    attend_back(columns_of(queries, 0), *keys_values, cross_shares, cross_context, grad_context,
                putter(queries, 0), putter(key_value, 0), putter(key_value, 512))
    at("cross_attend")
    pack(packed, 1, CROSS, dot_tn(first_low[1], queries[...]))
    gradient = work[...] + dot_nt(queries[...], w_cross[1, :, :512])
    gradient = norm_back(gradient, dec_norms, 0, *dec_self[3:], grad_norms)
    work[...] = gradient
    at("cross_end")
    self_back_a(gradient, 1, dec_self)
    at("dec_start")
    self_back_b(1, dec_self, "dec")
    self_back_c(1, dec_self)
    at("dec_end")
    pl.when(me != 1)(lambda: ready(1, 0))
    target_grad[...] = work[...] + dot_nt(dec_self[0][...], w_self_in[1])

    for i in range(2):
        pack(packed, 0, CROSS + 2 * i, dot_tn(memory_low[...], key_value[:, 512 * i : 512 * i + 512]))
    at("memory_start")
    ready(0, 6)
    gradient = cot[0].astype(F32) + dot_nt(key_value[...], w_cross[0])
    gradient = norm_back(gradient, enc_norms, 2, memory_normed, memory_scale, grad_norms)
    gradient = norm_back(gradient, enc_norms, 1, enc_normed, enc_scale, grad_norms)
    at("memory_end")
    gradient = gradient + ffn_back(gradient, first_low.at[0], 0, enc_active, enc_slopes, "enc")
    gradient = norm_back(gradient, enc_norms, 0, *enc_self[3:], grad_norms)
    work[...] = gradient
    self_back_a(gradient, 0, enc_self)
    at("enc_start")
    self_back_b(0, enc_self, "enc")
    self_back_c(0, enc_self)
    at("enc_end")
    pl.when(me != 0)(lambda: ready(0, 0))
    source_grad[...] = work[...] + dot_nt(enc_self[0][...], w_self_in[0])
    put_out(1, token_grads, (source_grad, target_grad))
    at("last")

    copy = pltpu.make_async_copy(s["totals"], totals_out, s["place_sems"].at[0])
    copy.start()
    for group in groups:
        group.close()
    landed(packed.at[:, :, :, pl.ds(0, 480), :], s["in_sends"].at[0])
    sent(7).wait_send()
    out_done(0, layer_out, (memory_low, third_low))
    out_done(1, token_grads, (source_grad, target_grad))
    copy.wait()


def finish_kernel(layer_in, grads_in, totals, layer_out, token_grads, *refs):
    grad_refs, grad_norms = refs[:5], refs[5]
    layer_out[...] = layer_in[...]
    token_grads[...] = grads_in[...]

    def tile(t):
        return totals[8 * t : 8 * t + 8, :]

    for which, unit, columns in ((0, SELF_IN, 1536), (1, SELF_OUT, 512), (2, CROSS, 1024), (3, HIDDEN_IN, 2048)):
        for i in range(columns // 128):
            grad_refs[which][0, :, 128 * i : 128 * i + 128] = tile(2 * unit + i)
    for r in range(4):
        for i in range(4):
            grad_refs[4][0, 8 * r : 8 * r + 8, 128 * i : 128 * i + 128] = tile(2 * HIDDEN_OUT + 4 * r + i)
    turned = jnp.concatenate([tile(2 * NORMS), jnp.zeros((120, 128), F32)], 0).T
    for i in range(6):
        grad_norms[i] = turned[i : i + 1, :8]


def body(tokens, cotangent, source_lengths, target_segments, self_in, self_out, cross_weight, hidden_in, hidden_out, norm_params):
    shapes, tree = jax.tree.flatten(scratch_shapes())
    vmem, hbm = [pl.BlockSpec(memory_space=space) for space in (pltpu.VMEM, pl.ANY)]
    large = [jax.ShapeDtypeStruct(tokens.shape, BF16), jax.ShapeDtypeStruct(tokens.shape, F32)]
    layer, grads, totals = pl.pallas_call(
        lambda *refs: whole_kernel(tree, *refs),
        out_shape=large + [jax.ShapeDtypeStruct((464, 128), F32)],
        in_specs=[hbm] * 10,
        out_specs=[hbm] * 3,
        scratch_shapes=shapes,
        compiler_params=pltpu.CompilerParams(collective_id=0, has_side_effects=True, vmem_limit_bytes=64 << 20),
        name="layer_pair",
    )(tokens, cotangent, source_lengths, target_segments, self_in, self_out, cross_weight, hidden_in, hidden_out,
      norm_params.transpose(1, 0, 2))
    small = [(1, 8, 1536), (1, 8, 512), (1, 8, 1024), (1, 8, 2048), (1, 32, 512), (6, 1, 8)]
    results = pl.pallas_call(
        finish_kernel,
        out_shape=large + [jax.ShapeDtypeStruct(shape, F32) for shape in small],
        in_specs=[vmem] * 3,
        out_specs=[vmem] * 8,
        name="finish",
    )(layer, grads, totals)
    return (*results[:7], results[7].transpose(1, 0, 2))


def solution(mesh):
    return jax.shard_map(
        body,
        mesh=mesh,
        in_specs=(
            P("section", None, "dp", None, None),
            P("section", None, "dp", None, None),
            P(None, "dp", None),
            P(None, "dp", None),
            P("section", None, None),
            P("section", None, None),
            P("section", None, None),
            P("section", None, None),
            P("section", None, None),
            P("section", None, None),
        ),
        out_specs=(
            P("section", None, "dp", None, None),
            P("section", None, "dp", None, None),
            P("section", "dp", None),
            P("section", "dp", None),
            P("section", "dp", None),
            P("section", "dp", None),
            P("section", "dp", None),
            P("section", None, "dp"),
        ),
        check_vma=False,
    )
```
